32 devices in a mesh: dom: 4 (over z), four: 8 (over y, x, core).
Axes of the slice: x: 2, y: 2, z: 4, core: 2. Of those that a mesh axis runs over, the one named last changes fastest.
Arguments:
- adjoint: float32 [3, 256, 64, 1024], P(None, 'four', None, 'dom'), may hold values from -6 to 6
- base_bank: float32 [4, 2, 64, 1024], P(None, None, None, 'dom'), may hold values from -6 to 6
- snapshot: int32 [1024], P('dom'), may hold values from 0 to 3
- geometry: float32 [2, 1024], P(None, 'dom'), may hold values from 0.5 to 4
- diff_r: float32 [64, 64], replicated, may hold values from -0.75 to 0.75
- diff_s: float32 [64, 64], replicated, may hold values from -0.75 to 0.75
- stiffness: float32 [64, 64], replicated, as said below
- upper_list: int32 [4, 512], P('dom'), may hold values from 7 to 16383, as said below
- lower_list: int32 [4, 512], P('dom'), may hold values from 0 to 14591, as said below
Outputs:
- advanced: float32 [3, 256, 64, 1024], P(None, 'four', None, 'dom')
The draws below stay inside these ranges and needn't reach their ends.
Inputs may be any that keep to these rules, and one draw needn't show every extreme that they name: `upper_list`: row p lists 64 distinct elements e of partition p, each with its eight nodes n = 8 s + 7, s = 0 .. 7, as n * 256 + e; element 256 - 1 is always among them. `lower_list`: row p lists 64 distinct elements e of partition p, each with its eight nodes n = 8 s, s = 0 .. 7, as n * 256 + e; elements 0 and 255 are always among them. `stiffness`: Symmetric. An off-diagonal entry (n, m) is negative where n and m lie on one line of the 8 x 8 node grid (n // 8 == m // 8 or n % 8 == m % 8) and zero elsewhere; the off-diagonal magnitudes of each row sum to less than its diagonal entry, which is positive.
All inputs are finite; a program needn't handle non-finite values.
Results may differ from the reference program's by a relative error of at most 0.0001.
Values sent between devices are 32-bit elements; how exact they have to be, the bound alone decides.
No kernel may reach another device: no remote copies, remote signals or barrier semaphores. Data moves between devices by JAX's collectives and lax.ppermute only.
A program may use at most 128 MiB of HBM per device.

```python
import math
import jax
import jax.numpy as jnp
import numpy as np
from jax import lax

NODES = 64
PLANES = 256
E_DEV = 256
NSNAP = 4
FACE = 64
SWEEPS = 6
ELEMS = 1024
SHARED = 512
N_DOM = 4


def face_elements(key):
    keys = jax.random.split(key, N_DOM)

    def one_row(row_key):
        order = jax.random.permutation(row_key, E_DEV)
        spot = jnp.argmax(order == E_DEV - 1)
        order = order.at[spot].set(order[0]).at[0].set(E_DEV - 1)
        spot = jnp.argmax(order == 0)
        order = order.at[spot].set(order[1]).at[1].set(0)
        return order[:FACE]
    return jax.vmap(one_row)(keys)


def node_indices(elements, column):
    rows = jnp.arange(8, dtype=jnp.int32) * 8 + column
    index = rows[None, None, :] * E_DEV + elements[:, :, None]
    return index.reshape(N_DOM, FACE * 8).astype(jnp.int32)


def draw_upper_list(key, part):
    key = jax.random.fold_in(key, 3)
    return node_indices(face_elements(key), 7)


def draw_lower_list(key, part):
    key = jax.random.fold_in(key, 5)
    return node_indices(face_elements(key), 0)


def line_reach():
    grid = np.arange(NODES)
    first = grid // 8
    second = grid % 8
    same_first = first[:, None] == first[None, :]
    same_second = second[:, None] == second[None, :]
    distance = np.where(same_first, np.abs(second[:, None] - second[None, :]), np.abs(first[:, None] - first[None, :]))
    linked = (same_first | same_second) & (grid[:, None] != grid[None, :])
    reach = np.where(linked, 0.25 / np.maximum(distance, 1), 0.0).astype(np.float32)
    bound = reach.sum(axis=1).astype(np.float32)
    return (reach, bound)


def spread_factor(raw, power):
    return 0.5 + 0.5 * raw ** power


def draw_stiffness(key, part):
    key = jax.random.fold_in(key, 11)
    key_off, key_diag = jax.random.split(key, 2)
    reach, bound = line_reach()
    raw = jax.random.uniform(key_off, (NODES, NODES), jnp.float32, 0.0, 1.0)
    factor = spread_factor(raw, 1.0)
    margin = jax.random.uniform(key_diag, (NODES,), jnp.float32, 0.02, 0.1)
    factor = 0.5 * (factor + factor.T)
    off_part = -jnp.asarray(reach) * factor
    unit = jnp.eye(NODES, dtype=jnp.float32)
    diag_part = jnp.asarray(bound) + margin
    return (off_part * (1.0 - unit) + diag_part[:, None] * unit).astype(jnp.float32)


def place_ends(array, stream_key, smallest, high):
    longest = array.shape.index(max(array.shape))
    spots = []
    for shift in (0, 1):
        where = [jax.random.randint(jax.random.fold_in(stream_key, axis), (), 0, length) for axis, length in enumerate(array.shape)]
        where[longest] = (where[longest] + shift) % array.shape[longest]
        spots.append(tuple(where))
    return array.at[spots[0]].set(smallest).at[spots[1]].set(high)


def block_levels(key, shape, shards, smallest, top_value):
    def one(axis_at, blocks):
        draws = jax.random.uniform(jax.random.fold_in(jax.random.fold_in(key, 6), axis_at), (blocks,), jnp.float32, smallest / len(shards), top_value / len(shards))
        return jnp.repeat(jnp.exp(draws), shape[axis_at] // blocks).reshape((-1,) + (1,) * (len(shape) - axis_at - 1))

    factor_of = one(*shards[0])
    for cut in shards[1:]:
        factor_of = factor_of * one(*cut)
    return factor_of


def bell_draw(stream_key, dims, spread, limit, shards=(), kind=jnp.bfloat16):
    level = block_levels(stream_key, dims, shards, -0.22, 0.18) if shards else 1.0
    entries = jax.random.normal(stream_key, dims, jnp.float32) * spread * level
    return jnp.minimum(jnp.maximum(entries, -limit), limit).astype(kind)


def setup_inputs(seed: int = 0) -> dict:
    streams_of = jax.random.split(jax.random.key(seed), 10)
    adjoint = bell_draw(streams_of[0], (3, PLANES, NODES, ELEMS), 1.0, 6.0, ((1, 8), (3, 4)), jnp.float32)
    base_bank = bell_draw(streams_of[1], (NSNAP, 2, NODES, ELEMS), 1.0, 6.0, ((3, 4),), jnp.float32)
    snapshot = place_ends(jax.random.randint(streams_of[2], (ELEMS,), 0, NSNAP), jax.random.fold_in(streams_of[2], 1), 0, NSNAP - 1).astype(jnp.int32)
    geometry = jnp.clip(jnp.exp(math.log(4.0) - 2.0794415 * jax.random.uniform(streams_of[3], (2, ELEMS), jnp.float32) ** block_levels(streams_of[3], (2, ELEMS), ((1, 4),), -0.2, 0.2)), 0.5, 4.0)
    diff_r = bell_draw(streams_of[4], (NODES, NODES), NODES ** -0.5, 0.75, (), jnp.float32)
    diff_s = bell_draw(streams_of[5], (NODES, NODES), NODES ** -0.5, 0.75, (), jnp.float32)
    stiffness = draw_stiffness(jax.random.fold_in(streams_of[9], 71), 0)
    upper_list = draw_upper_list(jax.random.fold_in(streams_of[9], 71), 0)
    lower_list = draw_lower_list(jax.random.fold_in(streams_of[9], 71), 0)
    return {"adjoint": adjoint, "base_bank": base_bank, "snapshot": snapshot, "geometry": geometry, "diff_r": diff_r, "diff_s": diff_s, "stiffness": stiffness, "upper_list": upper_list, "lower_list": lower_list}


HIGHEST = lax.Precision.HIGHEST
PENALTY = 0.5
RELAXATION = 0.8
TIME_STEP = 0.2
INTERACTION = 2.0

def along_nodes(matrix, field):
    return jnp.einsum('mn,...ne->...me', matrix, field, precision=HIGHEST)

def pick_base(base_bank, snapshot):
    levels = jnp.arange(base_bank.shape[0], dtype=jnp.int32)
    chosen = (snapshot[None, :] == levels[:, None]).astype(base_bank.dtype)
    return lax.optimization_barrier(jnp.sum(chosen[:, None, None, :] * base_bank, 0))

def advect(velocity, base_flow, grad_x, grad_y, diff_r, diff_s, scale_r, scale_s):
    slope_x = scale_r * along_nodes(diff_r, velocity)
    slope_y = scale_s * along_nodes(diff_s, velocity)
    transport = base_flow[0] * slope_x + base_flow[1] * slope_y
    product_x = velocity[0] * grad_x[0] + velocity[1] * grad_x[1]
    product_y = velocity[0] * grad_y[0] + velocity[1] * grad_y[1]
    return jnp.stack([product_x - transport[0], product_y - transport[1], -transport[2]])

def real_transform(field):
    length = field.shape[0]
    spectrum = jnp.fft.rfft(field, axis=0)
    pair_scale = math.sqrt(2.0 / length)
    cosines = jnp.real(spectrum[1:length // 2]) * pair_scale
    sines = -jnp.imag(spectrum[1:length // 2]) * pair_scale
    middle = jnp.stack([cosines, sines], 1).reshape((length - 2,) + field.shape[1:])
    head = jnp.stack([jnp.real(spectrum[0]), jnp.real(spectrum[length // 2])], 0) / math.sqrt(length)
    return jnp.concatenate([head, middle], 0).astype(field.dtype)

def derivative_z(field, waves):
    lead = field.shape[0]
    pairs = field.reshape((lead // 2, 2) + field.shape[1:])
    factor = waves[:, None, None]
    return jnp.stack([factor * pairs[:, 1], -factor * pairs[:, 0]], 1).reshape(field.shape)

def to_parts(field):
    planes_all = field.shape[0]
    split_field = field.reshape(planes_all, NODES, N_DOM, E_DEV)
    return jnp.moveaxis(split_field, 2, 0)

def from_parts(parts):
    moved = jnp.moveaxis(parts, 0, 2)
    return moved.reshape(moved.shape[0], NODES, N_DOM * E_DEV)

def place_one(target, upper_idx, lower_idx, upper_term, lower_term):
    return target.at[:, upper_idx].add(upper_term).at[:, lower_idx].add(lower_term)

def face_penalty(parts, upper_list, lower_list):
    flat_parts = parts.reshape(N_DOM, parts.shape[1], NODES * E_DEV)
    upper_vals = jax.vmap(lambda rows, idx: rows[:, idx])(flat_parts, upper_list)
    lower_vals = jax.vmap(lambda rows, idx: rows[:, idx])(flat_parts, lower_list)
    next_lower = jnp.roll(lower_vals, -1, axis=0)
    prev_upper = jnp.roll(upper_vals, 1, axis=0)
    penalty = jax.vmap(place_one)(jnp.zeros_like(flat_parts), upper_list, lower_list, PENALTY * (upper_vals - next_lower), PENALTY * (lower_vals - prev_upper))
    return penalty.reshape(parts.shape)

def reference(adjoint, base_bank, snapshot, geometry, diff_r, diff_s, stiffness, upper_list, lower_list):
    base_flow = pick_base(base_bank, snapshot)
    scale_r = geometry[0]
    scale_s = geometry[1]
    grad_x = scale_r * along_nodes(diff_r, base_flow)
    grad_y = scale_s * along_nodes(diff_s, base_flow)
    plane_span = min(32, PLANES)
    pieces = []
    for first_plane in range(0, PLANES, plane_span):
        pieces.append(advect(adjoint[:, first_plane:first_plane + plane_span], base_flow, grad_x, grad_y, diff_r, diff_s, scale_r, scale_s))
    rates = jnp.concatenate(pieces, 1)
    spectra = jnp.stack([real_transform(adjoint[comp]) for comp in range(3)])
    spectral_rates = jnp.stack([real_transform(rates[comp]) for comp in range(3)])
    beta = 4.0 / PLANES
    waves = beta * jnp.arange(PLANES // 2, dtype=jnp.int32).astype(jnp.float32)
    coef_index = jnp.arange(PLANES, dtype=jnp.int32)
    wave_number = jnp.where(coef_index == 1, PLANES // 2, coef_index // 2).astype(jnp.float32)
    shift = (beta * wave_number) ** 2
    source = -(scale_r * along_nodes(diff_r, spectra[2])) + derivative_z(spectra[0], waves)
    mass = 1.0 / (scale_r * scale_s)
    mass_parts = mass.reshape(N_DOM, E_DEV)
    source_parts = to_parts(source)
    ones_flat = jax.vmap(place_one)(jnp.zeros((N_DOM, 1, NODES * E_DEV), jnp.float32), upper_list, lower_list, jnp.ones((N_DOM, 1, SHARED), jnp.float32), jnp.ones((N_DOM, 1, SHARED), jnp.float32))
    face_count = ones_flat.reshape(N_DOM, 1, NODES, E_DEV)
    shifted_mass = shift[None, :, None, None] * mass_parts[:, None, None, :]
    diagonal_part = jnp.diagonal(stiffness)[None, None, :, None] + shifted_mass + PENALTY * face_count
    potential = RELAXATION * source_parts / diagonal_part
    for sweep_index in range(SWEEPS - 1):
        applied = along_nodes(stiffness, potential) + shifted_mass * potential
        applied = applied + face_penalty(potential, upper_list, lower_list)
        potential = potential + RELAXATION * (source_parts - applied) / diagonal_part
    potential = from_parts(potential)
    force_x = derivative_z(potential, waves) - spectra[0]
    force_z = -(scale_r * along_nodes(diff_r, potential)) - spectra[2]
    advanced_x = spectra[0] + TIME_STEP * (spectral_rates[0] + INTERACTION * force_x)
    advanced_y = spectra[1] + TIME_STEP * (spectral_rates[1] + INTERACTION * 0.0)
    advanced_z = spectra[2] + TIME_STEP * (spectral_rates[2] + INTERACTION * force_z)
    return jnp.stack([advanced_x, advanced_y, advanced_z])
```

```python
import functools
import math

import jax
import jax.numpy as jnp
import ml_dtypes
import numpy as np
from jax import lax
from jax.experimental import pallas as pl
from jax.experimental.pallas import tpu as pltpu
from jax.sharding import PartitionSpec as P

PLANES = 256
PENALTY = 0.5
RELAXATION = 0.8
TIME_STEP = 0.2
INTERACTION = 2.0
LINE = 8

F32 = jnp.float32
BF16 = jnp.bfloat16
VMEM_LIMIT = 48 * 1024 * 1024


def params():
    return pltpu.CompilerParams(vmem_limit_bytes=VMEM_LIMIT)


def cost(flops, moved):
    return pl.CostEstimate(flops=int(flops), bytes_accessed=int(moved), transcendentals=0)


def split(x):
    high = x.astype(BF16)
    low = (x - high.astype(F32)).astype(BF16)
    return high, low


def dot(a, b):
    return lax.dot_general(a, b, (((1,), (0,)), ((), ())), preferred_element_type=F32)


def pack_matrix(m):
    high, low = split(m)
    return jnp.concatenate([high, low, high], axis=1)


def pack_field(v):
    high, low = split(v)
    return jnp.concatenate([high, high, low], axis=0)


def coef_table(length):
    c = np.arange(length)[:, None]
    j = np.arange(length)[None, :]
    angle = ((c // 2) * j % length) * (2.0 * math.pi / length)
    table = np.where(c % 2 == 1, np.sin(angle), np.cos(angle)) * math.sqrt(2.0 / length)
    table[0] = 1.0 / math.sqrt(length)
    table[1] = np.where(np.arange(length) % 2 == 0, 1.0, -1.0) / math.sqrt(length)
    high = table.astype(ml_dtypes.bfloat16)
    low = (table - high.astype(np.float64)).astype(ml_dtypes.bfloat16)
    return np.concatenate([high, low], axis=0)


def transform_kernel(nodes, table_ref, x_ref, o_ref):
    planes = table_ref.shape[1]
    both = table_ref[...]
    high_table = both[:planes]
    for n in range(nodes):
        rows = pl.ds(n, planes, stride=nodes) if nodes > 1 else pl.ds(0, planes)
        high, low = split(x_ref[rows, :])
        wide = dot(both, high)
        o_ref[rows, :] = wide[:planes] + (wide[planes:] + dot(high_table, low))


def transform(columns, table):
    peers, per, nodes, elements = columns.shape
    rows = peers * per * nodes
    width = 128
    flat = columns.reshape(rows, elements)
    out = pl.pallas_call(
        functools.partial(transform_kernel, nodes),
        out_shape=jax.ShapeDtypeStruct((rows, elements), F32),
        grid=(elements // width,),
        in_specs=[
            pl.BlockSpec(table.shape, lambda i: (0, 0)),
            pl.BlockSpec((rows, width), lambda i: (0, i)),
        ],
        out_specs=pl.BlockSpec((rows, width), lambda i: (0, i)),
        compiler_params=params(),
        cost_estimate=cost(6 * PLANES * rows * elements, 8 * rows * elements),
        name="transform",
    )(table, flat)
    return out.reshape(columns.shape)


BXR, BYS, DXBX, DXBY, DYBX, DYBY, DIAG = range(7)


def prep_kernel(
    bank_ref, snap_ref, geo_ref, dr_ref, ds_ref, st_ref, up_ref, lo_ref,
    coef_ref, dpack_ref, spack_ref, gather_ref, scatter_ref, mask_ref,
):
    elements = geo_ref.shape[1]
    nodes = dr_ref.shape[0]
    snap = snap_ref[...]
    base = [
        sum(jnp.where(snap == k, bank_ref[k, i], 0.0) for k in range(bank_ref.shape[0]))
        for i in range(2)
    ]
    rx = geo_ref[0:1, :]
    sy = geo_ref[1:2, :]
    dpack = pack_matrix(jnp.concatenate([dr_ref[...], ds_ref[...]], axis=0))
    dpack_ref[...] = dpack
    bx = dot(dpack, pack_field(base[0]))
    by = dot(dpack, pack_field(base[1]))
    coef_ref[BXR] = base[0] * rx
    coef_ref[BYS] = base[1] * sy
    coef_ref[DXBX] = rx * bx[:nodes]
    coef_ref[DXBY] = rx * by[:nodes]
    coef_ref[DYBX] = sy * bx[nodes:]
    coef_ref[DYBY] = sy * by[nodes:]
    row = lax.broadcasted_iota(jnp.int32, (nodes, nodes), 0)
    col = lax.broadcasted_iota(jnp.int32, (nodes, nodes), 1)
    stiff = st_ref[...]
    spack_ref[...] = pack_matrix(jnp.where(row == col, 0.0, stiff))
    diag = jnp.sum(jnp.where(row == col, stiff, 0.0), axis=1, keepdims=True)
    coef_ref[DIAG] = jnp.broadcast_to(diag, (nodes, elements))
    shared = up_ref.shape[1]
    lines = nodes // LINE
    for side, (ref, first) in enumerate(((up_ref, LINE - 1), (lo_ref, 0))):
        index = ref[...]
        node = index // elements
        element = index - node * elements
        hot = lax.broadcasted_iota(jnp.int32, (elements, shared), 0) == element
        hot = jnp.where(hot, 1.0, 0.0)
        gather_ref[side] = hot.astype(BF16)
        back = hot.T.astype(BF16)
        scatter_ref[side] = back
        mask = lax.broadcasted_iota(jnp.int32, (lines, shared), 0) == node // LINE
        mask = jnp.where(mask, 1.0, 0.0)
        mask_ref[side] = mask
        count = dot(mask.astype(BF16), back)
        for s in range(lines):
            n = s * LINE + first
            coef_ref[DIAG, n : n + 1, :] = coef_ref[DIAG, n : n + 1, :] + PENALTY * count[s : s + 1]


def prepare(base_bank, snapshot, geometry, diff_r, diff_s, stiffness, upper, lower):
    nodes = diff_r.shape[0]
    elements = geometry.shape[1]
    shared = upper.shape[1]
    return pl.pallas_call(
        prep_kernel,
        out_shape=[
            jax.ShapeDtypeStruct((7, nodes, elements), F32),
            jax.ShapeDtypeStruct((2 * nodes, 3 * nodes), BF16),
            jax.ShapeDtypeStruct((nodes, 3 * nodes), BF16),
            jax.ShapeDtypeStruct((2, elements, shared), BF16),
            jax.ShapeDtypeStruct((2, shared, elements), BF16),
            jax.ShapeDtypeStruct((2, nodes // LINE, shared), F32),
        ],
        compiler_params=params(),
        cost_estimate=cost(1e7, 4e6),
        name="prepare",
    )(base_bank, snapshot.reshape(1, elements), geometry, diff_r, diff_s, stiffness, upper, lower)


def face_of(ref, side):
    rows, elements = ref.shape
    return ref.reshape(rows // LINE, LINE, elements).at[:, LINE - 1 if side == 0 else 0, :]


def gather_faces(side, fields, gather_ref, mask_ref):
    lines = mask_ref.shape[1]
    high, low = split(jnp.concatenate(fields, axis=0))
    rows = high.shape[0]
    both = dot(jnp.concatenate([high, low], axis=0), gather_ref[side])
    picked = both[:rows] + both[rows:]
    shared = picked.shape[1]
    return jnp.sum(picked.reshape(rows // lines, lines, shared) * mask_ref[side][None], axis=1)


def scatter_faces(side, values, scatter_ref, mask_ref):
    mask = mask_ref[side]
    coefs, shared = values.shape
    spread = (values[:, None, :] * mask[None]).reshape(coefs * mask.shape[0], shared)
    high, low = split(spread)
    rows = high.shape[0]
    both = dot(jnp.concatenate([high, low], axis=0), scatter_ref[side])
    return both[:rows] + both[rows:]


def local_sweep(pot, source, inverse, spack):
    applied = dot(spack, pack_field(pot))
    return (1.0 - RELAXATION) * pot + inverse * (source - applied)


def coef_block(coefs):
    return 8 if coefs % 8 == 0 else coefs


def start_kernel(
    block, pos_ref, z_ref, x_ref, geo_ref, diag_ref, dpack_ref, spack_ref, gather_ref, mask_ref,
    source_ref, inverse_ref, local_ref, up_ref, lo_ref, pot_ref,
):
    nodes, elements = diag_ref.shape[1:]
    beta = 4.0 / PLANES
    first = pos_ref[0] * (block * pl.num_programs(0)) + pl.program_id(0) * block
    rx = geo_ref[0:1, :]
    mass = 1.0 / (rx * geo_ref[1:2, :])
    diag = diag_ref[0]
    drpack = dpack_ref[:nodes]
    spack = spack_ref[...]
    for c in range(block):
        index = first + c
        wave = beta * (index // 2).astype(F32)
        shift = beta * jnp.where(index == 1, PLANES // 2, index // 2).astype(F32)
        shift = shift * shift
        z = z_ref[:, c].reshape(nodes, elements)
        other = x_ref[:, c + 1 if c % 2 == 0 else c - 1].reshape(nodes, elements)
        turned = (wave if c % 2 == 0 else -wave) * other
        source = turned - rx * dot(drpack, pack_field(z))
        inverse = RELAXATION / (diag + shift * mass)
        pot = inverse * source
        rows = pl.ds(c * nodes, nodes)
        source_ref[rows, :] = source
        inverse_ref[rows, :] = inverse
        pot_ref[rows, :] = pot
        local_ref[rows, :] = local_sweep(pot, source, inverse, spack)
    for side, out in ((0, up_ref), (1, lo_ref)):
        fields = [face_of(ref, side)[...] for ref in (pot_ref, local_ref, inverse_ref)]
        picked = gather_faces(side, fields, gather_ref, mask_ref)
        for k in range(3):
            out[k] = picked[k * block : (k + 1) * block]


def whole(shape):
    return pl.BlockSpec(shape, lambda *i: (0,) * len(shape))


SMEM_SPEC = pl.BlockSpec(memory_space=pltpu.SMEM)


def start_solve(position, z, x, geometry, coef, dpack, spack, gather, mask):
    groups, coefs, part, elements = z.shape
    nodes = groups * part
    shared = gather.shape[2]
    block = coef_block(coefs)
    field = pl.BlockSpec((groups, block, part, elements), lambda i: (0, i, 0, 0))
    flat = pl.BlockSpec((block * nodes, elements), lambda i: (i, 0))
    face = pl.BlockSpec((3, block, shared), lambda i: (0, i, 0))
    size = coefs * nodes * elements
    return pl.pallas_call(
        functools.partial(start_kernel, block),
        out_shape=[jax.ShapeDtypeStruct((coefs * nodes, elements), F32)] * 3
        + [jax.ShapeDtypeStruct((3, coefs, shared), F32)] * 2,
        grid=(coefs // block,),
        in_specs=[
            SMEM_SPEC, field, field, whole(geometry.shape),
            pl.BlockSpec((1, nodes, elements), lambda i: (DIAG, 0, 0)),
            whole(dpack.shape), whole(spack.shape), whole(gather.shape), whole(mask.shape),
        ],
        out_specs=[flat, flat, flat, face, face],
        scratch_shapes=[pltpu.VMEM((block * nodes, elements), F32)],
        compiler_params=params(),
        cost_estimate=cost(12 * nodes * size, 20 * size),
        name="start_solve",
    )(position, z, x, geometry, coef, dpack, spack, gather, mask)


def sweeps_kernel(
    block, keep, local_ref, source_ref, inverse_ref, own_up_ref, own_lo_ref,
    got_up_ref, got_lo_ref, inv_up_ref, inv_lo_ref, spack_ref, gather_ref, scatter_ref, mask_ref,
    next_ref, up_ref, lo_ref, pot_ref,
):
    nodes = spack_ref.shape[0]
    spack = spack_ref[...]
    lines = block * (nodes // LINE)
    partners = []
    for side, own, got, inv in (
        (0, own_up_ref, got_up_ref, inv_up_ref),
        (1, own_lo_ref, got_lo_ref, inv_lo_ref),
    ):
        now = got[0]
        later = got[1] + PENALTY * inv[0] * own[0]
        both = scatter_faces(side, jnp.concatenate([now, later], axis=0), scatter_ref, mask_ref)
        scale = PENALTY * face_of(inverse_ref, side)[...]
        partners.append((scale * both[:lines], scale * both[lines:]))
    pot_ref[...] = local_ref[...]
    for side in range(2):
        face = face_of(pot_ref, side)
        face[...] = face[...] + partners[side][0]
    for c in range(block):
        rows = pl.ds(c * nodes, nodes)
        pot_ref[rows, :] = local_sweep(pot_ref[rows, :], source_ref[rows, :], inverse_ref[rows, :], spack)
    for side in range(2):
        face = face_of(pot_ref, side)
        face[...] = face[...] + partners[side][1]
    for c in range(block):
        rows = pl.ds(c * nodes, nodes)
        next_ref[rows, :] = local_sweep(pot_ref[rows, :], source_ref[rows, :], inverse_ref[rows, :], spack)
    for side, out in ((0, up_ref), (1, lo_ref)):
        fields = [face_of(ref, side)[...] for ref in (pot_ref, next_ref)[:keep]]
        picked = gather_faces(side, fields, gather_ref, mask_ref)
        for k in range(keep):
            out[k] = picked[k * block : (k + 1) * block]


def two_sweeps(keep, local, source, inverse, own, got, inv, spack, gather, scatter, mask):
    nodes = spack.shape[0]
    elements = local.shape[1]
    coefs = local.shape[0] // nodes
    shared = gather.shape[2]
    block = coef_block(coefs)
    flat = pl.BlockSpec((block * nodes, elements), lambda i: (i, 0))
    one = pl.BlockSpec((1, block, shared), lambda i: (0, i, 0))
    two = pl.BlockSpec((2, block, shared), lambda i: (0, i, 0))
    third = pl.BlockSpec((1, block, shared), lambda i: (2, i, 0))
    face = pl.BlockSpec((keep, block, shared), lambda i: (0, i, 0))
    size = coefs * nodes * elements
    return pl.pallas_call(
        functools.partial(sweeps_kernel, block, keep),
        out_shape=[jax.ShapeDtypeStruct(local.shape, F32)]
        + [jax.ShapeDtypeStruct((keep, coefs, shared), F32)] * 2,
        grid=(coefs // block,),
        in_specs=[
            flat, flat, flat, one, one, two, two, third, third,
            whole(spack.shape), whole(gather.shape), whole(scatter.shape), whole(mask.shape),
        ],
        out_specs=[flat, face, face],
        scratch_shapes=[pltpu.VMEM((block * nodes, elements), F32)],
        compiler_params=params(),
        cost_estimate=cost(12 * nodes * size, 16 * size),
        name="two_sweeps",
    )(local, source, inverse, *own, *got, *inv, spack, gather, scatter, mask)


def partial_kernel(block, z_ref, x_ref, coef_ref, dpack_ref, o_ref):
    nodes, elements = coef_ref.shape[1:]
    dpack = dpack_ref[...]
    for c in range(block):
        z = z_ref[:, c].reshape(nodes, elements)
        slopes = dot(dpack, pack_field(z))
        moved = coef_ref[BXR] * slopes[:nodes] + coef_ref[BYS] * slopes[nodes:]
        o_ref[2, c] = z - TIME_STEP * (moved + INTERACTION * z)
        x = x_ref[:, c].reshape(nodes, elements)
        slopes = dot(dpack, pack_field(x))
        moved = coef_ref[BXR] * slopes[:nodes] + coef_ref[BYS] * slopes[nodes:]
        o_ref[0, c] = x + TIME_STEP * (x * coef_ref[DXBX] - moved - INTERACTION * x)
        o_ref[1, c] = TIME_STEP * (x * coef_ref[DYBX])


def partial_update(z, x, coef, dpack):
    groups, coefs, part, elements = z.shape
    nodes = groups * part
    block = coef_block(coefs)
    field = pl.BlockSpec((groups, block, part, elements), lambda i: (0, i, 0, 0))
    size = coefs * nodes * elements
    return pl.pallas_call(
        functools.partial(partial_kernel, block),
        out_shape=jax.ShapeDtypeStruct((3, coefs, nodes, elements), F32),
        grid=(coefs // block,),
        in_specs=[field, field, whole(coef.shape), whole(dpack.shape)],
        out_specs=pl.BlockSpec((3, block, nodes, elements), lambda i: (0, i, 0, 0)),
        compiler_params=params(),
        cost_estimate=cost(24 * nodes * size, 20 * size),
        name="partial_update",
    )(z, x, coef, dpack)


def force_kernel(
    block, pos_ref, local_ref, inverse_ref, got_up_ref, got_lo_ref, geo_ref, dpack_ref, scatter_ref,
    mask_ref, part_ref, o_ref, pot_ref,
):
    nodes = dpack_ref.shape[0] // 2
    scale = TIME_STEP * INTERACTION
    which = pl.program_id(1)

    @pl.when(which == 0)
    def _():
        pot_ref[...] = local_ref[...]
        for side, got in ((0, got_up_ref), (1, got_lo_ref)):
            face = face_of(pot_ref, side)
            partner = scatter_faces(side, got[0], scatter_ref, mask_ref)
            face[...] = face[...] + PENALTY * face_of(inverse_ref, side)[...] * partner
        first = pos_ref[0] * (block * pl.num_programs(0)) + pl.program_id(0) * block
        for c in range(block):
            wave = (4.0 / PLANES) * ((first + c) // 2).astype(F32)
            factor = scale * (wave if c % 2 == 0 else -wave)
            other = c + 1 if c % 2 == 0 else c - 1
            o_ref[0, c] = part_ref[0, c] + factor * pot_ref[pl.ds(other * nodes, nodes), :]

    @pl.when(which == 1)
    def _():
        drpack = dpack_ref[:nodes]
        factor = scale * geo_ref[0:1, :]
        for c in range(block):
            slope = dot(drpack, pack_field(pot_ref[pl.ds(c * nodes, nodes), :]))
            o_ref[0, c] = part_ref[0, c] - factor * slope


def add_force(position, local, inverse, got, geometry, dpack, scatter, mask, partial):
    _, coefs, nodes, elements = partial.shape
    shared = scatter.shape[1]
    block = coef_block(coefs)
    flat = pl.BlockSpec((block * nodes, elements), lambda i, j: (i, 0))
    one = pl.BlockSpec((1, block, shared), lambda i, j: (0, i, 0))
    comp = pl.BlockSpec((1, block, nodes, elements), lambda i, j: (2 * j, i, 0, 0))
    size = coefs * nodes * elements
    return pl.pallas_call(
        functools.partial(force_kernel, block),
        out_shape=jax.ShapeDtypeStruct(partial.shape, F32),
        grid=(coefs // block, 2),
        in_specs=[
            SMEM_SPEC, flat, flat, one, one, whole(geometry.shape), whole(dpack.shape),
            whole(scatter.shape), whole(mask.shape), comp,
        ],
        out_specs=comp,
        scratch_shapes=[pltpu.VMEM((block * nodes, elements), F32)],
        input_output_aliases={9: 0},
        compiler_params=params(),
        cost_estimate=cost(6 * nodes * size, 24 * size),
        name="add_force",
    )(position, local, inverse, *got, geometry, dpack, scatter, mask, partial)


def finish_kernel(block, y_ref, coef_ref, dpack_ref, part_ref, o_ref):
    nodes, elements = coef_ref.shape[1:]
    which = pl.program_id(1)

    @pl.when(which == 0)
    def _():
        for c in range(block):
            y = y_ref[:, c].reshape(nodes, elements)
            o_ref[0, c] = part_ref[0, c] + TIME_STEP * (y * coef_ref[DXBY])

    @pl.when(which == 1)
    def _():
        dpack = dpack_ref[...]
        for c in range(block):
            y = y_ref[:, c].reshape(nodes, elements)
            slopes = dot(dpack, pack_field(y))
            moved = coef_ref[BXR] * slopes[:nodes] + coef_ref[BYS] * slopes[nodes:]
            o_ref[0, c] = part_ref[0, c] + y + TIME_STEP * (y * coef_ref[DYBY] - moved)


def finish(y, coef, dpack, partial):
    groups, coefs, part, elements = y.shape
    nodes = groups * part
    block = coef_block(coefs)
    comp = pl.BlockSpec((1, block, nodes, elements), lambda i, j: (j, i, 0, 0))
    size = coefs * nodes * elements
    return pl.pallas_call(
        functools.partial(finish_kernel, block),
        out_shape=jax.ShapeDtypeStruct(partial.shape, F32),
        grid=(coefs // block, 2),
        in_specs=[
            pl.BlockSpec((groups, block, part, elements), lambda i, j: (0, i, 0, 0)),
            whole(coef.shape), whole(dpack.shape), comp,
        ],
        out_specs=comp,
        input_output_aliases={3: 0},
        compiler_params=params(),
        cost_estimate=cost(12 * nodes * size, 20 * size),
        name="finish",
    )(y, coef, dpack, partial)


def to_all(blocks):
    return lax.all_to_all(blocks, "four", split_axis=0, concat_axis=0, tiled=True)


def swap_faces(up, lo):
    peers = lax.axis_size("dom")
    up_way = [(i, (i + 1) % peers) for i in range(peers)]
    down_way = [(j, i) for i, j in up_way]
    return lax.ppermute(lo, "dom", down_way), lax.ppermute(up, "dom", up_way)


def per_device(
    adjoint, base_bank, snapshot, geometry, diff_r, diff_s, stiffness, upper_list, lower_list
):
    _, per, nodes, elements = adjoint.shape
    peers = lax.axis_size("four")
    share = nodes // peers
    table = jnp.asarray(coef_table(PLANES))
    position = lax.axis_index("four").astype(jnp.int32).reshape(1)

    def columns(comp):
        blocks = adjoint[comp].reshape(per, peers, share, elements)
        return to_all(jnp.swapaxes(blocks, 0, 1))

    def coefficients(cols):
        got = to_all(transform(cols, table))
        if share % 8:
            got = jnp.swapaxes(got, 0, 1).reshape(1, per, nodes, elements)
        return got

    z_cols = columns(2)
    x_cols = columns(0)
    coef, dpack, spack, gather, scatter, mask = prepare(
        base_bank, snapshot, geometry, diff_r, diff_s, stiffness, upper_list, lower_list
    )
    z = coefficients(z_cols)
    x = coefficients(x_cols)
    y_cols = columns(1)
    source, inverse, local, up, lo = start_solve(
        position, z, x, geometry, coef, dpack, spack, gather, mask
    )
    got = swap_faces(up, lo)
    inv = got
    partial = partial_update(z, x, coef, dpack)
    local, up, lo = two_sweeps(
        2, local, source, inverse, (up, lo), got, inv, spack, gather, scatter, mask
    )
    got = swap_faces(up, lo)
    local, up, lo = two_sweeps(
        1, local, source, inverse, (up, lo), got, inv, spack, gather, scatter, mask
    )
    got = swap_faces(up, lo)
    partial = add_force(position, local, inverse, got, geometry, dpack, scatter, mask, partial)
    y = coefficients(y_cols)
    return finish(y, coef, dpack, partial)


def solution(mesh):
    in_specs = (
        P(None, "four", None, "dom"),
        P(None, None, None, "dom"),
        P("dom"),
        P(None, "dom"),
        P(),
        P(),
        P(),
        P("dom", None),
        P("dom", None),
    )
    out_specs = P(None, "four", None, "dom")
    return jax.shard_map(
        per_device, mesh=mesh, in_specs=in_specs, out_specs=out_specs, check_vma=False
    )
```

```python
import functools
import math

import jax
import jax.numpy as jnp
import ml_dtypes
import numpy as np
from jax import lax
from jax.experimental import pallas as pl
from jax.experimental.pallas import tpu as pltpu
from jax.sharding import PartitionSpec as P

PLANES = 256
PENALTY = 0.5
RELAXATION = 0.8
TIME_STEP = 0.2
INTERACTION = 2.0
LINE = 8

F32 = jnp.float32
BF16 = jnp.bfloat16
VMEM_LIMIT = 60 * 1024 * 1024


def params():
    return pltpu.CompilerParams(vmem_limit_bytes=VMEM_LIMIT)


def cost(flops, moved):
    return pl.CostEstimate(flops=int(flops), bytes_accessed=int(moved), transcendentals=0)


def split(x):
    high = x.astype(BF16)
    low = (x - high.astype(F32)).astype(BF16)
    return high, low


def dot(a, b):
    return lax.dot_general(a, b, (((1,), (0,)), ((), ())), preferred_element_type=F32)


def pack_matrix(m):
    high, low = split(m)
    return jnp.concatenate([high, low, high], axis=1)


def pack_field(v):
    high, low = split(v)
    return jnp.concatenate([high, high, low], axis=0)


def coef_table(length):
    c = np.arange(length)[:, None]
    j = np.arange(length)[None, :]
    angle = ((c // 2) * j % length) * (2.0 * math.pi / length)
    table = np.where(c % 2 == 1, np.sin(angle), np.cos(angle)) * math.sqrt(2.0 / length)
    table[0] = 1.0 / math.sqrt(length)
    table[1] = np.where(np.arange(length) % 2 == 0, 1.0, -1.0) / math.sqrt(length)
    high = table.astype(ml_dtypes.bfloat16)
    low = (table - high.astype(np.float64)).astype(ml_dtypes.bfloat16)
    return np.concatenate([high, low], axis=0)


def transform_kernel(nodes, table_ref, x_ref, o_ref):
    planes = table_ref.shape[1]
    both = table_ref[...]
    high_table = both[:planes]
    width = x_ref.shape[-1]
    x_flat = x_ref.reshape(planes * nodes, width)
    o_flat = o_ref.reshape(planes * nodes, width)
    for n in range(nodes):
        rows = pl.ds(n, planes, stride=nodes) if nodes > 1 else pl.ds(0, planes)
        high, low = split(x_flat[rows, :])
        wide = dot(both, high)
        o_flat[rows, :] = wide[:planes] + (wide[planes:] + dot(high_table, low))


def transform(columns, table):
    peers, comps, per, nodes, elements = columns.shape
    width = 128
    block = pl.BlockSpec((peers, 1, per, nodes, width), lambda k, i: (0, k, 0, 0, i))
    size = columns.size
    return pl.pallas_call(
        functools.partial(transform_kernel, nodes),
        out_shape=jax.ShapeDtypeStruct(columns.shape, F32),
        grid=(comps, elements // width),
        in_specs=[pl.BlockSpec(table.shape, lambda k, i: (0, 0)), block],
        out_specs=block,
        compiler_params=params(),
        cost_estimate=cost(6 * PLANES * size, 8 * size),
        name="transform",
    )(table, columns)


def pack_kernel(x_ref, o_ref):
    part = o_ref.shape[3]
    for d in range(o_ref.shape[0]):
        o_ref[d, 0] = x_ref[0, :, d * part : (d + 1) * part, :]


def pack(adjoint, comps, peers):
    _, per, nodes, elements = adjoint.shape
    part = nodes // peers
    if part % 8:
        picked = jnp.stack([adjoint[k] for k in comps])
        return jnp.moveaxis(picked.reshape(len(comps), per, peers, part, elements), 2, 0)
    block = per // 4
    first = comps[0]
    step = comps[1] - first if len(comps) > 1 else 0
    size = len(comps) * per * nodes * elements
    return pl.pallas_call(
        pack_kernel,
        out_shape=jax.ShapeDtypeStruct((peers, len(comps), per, part, elements), F32),
        grid=(len(comps), per // block),
        in_specs=[pl.BlockSpec((1, block, nodes, elements), lambda k, q: (first + step * k, q, 0, 0))],
        out_specs=pl.BlockSpec((peers, 1, block, part, elements), lambda k, q: (0, k, q, 0, 0)),
        compiler_params=params(),
        cost_estimate=cost(0, 8 * size),
        name="pack",
    )(adjoint)


BXR, BYS, DXBX, DXBY, DYBX, DYBY, DIAG = range(7)


def prep_kernel(
    bank_ref, snap_ref, geo_ref, dr_ref, ds_ref, st_ref, up_ref, lo_ref,
    coef_ref, dpack_ref, spack_ref, gather_ref, scatter_ref, mask_ref,
):
    elements = geo_ref.shape[1]
    nodes = dr_ref.shape[0]
    snap = snap_ref[...]
    base = [
        sum(jnp.where(snap == k, bank_ref[k, i], 0.0) for k in range(bank_ref.shape[0]))
        for i in range(2)
    ]
    rx = geo_ref[0:1, :]
    sy = geo_ref[1:2, :]
    dpack = pack_matrix(jnp.concatenate([dr_ref[...], ds_ref[...]], axis=0))
    dpack_ref[...] = dpack
    bx = dot(dpack, pack_field(base[0]))
    by = dot(dpack, pack_field(base[1]))
    coef_ref[BXR] = base[0] * rx
    coef_ref[BYS] = base[1] * sy
    coef_ref[DXBX] = rx * bx[:nodes]
    coef_ref[DXBY] = rx * by[:nodes]
    coef_ref[DYBX] = sy * bx[nodes:]
    coef_ref[DYBY] = sy * by[nodes:]
    row = lax.broadcasted_iota(jnp.int32, (nodes, nodes), 0)
    col = lax.broadcasted_iota(jnp.int32, (nodes, nodes), 1)
    stiff = st_ref[...]
    spack_ref[...] = pack_matrix(jnp.where(row == col, 0.0, stiff))
    diag = jnp.sum(jnp.where(row == col, stiff, 0.0), axis=1, keepdims=True)
    coef_ref[DIAG] = jnp.broadcast_to(diag, (nodes, elements))
    shared = up_ref.shape[1]
    lines = nodes // LINE
    for side, (ref, first) in enumerate(((up_ref, LINE - 1), (lo_ref, 0))):
        index = ref[...]
        node = index // elements
        element = index - node * elements
        hot = lax.broadcasted_iota(jnp.int32, (elements, shared), 0) == element
        hot = jnp.where(hot, 1.0, 0.0)
        gather_ref[side] = hot.astype(BF16)
        back = hot.T.astype(BF16)
        scatter_ref[side] = back
        mask = lax.broadcasted_iota(jnp.int32, (lines, shared), 0) == node // LINE
        mask = jnp.where(mask, 1.0, 0.0)
        mask_ref[side] = mask
        count = dot(mask.astype(BF16), back)
        for s in range(lines):
            n = s * LINE + first
            coef_ref[DIAG, n : n + 1, :] = coef_ref[DIAG, n : n + 1, :] + PENALTY * count[s : s + 1]


def prepare(base_bank, snapshot, geometry, diff_r, diff_s, stiffness, upper, lower):
    nodes = diff_r.shape[0]
    elements = geometry.shape[1]
    shared = upper.shape[1]
    return pl.pallas_call(
        prep_kernel,
        out_shape=[
            jax.ShapeDtypeStruct((7, nodes, elements), F32),
            jax.ShapeDtypeStruct((2 * nodes, 3 * nodes), BF16),
            jax.ShapeDtypeStruct((nodes, 3 * nodes), BF16),
            jax.ShapeDtypeStruct((2, elements, shared), BF16),
            jax.ShapeDtypeStruct((2, shared, elements), BF16),
            jax.ShapeDtypeStruct((2, nodes // LINE, shared), F32),
        ],
        compiler_params=params(),
        cost_estimate=cost(1e7, 4e6),
        name="prepare",
    )(base_bank, snapshot.reshape(1, elements), geometry, diff_r, diff_s, stiffness, upper, lower)


def face_of(ref, side):
    rows, elements = ref.shape
    return ref.reshape(rows // LINE, LINE, elements).at[:, LINE - 1 if side == 0 else 0, :]


def gather_faces(side, fields, gather_ref, mask_ref):
    lines = mask_ref.shape[1]
    high, low = split(jnp.concatenate(fields, axis=0))
    rows = high.shape[0]
    both = dot(jnp.concatenate([high, low], axis=0), gather_ref[side])
    picked = both[:rows] + both[rows:]
    shared = picked.shape[1]
    return jnp.sum(picked.reshape(rows // lines, lines, shared) * mask_ref[side][None], axis=1)


def scatter_faces(side, values, scatter_ref, mask_ref):
    mask = mask_ref[side]
    coefs, shared = values.shape
    spread = (values[:, None, :] * mask[None]).reshape(coefs * mask.shape[0], shared)
    high, low = split(spread)
    rows = high.shape[0]
    both = dot(jnp.concatenate([high, low], axis=0), scatter_ref[side])
    return both[:rows] + both[rows:]


def local_sweep(pot, source, inverse, spack):
    applied = dot(spack, pack_field(pot))
    return (1.0 - RELAXATION) * pot + inverse * (source - applied)


def coef_block(coefs):
    return 8 if coefs % 8 == 0 else coefs


def start_kernel(
    block, pos_ref, z_ref, x_ref, geo_ref, diag_ref, dpack_ref, spack_ref, gather_ref, mask_ref,
    source_ref, inverse_ref, local_ref, up_ref, lo_ref, pot_ref,
):
    nodes, elements = diag_ref.shape[1:]
    beta = 4.0 / PLANES
    first = pos_ref[0] * (block * pl.num_programs(0)) + pl.program_id(0) * block
    rx = geo_ref[0:1, :]
    mass = 1.0 / (rx * geo_ref[1:2, :])
    diag = diag_ref[0]
    drpack = dpack_ref[:nodes]
    spack = spack_ref[...]
    for c in range(block):
        index = first + c
        wave = beta * (index // 2).astype(F32)
        shift = beta * jnp.where(index == 1, PLANES // 2, index // 2).astype(F32)
        shift = shift * shift
        z = z_ref[:, 0, c].reshape(nodes, elements)
        other = x_ref[:, 0, c + 1 if c % 2 == 0 else c - 1].reshape(nodes, elements)
        turned = (wave if c % 2 == 0 else -wave) * other
        source = turned - rx * dot(drpack, pack_field(z))
        inverse = RELAXATION / (diag + shift * mass)
        pot = inverse * source
        rows = pl.ds(c * nodes, nodes)
        source_ref[rows, :] = source
        inverse_ref[rows, :] = inverse
        pot_ref[rows, :] = pot
        local_ref[rows, :] = local_sweep(pot, source, inverse, spack)
    for side, out in ((0, up_ref), (1, lo_ref)):
        fields = [face_of(ref, side)[...] for ref in (pot_ref, local_ref, inverse_ref)]
        picked = gather_faces(side, fields, gather_ref, mask_ref)
        for k in range(3):
            out[k] = picked[k * block : (k + 1) * block]


def whole(shape):
    return pl.BlockSpec(shape, lambda *i: (0,) * len(shape))


SMEM_SPEC = pl.BlockSpec(memory_space=pltpu.SMEM)


def start_solve(position, zx, geometry, coef, dpack, spack, gather, mask):
    groups, _, coefs, part, elements = zx.shape
    nodes = groups * part
    shared = gather.shape[2]
    block = coef_block(coefs)
    z_spec, x_spec = (
        pl.BlockSpec((groups, 1, block, part, elements), lambda i, k=k: (0, k, i, 0, 0)) for k in range(2)
    )
    flat = pl.BlockSpec((block * nodes, elements), lambda i: (i, 0))
    face = pl.BlockSpec((3, block, shared), lambda i: (0, i, 0))
    size = coefs * nodes * elements
    return pl.pallas_call(
        functools.partial(start_kernel, block),
        out_shape=[jax.ShapeDtypeStruct((coefs * nodes, elements), F32)] * 3
        + [jax.ShapeDtypeStruct((3, coefs, shared), F32)] * 2,
        grid=(coefs // block,),
        in_specs=[
            SMEM_SPEC, z_spec, x_spec, whole(geometry.shape),
            pl.BlockSpec((1, nodes, elements), lambda i: (DIAG, 0, 0)),
            whole(dpack.shape), whole(spack.shape), whole(gather.shape), whole(mask.shape),
        ],
        out_specs=[flat, flat, flat, face, face],
        scratch_shapes=[pltpu.VMEM((block * nodes, elements), F32)],
        compiler_params=params(),
        cost_estimate=cost(12 * nodes * size, 20 * size),
        name="start_solve",
    )(position, zx, zx, geometry, coef, dpack, spack, gather, mask)


def sweeps_kernel(
    block, keep, local_ref, source_ref, inverse_ref, own_up_ref, own_lo_ref,
    got_up_ref, got_lo_ref, inv_up_ref, inv_lo_ref, spack_ref, gather_ref, scatter_ref, mask_ref,
    next_ref, up_ref, lo_ref, pot_ref,
):
    nodes = spack_ref.shape[0]
    spack = spack_ref[...]
    lines = block * (nodes // LINE)
    partners = []
    for side, own, got, inv in (
        (0, own_up_ref, got_up_ref, inv_up_ref),
        (1, own_lo_ref, got_lo_ref, inv_lo_ref),
    ):
        now = got[0]
        later = got[1] + PENALTY * inv[0] * own[0]
        both = scatter_faces(side, jnp.concatenate([now, later], axis=0), scatter_ref, mask_ref)
        scale = PENALTY * face_of(inverse_ref, side)[...]
        partners.append((scale * both[:lines], scale * both[lines:]))
    pot_ref[...] = local_ref[...]
    for side in range(2):
        face = face_of(pot_ref, side)
        face[...] = face[...] + partners[side][0]
    for c in range(block):
        rows = pl.ds(c * nodes, nodes)
        pot_ref[rows, :] = local_sweep(pot_ref[rows, :], source_ref[rows, :], inverse_ref[rows, :], spack)
    for side in range(2):
        face = face_of(pot_ref, side)
        face[...] = face[...] + partners[side][1]
    for c in range(block):
        rows = pl.ds(c * nodes, nodes)
        next_ref[rows, :] = local_sweep(pot_ref[rows, :], source_ref[rows, :], inverse_ref[rows, :], spack)
    for side, out in ((0, up_ref), (1, lo_ref)):
        fields = [face_of(ref, side)[...] for ref in (pot_ref, next_ref)[:keep]]
        picked = gather_faces(side, fields, gather_ref, mask_ref)
        for k in range(keep):
            out[k] = picked[k * block : (k + 1) * block]


def two_sweeps(keep, local, source, inverse, own, got, inv, spack, gather, scatter, mask):
    nodes = spack.shape[0]
    elements = local.shape[1]
    coefs = local.shape[0] // nodes
    shared = gather.shape[2]
    block = coef_block(coefs)
    flat = pl.BlockSpec((block * nodes, elements), lambda i: (i, 0))
    one = pl.BlockSpec((1, block, shared), lambda i: (0, i, 0))
    two = pl.BlockSpec((2, block, shared), lambda i: (0, i, 0))
    third = pl.BlockSpec((1, block, shared), lambda i: (2, i, 0))
    face = pl.BlockSpec((keep, block, shared), lambda i: (0, i, 0))
    size = coefs * nodes * elements
    return pl.pallas_call(
        functools.partial(sweeps_kernel, block, keep),
        out_shape=[jax.ShapeDtypeStruct(local.shape, F32)]
        + [jax.ShapeDtypeStruct((keep, coefs, shared), F32)] * 2,
        grid=(coefs // block,),
        in_specs=[
            flat, flat, flat, one, one, two, two, third, third,
            whole(spack.shape), whole(gather.shape), whole(scatter.shape), whole(mask.shape),
        ],
        out_specs=[flat, face, face],
        scratch_shapes=[pltpu.VMEM((block * nodes, elements), F32)],
        compiler_params=params(),
        cost_estimate=cost(12 * nodes * size, 16 * size),
        name="two_sweeps",
    )(local, source, inverse, *own, *got, *inv, spack, gather, scatter, mask)


def partial_kernel(block, z_ref, x_ref, coef_ref, dpack_ref, o_ref):
    nodes, elements = coef_ref.shape[1:]
    dpack = dpack_ref[...]
    for c in range(block):
        z = z_ref[:, 0, c].reshape(nodes, elements)
        slopes = dot(dpack, pack_field(z))
        moved = coef_ref[BXR] * slopes[:nodes] + coef_ref[BYS] * slopes[nodes:]
        o_ref[2, c] = z - TIME_STEP * (moved + INTERACTION * z)
        x = x_ref[:, 0, c].reshape(nodes, elements)
        slopes = dot(dpack, pack_field(x))
        moved = coef_ref[BXR] * slopes[:nodes] + coef_ref[BYS] * slopes[nodes:]
        o_ref[0, c] = x + TIME_STEP * (x * coef_ref[DXBX] - moved - INTERACTION * x)
        o_ref[1, c] = TIME_STEP * (x * coef_ref[DYBX])


def partial_update(zx, coef, dpack):
    groups, _, coefs, part, elements = zx.shape
    nodes = groups * part
    block = coef_block(coefs)
    z_spec, x_spec = (
        pl.BlockSpec((groups, 1, block, part, elements), lambda i, k=k: (0, k, i, 0, 0)) for k in range(2)
    )
    size = coefs * nodes * elements
    return pl.pallas_call(
        functools.partial(partial_kernel, block),
        out_shape=jax.ShapeDtypeStruct((3, coefs, nodes, elements), F32),
        grid=(coefs // block,),
        in_specs=[z_spec, x_spec, whole(coef.shape), whole(dpack.shape)],
        out_specs=pl.BlockSpec((3, block, nodes, elements), lambda i: (0, i, 0, 0)),
        compiler_params=params(),
        cost_estimate=cost(24 * nodes * size, 20 * size),
        name="partial_update",
    )(zx, zx, coef, dpack)


def force_kernel(
    block, pos_ref, local_ref, inverse_ref, got_up_ref, got_lo_ref, geo_ref, dpack_ref, scatter_ref,
    mask_ref, part_ref, o_ref, pot_ref,
):
    nodes = dpack_ref.shape[0] // 2
    scale = TIME_STEP * INTERACTION
    which = pl.program_id(1)

    @pl.when(which == 0)
    def _():
        pot_ref[...] = local_ref[...]
        for side, got in ((0, got_up_ref), (1, got_lo_ref)):
            face = face_of(pot_ref, side)
            partner = scatter_faces(side, got[0], scatter_ref, mask_ref)
            face[...] = face[...] + PENALTY * face_of(inverse_ref, side)[...] * partner
        first = pos_ref[0] * (block * pl.num_programs(0)) + pl.program_id(0) * block
        for c in range(block):
            wave = (4.0 / PLANES) * ((first + c) // 2).astype(F32)
            factor = scale * (wave if c % 2 == 0 else -wave)
            other = c + 1 if c % 2 == 0 else c - 1
            o_ref[0, c] = part_ref[0, c] + factor * pot_ref[pl.ds(other * nodes, nodes), :]

    @pl.when(which == 1)
    def _():
        drpack = dpack_ref[:nodes]
        factor = scale * geo_ref[0:1, :]
        for c in range(block):
            slope = dot(drpack, pack_field(pot_ref[pl.ds(c * nodes, nodes), :]))
            o_ref[0, c] = part_ref[0, c] - factor * slope


def add_force(position, local, inverse, got, geometry, dpack, scatter, mask, partial):
    _, coefs, nodes, elements = partial.shape
    shared = scatter.shape[1]
    block = coef_block(coefs)
    flat = pl.BlockSpec((block * nodes, elements), lambda i, j: (i, 0))
    one = pl.BlockSpec((1, block, shared), lambda i, j: (0, i, 0))
    comp = pl.BlockSpec((1, block, nodes, elements), lambda i, j: (2 * j, i, 0, 0))
    size = coefs * nodes * elements
    return pl.pallas_call(
        functools.partial(force_kernel, block),
        out_shape=jax.ShapeDtypeStruct(partial.shape, F32),
        grid=(coefs // block, 2),
        in_specs=[
            SMEM_SPEC, flat, flat, one, one, whole(geometry.shape), whole(dpack.shape),
            whole(scatter.shape), whole(mask.shape), comp,
        ],
        out_specs=comp,
        scratch_shapes=[pltpu.VMEM((block * nodes, elements), F32)],
        input_output_aliases={9: 0},
        compiler_params=params(),
        cost_estimate=cost(6 * nodes * size, 24 * size),
        name="add_force",
    )(position, local, inverse, *got, geometry, dpack, scatter, mask, partial)


def finish_kernel(block, y_ref, coef_ref, dpack_ref, part_ref, o_ref):
    nodes, elements = coef_ref.shape[1:]
    which = pl.program_id(1)

    @pl.when(which == 0)
    def _():
        for c in range(block):
            y = y_ref[:, 0, c].reshape(nodes, elements)
            o_ref[0, c] = part_ref[0, c] + TIME_STEP * (y * coef_ref[DXBY])

    @pl.when(which == 1)
    def _():
        dpack = dpack_ref[...]
        for c in range(block):
            y = y_ref[:, 0, c].reshape(nodes, elements)
            slopes = dot(dpack, pack_field(y))
            moved = coef_ref[BXR] * slopes[:nodes] + coef_ref[BYS] * slopes[nodes:]
            o_ref[0, c] = part_ref[0, c] + y + TIME_STEP * (y * coef_ref[DYBY] - moved)


def finish(y, coef, dpack, partial):
    groups, _, coefs, part, elements = y.shape
    nodes = groups * part
    block = coef_block(coefs)
    comp = pl.BlockSpec((1, block, nodes, elements), lambda i, j: (j, i, 0, 0))
    size = coefs * nodes * elements
    return pl.pallas_call(
        functools.partial(finish_kernel, block),
        out_shape=jax.ShapeDtypeStruct(partial.shape, F32),
        grid=(coefs // block, 2),
        in_specs=[
            pl.BlockSpec((groups, 1, block, part, elements), lambda i, j: (0, 0, i, 0, 0)),
            whole(coef.shape), whole(dpack.shape), comp,
        ],
        out_specs=comp,
        input_output_aliases={3: 0},
        compiler_params=params(),
        cost_estimate=cost(12 * nodes * size, 20 * size),
        name="finish",
    )(y, coef, dpack, partial)


def to_all(blocks):
    return lax.all_to_all(blocks, "four", split_axis=0, concat_axis=0, tiled=True)


def swap_faces(up, lo):
    peers = lax.axis_size("dom")
    up_way = [(i, (i + 1) % peers) for i in range(peers)]
    down_way = [(j, i) for i, j in up_way]
    return lax.ppermute(lo, "dom", down_way), lax.ppermute(up, "dom", up_way)


def per_device(
    adjoint, base_bank, snapshot, geometry, diff_r, diff_s, stiffness, upper_list, lower_list
):
    _, per, nodes, elements = adjoint.shape
    peers = lax.axis_size("four")
    share = nodes // peers
    table = jnp.asarray(coef_table(PLANES))
    position = lax.axis_index("four").astype(jnp.int32).reshape(1)

    def coefficients(columns):
        got = to_all(transform(columns, table))
        if share % 8:
            comps = got.shape[1]
            got = jnp.moveaxis(got, 0, 2).reshape(1, comps, per, nodes, elements)
        return got

    zx_sent = pack(adjoint, (2, 0), peers)
    zx_columns = to_all(zx_sent)
    coef, dpack, spack, gather, scatter, mask = prepare(
        base_bank, snapshot, geometry, diff_r, diff_s, stiffness, upper_list, lower_list
    )
    y_sent = pack(adjoint, (1,), peers)
    zx = coefficients(zx_columns)
    zx, y_sent = lax.optimization_barrier((zx, y_sent))
    y_columns = to_all(y_sent)
    source, inverse, local, up, lo = start_solve(
        position, zx, geometry, coef, dpack, spack, gather, mask
    )
    got = swap_faces(up, lo)
    inv = got
    partial = partial_update(zx, coef, dpack)
    local, up, lo = two_sweeps(
        2, local, source, inverse, (up, lo), got, inv, spack, gather, scatter, mask
    )
    got = swap_faces(up, lo)
    local, up, lo = two_sweeps(
        1, local, source, inverse, (up, lo), got, inv, spack, gather, scatter, mask
    )
    got = swap_faces(up, lo)
    partial = add_force(position, local, inverse, got, geometry, dpack, scatter, mask, partial)
    y = coefficients(y_columns)
    return finish(y, coef, dpack, partial)


def solution(mesh):
    in_specs = (
        P(None, "four", None, "dom"),
        P(None, None, None, "dom"),
        P("dom"),
        P(None, "dom"),
        P(),
        P(),
        P(),
        P("dom", None),
        P("dom", None),
    )
    out_specs = P(None, "four", None, "dom")
    return jax.shard_map(
        per_device, mesh=mesh, in_specs=in_specs, out_specs=out_specs, check_vma=False
    )
```

```python
import functools
import math

import jax
import jax.numpy as jnp
import ml_dtypes
import numpy as np
from jax import lax
from jax.experimental import pallas as pl
from jax.experimental.pallas import tpu as pltpu
from jax.sharding import PartitionSpec as P

PLANES = 256
PENALTY = 0.5
RELAXATION = 0.8
TIME_STEP = 0.2
INTERACTION = 2.0
LINE = 8

F32 = jnp.float32
BF16 = jnp.bfloat16
VMEM_LIMIT = 48 * 1024 * 1024
SMEM_SPEC = pl.BlockSpec(memory_space=pltpu.SMEM)


def params():
    return pltpu.CompilerParams(vmem_limit_bytes=VMEM_LIMIT)


def cost(flops, moved):
    return pl.CostEstimate(flops=int(flops), bytes_accessed=int(moved), transcendentals=0)


def split(x):
    high = x.astype(BF16)
    low = (x - high.astype(F32)).astype(BF16)
    return high, low


def dot(a, b):
    return lax.dot_general(a, b, (((1,), (0,)), ((), ())), preferred_element_type=F32)


def pack_matrix(m):
    high, low = split(m)
    return jnp.concatenate([high, low, high], axis=1)


def slab(refs, c):
    return jnp.concatenate([ref[c] for ref in refs], axis=0)


def pack_field(v):
    high, low = split(v)
    return jnp.concatenate([high, high, low], axis=0)


def coef_table(length):
    c = np.arange(length)[:, None]
    j = np.arange(length)[None, :]
    angle = ((c // 2) * j % length) * (2.0 * math.pi / length)
    table = np.where(c % 2 == 1, np.sin(angle), np.cos(angle)) * math.sqrt(2.0 / length)
    table[0] = 1.0 / math.sqrt(length)
    table[1] = np.where(np.arange(length) % 2 == 0, 1.0, -1.0) / math.sqrt(length)
    high = table.astype(ml_dtypes.bfloat16)
    low = (table - high.astype(np.float64)).astype(ml_dtypes.bfloat16)
    return np.concatenate([high, low], axis=0)


def permute_kernel(peers, pos_ref, table_ref, o_ref):
    planes = table_ref.shape[1]
    per = planes // peers
    me = pos_ref[1]
    row = lax.broadcasted_iota(jnp.int32, (planes, planes), 0)
    col = lax.broadcasted_iota(jnp.int32, (planes, planes), 1)
    swap = jnp.where(row == ((col // per) ^ me) * per + col % per, 1.0, 0.0).astype(BF16)
    for half in range(2):
        rows = pl.ds(half * planes, planes)
        turned = dot(swap, table_ref[rows, :]).astype(BF16)
        o_ref[rows, :] = dot(turned, swap).astype(BF16)


def permuted_table(position, table, peers):
    return pl.pallas_call(
        functools.partial(permute_kernel, peers),
        out_shape=jax.ShapeDtypeStruct(table.shape, BF16),
        in_specs=[SMEM_SPEC, pl.BlockSpec(memory_space=pltpu.VMEM)],
        compiler_params=params(),
        cost_estimate=cost(1e8, 4e6),
        name="permuted_table",
    )(position, table)


def transform_kernel(count, table_ref, *refs):
    planes = table_ref.shape[1]
    both = table_ref[...]
    high_table = both[:planes]
    per, nodes, width = refs[0].shape
    flat = [ref.reshape(per * nodes, width) for ref in refs]
    for n in range(nodes):
        rows = pl.ds(n, per, stride=nodes) if nodes > 1 else pl.ds(0, per)
        high, low = split(jnp.concatenate([ref[rows, :] for ref in flat[:count]], axis=0))
        wide = dot(both, high)
        result = wide[:planes] + (wide[planes:] + dot(high_table, low))
        for d, ref in enumerate(flat[count:]):
            ref[rows, :] = result[d * per : (d + 1) * per]


def transform(blocks, table):
    per, nodes, elements = blocks[0].shape
    width = 128
    block = pl.BlockSpec((per, nodes, width), lambda i: (0, 0, i))
    size = len(blocks) * blocks[0].size
    return pl.pallas_call(
        functools.partial(transform_kernel, len(blocks)),
        out_shape=[jax.ShapeDtypeStruct(v.shape, F32) for v in blocks],
        grid=(elements // width,),
        in_specs=[pl.BlockSpec(table.shape, lambda i: (0, 0))] + [block] * len(blocks),
        out_specs=[block] * len(blocks),
        compiler_params=params(),
        cost_estimate=cost(6 * PLANES * size, 20 * size),
        name="transform",
    )(table, *blocks)


def pack_kernel(pos_ref, *refs):
    count = len(refs) // 2
    for source, target in zip(refs[:count], refs[count:]):
        target[...] = source[0]


def pack(position, adjoint, comp, peers):
    _, per, nodes, elements = adjoint.shape
    part = nodes // peers
    block = per // 2

    def source(d):
        return pl.BlockSpec((1, block, part, elements), lambda i, pos: (comp, i, pos[1] ^ d, 0))

    size = per * nodes * elements
    return pl.pallas_call(
        pack_kernel,
        out_shape=[jax.ShapeDtypeStruct((per, part, elements), F32)] * peers,
        grid_spec=pltpu.PrefetchScalarGridSpec(
            num_scalar_prefetch=1,
            grid=(per // block,),
            in_specs=[source(d) for d in range(peers)],
            out_specs=[pl.BlockSpec((block, part, elements), lambda i, pos: (i, 0, 0))] * peers,
        ),
        compiler_params=params(),
        cost_estimate=cost(0, 16 * size),
        name="pack",
    )(position, *[adjoint] * peers)


BXR, BYS, DXBX, DXBY, DYBX, DYBY, DIAG = range(7)


def line_of(me, d):
    return pl.ds(pl.multiple_of((me ^ d) * LINE, LINE), LINE)


def own_order(ref, me, *lead):
    lines = ref.shape[-2] // LINE
    return jnp.concatenate([ref[(*lead, line_of(me, d), slice(None))] for d in range(lines)], axis=0)


def prep_kernel(
    pos_ref, bank_ref, snap_ref, geo_ref, dr_ref, ds_ref, st_ref, up_ref, lo_ref,
    coef_ref, dpack_ref, spack_ref, gather_ref, scatter_ref, mask_ref,
):
    elements = geo_ref.shape[1]
    nodes = dr_ref.shape[0]
    lines = nodes // LINE
    me = pos_ref[1]
    row = lax.broadcasted_iota(jnp.int32, (nodes, nodes), 0)
    col = lax.broadcasted_iota(jnp.int32, (nodes, nodes), 1)
    swap = jnp.where(row == ((col // LINE) ^ me) * LINE + col % LINE, 1.0, 0.0).astype(BF16)

    def permuted(ref):
        high, low = split(own_order(ref, me))
        return dot(high, swap) + dot(low, swap)

    snap = snap_ref[...]
    base = [
        sum(
            jnp.where(snap == k, own_order(bank_ref, me, k, i), 0.0)
            for k in range(bank_ref.shape[0])
        )
        for i in range(2)
    ]
    rx = geo_ref[0:1, :]
    sy = geo_ref[1:2, :]
    dpack = pack_matrix(jnp.concatenate([permuted(dr_ref), permuted(ds_ref)], axis=0))
    dpack_ref[...] = dpack
    bx = dot(dpack, pack_field(base[0]))
    by = dot(dpack, pack_field(base[1]))
    coef_ref[BXR] = base[0] * rx
    coef_ref[BYS] = base[1] * sy
    coef_ref[DXBX] = rx * bx[:nodes]
    coef_ref[DXBY] = rx * by[:nodes]
    coef_ref[DYBX] = sy * bx[nodes:]
    coef_ref[DYBY] = sy * by[nodes:]
    diag = jnp.sum(jnp.where(row == col, st_ref[...], 0.0), axis=0, keepdims=True)
    own = ((row // LINE) ^ me) * LINE + row % LINE == col
    diag = jnp.sum(jnp.where(own, diag, 0.0), axis=1, keepdims=True)
    spack_ref[...] = pack_matrix(jnp.where(row == col, 0.0, permuted(st_ref)))
    coef_ref[DIAG] = jnp.broadcast_to(diag, (nodes, elements))
    shared = up_ref.shape[1]
    for side, (ref, first) in enumerate(((up_ref, LINE - 1), (lo_ref, 0))):
        index = ref[...]
        node = index // elements
        element = index - node * elements
        hot = lax.broadcasted_iota(jnp.int32, (elements, shared), 0) == element
        hot = jnp.where(hot, 1.0, 0.0)
        gather_ref[side] = hot.astype(BF16)
        back = hot.T.astype(BF16)
        scatter_ref[side] = back
        mask = (lax.broadcasted_iota(jnp.int32, (lines, shared), 0) ^ me) == node // LINE
        mask = jnp.where(mask, 1.0, 0.0)
        mask_ref[side] = mask
        count = dot(mask.astype(BF16), back)
        for s in range(lines):
            n = s * LINE + first
            coef_ref[DIAG, n : n + 1, :] = coef_ref[DIAG, n : n + 1, :] + PENALTY * count[s : s + 1]


def prepare(position, base_bank, snapshot, geometry, diff_r, diff_s, stiffness, upper, lower):
    nodes = diff_r.shape[0]
    elements = geometry.shape[1]
    shared = upper.shape[1]
    return pl.pallas_call(
        prep_kernel,
        out_shape=[
            jax.ShapeDtypeStruct((7, nodes, elements), F32),
            jax.ShapeDtypeStruct((2 * nodes, 3 * nodes), BF16),
            jax.ShapeDtypeStruct((nodes, 3 * nodes), BF16),
            jax.ShapeDtypeStruct((2, elements, shared), BF16),
            jax.ShapeDtypeStruct((2, shared, elements), BF16),
            jax.ShapeDtypeStruct((2, nodes // LINE, shared), F32),
        ],
        in_specs=[SMEM_SPEC] + [pl.BlockSpec(memory_space=pltpu.VMEM)] * 8,
        compiler_params=params(),
        cost_estimate=cost(1e7, 8e6),
        name="prepare",
    )(position, base_bank, snapshot.reshape(1, elements), geometry, diff_r, diff_s, stiffness, upper, lower)


def face_of(ref, side):
    rows, elements = ref.shape
    return ref.reshape(rows // LINE, LINE, elements).at[:, LINE - 1 if side == 0 else 0, :]


def gather_faces(side, fields, gather_ref, mask_ref):
    lines = mask_ref.shape[1]
    high, low = split(jnp.concatenate(fields, axis=0))
    rows = high.shape[0]
    both = dot(jnp.concatenate([high, low], axis=0), gather_ref[side])
    picked = both[:rows] + both[rows:]
    shared = picked.shape[1]
    return jnp.sum(picked.reshape(rows // lines, lines, shared) * mask_ref[side][None], axis=1)


def scatter_faces(side, values, scatter_ref, mask_ref):
    mask = mask_ref[side]
    coefs, shared = values.shape
    spread = (values[:, None, :] * mask[None]).reshape(coefs * mask.shape[0], shared)
    high, low = split(spread)
    rows = high.shape[0]
    both = dot(jnp.concatenate([high, low], axis=0), scatter_ref[side])
    return both[:rows] + both[rows:]


def local_sweep(pot, source, inverse, spack):
    applied = dot(spack, pack_field(pot))
    return (1.0 - RELAXATION) * pot + inverse * (source - applied)


def coef_block(coefs):
    return 8 if coefs % 8 == 0 else coefs


def start_kernel(
    block, count, pos_ref, geo_ref, diag_ref, dpack_ref, spack_ref, gather_ref, mask_ref, *refs
):
    z_refs, x_refs = refs[:count], refs[count : 2 * count]
    source_ref, inverse_ref, local_ref, up_ref, lo_ref, pot_ref = refs[2 * count :]
    nodes, elements = diag_ref.shape[1:]
    beta = 4.0 / PLANES
    first = pos_ref[0] * (block * pl.num_programs(0)) + pl.program_id(0) * block
    rx = geo_ref[0:1, :]
    mass = 1.0 / (rx * geo_ref[1:2, :])
    diag = diag_ref[0]
    drpack = dpack_ref[:nodes]
    spack = spack_ref[...]
    for c in range(block):
        index = first + c
        wave = beta * (index // 2).astype(F32)
        shift = beta * jnp.where(index == 1, PLANES // 2, index // 2).astype(F32)
        shift = shift * shift
        z = slab(z_refs, c)
        other = slab(x_refs, c + 1 if c % 2 == 0 else c - 1)
        turned = (wave if c % 2 == 0 else -wave) * other
        source = turned - rx * dot(drpack, pack_field(z))
        inverse = RELAXATION / (diag + shift * mass)
        pot = inverse * source
        rows = pl.ds(c * nodes, nodes)
        source_ref[rows, :] = source
        inverse_ref[rows, :] = inverse
        pot_ref[rows, :] = pot
        local_ref[rows, :] = local_sweep(pot, source, inverse, spack)
    for side, out in ((0, up_ref), (1, lo_ref)):
        fields = [face_of(ref, side)[...] for ref in (pot_ref, local_ref, inverse_ref)]
        picked = gather_faces(side, fields, gather_ref, mask_ref)
        for k in range(3):
            out[k] = picked[k * block : (k + 1) * block]


def whole(shape):
    return pl.BlockSpec(shape, lambda *i: (0,) * len(shape))


def start_solve(position, z, x, geometry, coef, dpack, spack, gather, mask):
    coefs, part, elements = z[0].shape
    nodes = len(z) * part
    shared = gather.shape[2]
    block = coef_block(coefs)
    field = [pl.BlockSpec((block, part, elements), lambda i: (i, 0, 0))] * len(z)
    flat = pl.BlockSpec((block * nodes, elements), lambda i: (i, 0))
    face = pl.BlockSpec((3, block, shared), lambda i: (0, i, 0))
    size = coefs * nodes * elements
    return pl.pallas_call(
        functools.partial(start_kernel, block, len(z)),
        out_shape=[jax.ShapeDtypeStruct((coefs * nodes, elements), F32)] * 3
        + [jax.ShapeDtypeStruct((3, coefs, shared), F32)] * 2,
        grid=(coefs // block,),
        in_specs=[
            SMEM_SPEC, whole(geometry.shape),
            pl.BlockSpec((1, nodes, elements), lambda i: (DIAG, 0, 0)),
            whole(dpack.shape), whole(spack.shape), whole(gather.shape), whole(mask.shape),
            *field, *field,
        ],
        out_specs=[flat, flat, flat, face, face],
        scratch_shapes=[pltpu.VMEM((block * nodes, elements), F32)],
        compiler_params=params(),
        cost_estimate=cost(12 * nodes * size, 20 * size),
        name="start_solve",
    )(position, geometry, coef, dpack, spack, gather, mask, *z, *x)


def sweeps_kernel(
    block, keep, local_ref, source_ref, inverse_ref, own_up_ref, own_lo_ref,
    got_up_ref, got_lo_ref, inv_up_ref, inv_lo_ref, spack_ref, gather_ref, scatter_ref, mask_ref,
    next_ref, up_ref, lo_ref, pot_ref,
):
    nodes = spack_ref.shape[0]
    spack = spack_ref[...]
    lines = block * (nodes // LINE)
    partners = []
    for side, own, got, inv in (
        (0, own_up_ref, got_up_ref, inv_up_ref),
        (1, own_lo_ref, got_lo_ref, inv_lo_ref),
    ):
        now = got[0]
        later = got[1] + PENALTY * inv[0] * own[0]
        both = scatter_faces(side, jnp.concatenate([now, later], axis=0), scatter_ref, mask_ref)
        scale = PENALTY * face_of(inverse_ref, side)[...]
        partners.append((scale * both[:lines], scale * both[lines:]))
    pot_ref[...] = local_ref[...]
    for side in range(2):
        face = face_of(pot_ref, side)
        face[...] = face[...] + partners[side][0]
    for c in range(block):
        rows = pl.ds(c * nodes, nodes)
        pot_ref[rows, :] = local_sweep(pot_ref[rows, :], source_ref[rows, :], inverse_ref[rows, :], spack)
    for side in range(2):
        face = face_of(pot_ref, side)
        face[...] = face[...] + partners[side][1]
    for c in range(block):
        rows = pl.ds(c * nodes, nodes)
        next_ref[rows, :] = local_sweep(pot_ref[rows, :], source_ref[rows, :], inverse_ref[rows, :], spack)
    for side, out in ((0, up_ref), (1, lo_ref)):
        fields = [face_of(ref, side)[...] for ref in (pot_ref, next_ref)[:keep]]
        picked = gather_faces(side, fields, gather_ref, mask_ref)
        for k in range(keep):
            out[k] = picked[k * block : (k + 1) * block]


def two_sweeps(keep, local, source, inverse, own, got, inv, spack, gather, scatter, mask):
    nodes = spack.shape[0]
    elements = local.shape[1]
    coefs = local.shape[0] // nodes
    shared = gather.shape[2]
    block = coef_block(coefs)
    flat = pl.BlockSpec((block * nodes, elements), lambda i: (i, 0))
    one = pl.BlockSpec((1, block, shared), lambda i: (0, i, 0))
    two = pl.BlockSpec((2, block, shared), lambda i: (0, i, 0))
    third = pl.BlockSpec((1, block, shared), lambda i: (2, i, 0))
    face = pl.BlockSpec((keep, block, shared), lambda i: (0, i, 0))
    size = coefs * nodes * elements
    return pl.pallas_call(
        functools.partial(sweeps_kernel, block, keep),
        out_shape=[jax.ShapeDtypeStruct(local.shape, F32)]
        + [jax.ShapeDtypeStruct((keep, coefs, shared), F32)] * 2,
        grid=(coefs // block,),
        in_specs=[
            flat, flat, flat, one, one, two, two, third, third,
            whole(spack.shape), whole(gather.shape), whole(scatter.shape), whole(mask.shape),
        ],
        out_specs=[flat, face, face],
        scratch_shapes=[pltpu.VMEM((block * nodes, elements), F32)],
        compiler_params=params(),
        cost_estimate=cost(12 * nodes * size, 16 * size),
        name="two_sweeps",
    )(local, source, inverse, *own, *got, *inv, spack, gather, scatter, mask)


def store_own(ref, me, value, *lead):
    for d in range(value.shape[0] // LINE):
        ref[(*lead, line_of(me, d), slice(None))] = value[d * LINE : (d + 1) * LINE]


def partial_kernel(block, count, pos_ref, coef_ref, dpack_ref, *refs):
    z_refs, x_refs, o_ref = refs[:count], refs[count : 2 * count], refs[2 * count]
    nodes = coef_ref.shape[1]
    dpack = dpack_ref[...]
    me = pos_ref[1]
    for c in range(block):
        z = slab(z_refs, c)
        slopes = dot(dpack, pack_field(z))
        moved = coef_ref[BXR] * slopes[:nodes] + coef_ref[BYS] * slopes[nodes:]
        store_own(o_ref, me, z - TIME_STEP * (moved + INTERACTION * z), 2, c)
        x = slab(x_refs, c)
        slopes = dot(dpack, pack_field(x))
        moved = coef_ref[BXR] * slopes[:nodes] + coef_ref[BYS] * slopes[nodes:]
        store_own(o_ref, me, x + TIME_STEP * (x * coef_ref[DXBX] - moved - INTERACTION * x), 0, c)
        store_own(o_ref, me, TIME_STEP * (x * coef_ref[DYBX]), 1, c)


def partial_update(position, z, x, coef, dpack):
    coefs, part, elements = z[0].shape
    nodes = len(z) * part
    block = coef_block(coefs)
    field = [pl.BlockSpec((block, part, elements), lambda i: (i, 0, 0))] * len(z)
    size = coefs * nodes * elements
    return pl.pallas_call(
        functools.partial(partial_kernel, block, len(z)),
        out_shape=jax.ShapeDtypeStruct((3, coefs, nodes, elements), F32),
        grid=(coefs // block,),
        in_specs=[SMEM_SPEC, whole(coef.shape), whole(dpack.shape), *field, *field],
        out_specs=pl.BlockSpec((3, block, nodes, elements), lambda i: (0, i, 0, 0)),
        compiler_params=params(),
        cost_estimate=cost(24 * nodes * size, 45 * size),
        name="partial_update",
    )(position, coef, dpack, *z, *x)


def force_kernel(
    block, pos_ref, local_ref, inverse_ref, got_up_ref, got_lo_ref, geo_ref, dpack_ref, scatter_ref,
    mask_ref, part_ref, o_ref, pot_ref,
):
    nodes = dpack_ref.shape[0] // 2
    scale = TIME_STEP * INTERACTION
    which = pl.program_id(1)
    me = pos_ref[1]

    @pl.when(which == 0)
    def _():
        pot_ref[...] = local_ref[...]
        for side, got in ((0, got_up_ref), (1, got_lo_ref)):
            face = face_of(pot_ref, side)
            partner = scatter_faces(side, got[0], scatter_ref, mask_ref)
            face[...] = face[...] + PENALTY * face_of(inverse_ref, side)[...] * partner
        first = pos_ref[0] * (block * pl.num_programs(0)) + pl.program_id(0) * block
        for c in range(block):
            wave = (4.0 / PLANES) * ((first + c) // 2).astype(F32)
            factor = scale * (wave if c % 2 == 0 else -wave)
            other = c + 1 if c % 2 == 0 else c - 1
            turned = factor * pot_ref[pl.ds(other * nodes, nodes), :]
            store_own(o_ref, me, own_order(part_ref, me, 0, c) + turned, 0, c)

    @pl.when(which == 1)
    def _():
        drpack = dpack_ref[:nodes]
        factor = scale * geo_ref[0:1, :]
        for c in range(block):
            slope = dot(drpack, pack_field(pot_ref[pl.ds(c * nodes, nodes), :]))
            store_own(o_ref, me, own_order(part_ref, me, 0, c) - factor * slope, 0, c)


def add_force(position, local, inverse, got, geometry, dpack, scatter, mask, partial):
    _, coefs, nodes, elements = partial.shape
    shared = scatter.shape[1]
    block = coef_block(coefs)
    flat = pl.BlockSpec((block * nodes, elements), lambda i, j: (i, 0))
    one = pl.BlockSpec((1, block, shared), lambda i, j: (0, i, 0))
    comp = pl.BlockSpec((1, block, nodes, elements), lambda i, j: (2 * j, i, 0, 0))
    size = coefs * nodes * elements
    return pl.pallas_call(
        functools.partial(force_kernel, block),
        out_shape=jax.ShapeDtypeStruct(partial.shape, F32),
        grid=(coefs // block, 2),
        in_specs=[
            SMEM_SPEC, flat, flat, one, one, whole(geometry.shape), whole(dpack.shape),
            whole(scatter.shape), whole(mask.shape), comp,
        ],
        out_specs=comp,
        scratch_shapes=[pltpu.VMEM((block * nodes, elements), F32)],
        input_output_aliases={9: 0},
        compiler_params=params(),
        cost_estimate=cost(6 * nodes * size, 24 * size),
        name="add_force",
    )(position, local, inverse, *got, geometry, dpack, scatter, mask, partial)


def finish_kernel(block, count, pos_ref, coef_ref, dpack_ref, part_ref, *refs):
    y_refs, o_ref = refs[:count], refs[count]
    nodes = coef_ref.shape[1]
    which = pl.program_id(1)
    me = pos_ref[1]

    @pl.when(which == 0)
    def _():
        for c in range(block):
            y = slab(y_refs, c)
            store_own(o_ref, me, own_order(part_ref, me, 0, c) + TIME_STEP * (y * coef_ref[DXBY]), 0, c)

    @pl.when(which == 1)
    def _():
        dpack = dpack_ref[...]
        for c in range(block):
            y = slab(y_refs, c)
            slopes = dot(dpack, pack_field(y))
            moved = coef_ref[BXR] * slopes[:nodes] + coef_ref[BYS] * slopes[nodes:]
            change = y + TIME_STEP * (y * coef_ref[DYBY] - moved)
            store_own(o_ref, me, own_order(part_ref, me, 0, c) + change, 0, c)


def finish(position, y, coef, dpack, partial):
    coefs, part, elements = y[0].shape
    nodes = len(y) * part
    block = coef_block(coefs)
    comp = pl.BlockSpec((1, block, nodes, elements), lambda i, j: (j, i, 0, 0))
    size = coefs * nodes * elements
    return pl.pallas_call(
        functools.partial(finish_kernel, block, len(y)),
        out_shape=jax.ShapeDtypeStruct(partial.shape, F32),
        grid=(coefs // block, 2),
        in_specs=[SMEM_SPEC, whole(coef.shape), whole(dpack.shape), comp]
        + [pl.BlockSpec((block, part, elements), lambda i, j: (i, 0, 0))] * len(y),
        out_specs=comp,
        input_output_aliases={3: 0},
        compiler_params=params(),
        cost_estimate=cost(12 * nodes * size, 50 * size),
        name="finish",
    )(position, coef, dpack, partial, *y)


def to_all(blocks):
    return lax.all_to_all(blocks, "four", split_axis=0, concat_axis=0, tiled=True)


def swap_faces(up, lo):
    peers = lax.axis_size("dom")
    up_way = [(i, (i + 1) % peers) for i in range(peers)]
    down_way = [(j, i) for i, j in up_way]
    return lax.ppermute(lo, "dom", down_way), lax.ppermute(up, "dom", up_way)


def per_device(
    adjoint, base_bank, snapshot, geometry, diff_r, diff_s, stiffness, upper_list, lower_list
):
    _, per, nodes, elements = adjoint.shape
    peers = lax.axis_size("four")
    lines = nodes // LINE
    direct = peers == lines
    place = lax.axis_index("four").astype(jnp.int32)
    position = jnp.stack([place, place if direct else jnp.zeros_like(place)])
    table = permuted_table(position, jnp.asarray(coef_table(PLANES)), lines)

    def exchange(blocks):
        return [blocks[0]] + [
            lax.ppermute(blocks[d], "four", [(i, i ^ d) for i in range(peers)]) for d in range(1, peers)
        ]

    def columns(comp):
        if direct:
            return pack(position, adjoint, comp, peers)
        return [jnp.moveaxis(adjoint[comp].reshape(per, peers, nodes // peers, elements), 1, 0)]

    def spread(blocks):
        if direct:
            return exchange(blocks)
        return [to_all(blocks[0]).reshape(per * peers, nodes // peers, elements)]

    def collect(blocks):
        if direct:
            return exchange(blocks)
        got = to_all(blocks[0].reshape(peers, per, nodes // peers, elements))
        got = jnp.moveaxis(got, 0, 1).reshape(per, lines, LINE, elements)
        return [got[:, d] for d in range(lines)]

    z_blocks = columns(2)
    x_blocks = columns(0)
    y_blocks = columns(1)
    z_blocks, x_blocks = lax.optimization_barrier((z_blocks, x_blocks))
    z_columns = spread(z_blocks)
    x_columns = spread(x_blocks)
    coef, dpack, spack, gather, scatter, mask = prepare(
        position, base_bank, snapshot, geometry, diff_r, diff_s, stiffness, upper_list, lower_list
    )
    z_coefs = transform(z_columns, table)
    z = collect(z_coefs)
    x_coefs = transform(x_columns, table)
    x_coefs, y_blocks = lax.optimization_barrier((x_coefs, y_blocks))
    x = collect(x_coefs)
    y_columns = spread(y_blocks)
    source, inverse, local, up, lo = start_solve(
        position, z, x, geometry, coef, dpack, spack, gather, mask
    )
    got = swap_faces(up, lo)
    inv = got
    partial = partial_update(position, z, x, coef, dpack)
    local, up, lo = two_sweeps(
        2, local, source, inverse, (up, lo), got, inv, spack, gather, scatter, mask
    )
    got = swap_faces(up, lo)
    y = collect(transform(y_columns, table))
    local, up, lo = two_sweeps(
        1, local, source, inverse, (up, lo), got, inv, spack, gather, scatter, mask
    )
    got = swap_faces(up, lo)
    partial = add_force(position, local, inverse, got, geometry, dpack, scatter, mask, partial)
    return finish(position, y, coef, dpack, partial)


def solution(mesh):
    in_specs = (
        P(None, "four", None, "dom"),
        P(None, None, None, "dom"),
        P("dom"),
        P(None, "dom"),
        P(),
        P(),
        P(),
        P("dom", None),
        P("dom", None),
    )
    out_specs = P(None, "four", None, "dom")
    return jax.shard_map(
        per_device, mesh=mesh, in_specs=in_specs, out_specs=out_specs, check_vma=False
    )
```

```python
import functools
import math

import jax
import jax.numpy as jnp
import ml_dtypes
import numpy as np
from jax import lax
from jax.experimental import pallas as pl
from jax.experimental.pallas import tpu as pltpu
from jax.sharding import PartitionSpec as P

PLANES = 256
PENALTY = 0.5
RELAXATION = 0.8
TIME_STEP = 0.2
INTERACTION = 2.0
LINE = 8
IN_FLIGHT = 5

F32 = jnp.float32
BF16 = jnp.bfloat16
VMEM_LIMIT = 48 * 1024 * 1024
SMEM_SPEC = pl.BlockSpec(memory_space=pltpu.SMEM)


def params():
    return pltpu.CompilerParams(vmem_limit_bytes=VMEM_LIMIT)


def cost(flops, moved):
    return pl.CostEstimate(flops=int(flops), bytes_accessed=int(moved), transcendentals=0)


def split(x):
    high = x.astype(BF16)
    low = (x - high.astype(F32)).astype(BF16)
    return high, low


def dot(a, b):
    return lax.dot_general(a, b, (((1,), (0,)), ((), ())), preferred_element_type=F32)


def pack_matrix(m):
    high, low = split(m)
    return jnp.concatenate([high, low, high], axis=1)


def slab(refs, c):
    return jnp.concatenate([ref[c] for ref in refs], axis=0)


def pack_field(v):
    high, low = split(v)
    return jnp.concatenate([high, high, low], axis=0)


def coef_table(length):
    c = np.arange(length)[:, None]
    j = np.arange(length)[None, :]
    angle = ((c // 2) * j % length) * (2.0 * math.pi / length)
    table = np.where(c % 2 == 1, np.sin(angle), np.cos(angle)) * math.sqrt(2.0 / length)
    table[0] = 1.0 / math.sqrt(length)
    table[1] = np.where(np.arange(length) % 2 == 0, 1.0, -1.0) / math.sqrt(length)
    high = table.astype(ml_dtypes.bfloat16)
    low = (table - high.astype(np.float64)).astype(ml_dtypes.bfloat16)
    return np.concatenate([high, low], axis=0)


def permute_kernel(peers, pos_ref, table_ref, o_ref):
    planes = table_ref.shape[1]
    per = planes // peers
    me = pos_ref[1]
    row = lax.broadcasted_iota(jnp.int32, (planes, planes), 0)
    col = lax.broadcasted_iota(jnp.int32, (planes, planes), 1)
    swap = jnp.where(row == ((col // per) ^ me) * per + col % per, 1.0, 0.0).astype(BF16)
    for half in range(2):
        rows = pl.ds(half * planes, planes)
        turned = dot(swap, table_ref[rows, :]).astype(BF16)
        o_ref[rows, :] = dot(turned, swap).astype(BF16)


def permuted_table(position, table, peers):
    return pl.pallas_call(
        functools.partial(permute_kernel, peers),
        out_shape=jax.ShapeDtypeStruct(table.shape, BF16),
        in_specs=[SMEM_SPEC, pl.BlockSpec(memory_space=pltpu.VMEM)],
        compiler_params=params(),
        cost_estimate=cost(1e8, 4e6),
        name="permuted_table",
    )(position, table)


def transform_kernel(count, table_ref, *refs):
    planes = table_ref.shape[1]
    both = table_ref[...]
    high_table = both[:planes]
    width = refs[0].shape[-1]
    nodes = refs[0].shape[-2]
    per = planes // count
    flat = [ref.reshape(per * nodes, width) for ref in refs]
    for n in range(nodes):
        rows = pl.ds(n, per, stride=nodes) if nodes > 1 else pl.ds(0, per)
        high, low = split(jnp.concatenate([ref[rows, :] for ref in flat[:count]], axis=0))
        wide = dot(both, high)
        result = wide[:planes] + (wide[planes:] + dot(high_table, low))
        for d, ref in enumerate(flat[count:]):
            ref[rows, :] = result[d * per : (d + 1) * per]


def transform(blocks, table):
    *lead, nodes, elements = blocks[0].shape
    zeros = (0,) * (len(lead) + 1)
    width = 128
    block = pl.BlockSpec((*lead, nodes, width), lambda i: (*zeros, i))
    size = len(blocks) * blocks[0].size
    return pl.pallas_call(
        functools.partial(transform_kernel, len(blocks)),
        out_shape=[jax.ShapeDtypeStruct(v.shape, F32) for v in blocks],
        grid=(elements // width,),
        in_specs=[pl.BlockSpec(table.shape, lambda i: (0, 0))] + [block] * len(blocks),
        out_specs=[block] * len(blocks),
        compiler_params=params(),
        cost_estimate=cost(6 * PLANES * size, 8 * size),
        name="transform",
    )(table, *blocks)


def pack_kernel(pos_ref, *refs):
    count = len(refs) // 2
    for source, target in zip(refs[:count], refs[count:]):
        target[...] = source[0]


def pack(position, adjoint, comp, peers):
    _, per, nodes, elements = adjoint.shape
    part = nodes // peers
    block = per // 2

    def source(d):
        return pl.BlockSpec((1, block, part, elements), lambda i, pos: (comp, i, pos[1] ^ d, 0))

    size = per * nodes * elements
    return pl.pallas_call(
        pack_kernel,
        out_shape=[jax.ShapeDtypeStruct((per, part, elements), F32)] * peers,
        grid_spec=pltpu.PrefetchScalarGridSpec(
            num_scalar_prefetch=1,
            grid=(per // block,),
            in_specs=[source(d) for d in range(peers)],
            out_specs=[pl.BlockSpec((block, part, elements), lambda i, pos: (i, 0, 0))] * peers,
        ),
        compiler_params=params(),
        cost_estimate=cost(0, 16 * size),
        name="pack",
    )(position, *[adjoint] * peers)


def pack_joined_kernel(x_ref, o_ref):
    part = o_ref.shape[2]
    for d in range(o_ref.shape[0]):
        o_ref[d] = x_ref[0, :, d * part : (d + 1) * part, :]


def pack_joined(adjoint, comp, peers):
    _, per, nodes, elements = adjoint.shape
    part = nodes // peers
    if part % 8:
        return jnp.moveaxis(adjoint[comp].reshape(per, peers, part, elements), 1, 0)
    block = per // 4
    size = per * nodes * elements
    return pl.pallas_call(
        pack_joined_kernel,
        out_shape=jax.ShapeDtypeStruct((peers, per, part, elements), F32),
        grid=(per // block,),
        in_specs=[pl.BlockSpec((1, block, nodes, elements), lambda q: (comp, q, 0, 0))],
        out_specs=pl.BlockSpec((peers, block, part, elements), lambda q: (0, q, 0, 0)),
        compiler_params=params(),
        cost_estimate=cost(0, 8 * size),
        name="pack_joined",
    )(adjoint)


BXR, BYS, DXBX, DXBY, DYBX, DYBY, DIAG = range(7)


def line_of(me, d):
    return pl.ds(pl.multiple_of((me ^ d) * LINE, LINE), LINE)


def own_order(ref, me, *lead):
    lines = ref.shape[-2] // LINE
    return jnp.concatenate([ref[(*lead, line_of(me, d), slice(None))] for d in range(lines)], axis=0)


def prep_kernel(
    pos_ref, bank_ref, snap_ref, geo_ref, dr_ref, ds_ref, st_ref, up_ref, lo_ref,
    coef_ref, dpack_ref, spack_ref, gather_ref, scatter_ref, mask_ref,
):
    elements = geo_ref.shape[1]
    nodes = dr_ref.shape[0]
    lines = nodes // LINE
    me = pos_ref[1]
    row = lax.broadcasted_iota(jnp.int32, (nodes, nodes), 0)
    col = lax.broadcasted_iota(jnp.int32, (nodes, nodes), 1)
    swap = jnp.where(row == ((col // LINE) ^ me) * LINE + col % LINE, 1.0, 0.0).astype(BF16)

    def permuted(ref):
        high, low = split(own_order(ref, me))
        return dot(high, swap) + dot(low, swap)

    snap = snap_ref[...]
    base = [
        sum(
            jnp.where(snap == k, own_order(bank_ref, me, k, i), 0.0)
            for k in range(bank_ref.shape[0])
        )
        for i in range(2)
    ]
    rx = geo_ref[0:1, :]
    sy = geo_ref[1:2, :]
    dpack = pack_matrix(jnp.concatenate([permuted(dr_ref), permuted(ds_ref)], axis=0))
    dpack_ref[...] = dpack
    bx = dot(dpack, pack_field(base[0]))
    by = dot(dpack, pack_field(base[1]))
    coef_ref[BXR] = base[0] * rx
    coef_ref[BYS] = base[1] * sy
    coef_ref[DXBX] = rx * bx[:nodes]
    coef_ref[DXBY] = rx * by[:nodes]
    coef_ref[DYBX] = sy * bx[nodes:]
    coef_ref[DYBY] = sy * by[nodes:]
    diag = jnp.sum(jnp.where(row == col, st_ref[...], 0.0), axis=0, keepdims=True)
    own = ((row // LINE) ^ me) * LINE + row % LINE == col
    diag = jnp.sum(jnp.where(own, diag, 0.0), axis=1, keepdims=True)
    spack_ref[...] = pack_matrix(jnp.where(row == col, 0.0, permuted(st_ref)))
    coef_ref[DIAG] = jnp.broadcast_to(diag, (nodes, elements))
    shared = up_ref.shape[1]
    for side, (ref, first) in enumerate(((up_ref, LINE - 1), (lo_ref, 0))):
        index = ref[...]
        node = index // elements
        element = index - node * elements
        hot = lax.broadcasted_iota(jnp.int32, (elements, shared), 0) == element
        hot = jnp.where(hot, 1.0, 0.0)
        gather_ref[side] = hot.astype(BF16)
        back = hot.T.astype(BF16)
        scatter_ref[side] = back
        mask = (lax.broadcasted_iota(jnp.int32, (lines, shared), 0) ^ me) == node // LINE
        mask = jnp.where(mask, 1.0, 0.0)
        mask_ref[side] = mask
        count = dot(mask.astype(BF16), back)
        for s in range(lines):
            n = s * LINE + first
            coef_ref[DIAG, n : n + 1, :] = coef_ref[DIAG, n : n + 1, :] + PENALTY * count[s : s + 1]


def prepare(position, base_bank, snapshot, geometry, diff_r, diff_s, stiffness, upper, lower):
    nodes = diff_r.shape[0]
    elements = geometry.shape[1]
    shared = upper.shape[1]
    return pl.pallas_call(
        prep_kernel,
        out_shape=[
            jax.ShapeDtypeStruct((7, nodes, elements), F32),
            jax.ShapeDtypeStruct((2 * nodes, 3 * nodes), BF16),
            jax.ShapeDtypeStruct((nodes, 3 * nodes), BF16),
            jax.ShapeDtypeStruct((2, elements, shared), BF16),
            jax.ShapeDtypeStruct((2, shared, elements), BF16),
            jax.ShapeDtypeStruct((2, nodes // LINE, shared), F32),
        ],
        in_specs=[SMEM_SPEC] + [pl.BlockSpec(memory_space=pltpu.VMEM)] * 8,
        compiler_params=params(),
        cost_estimate=cost(1e7, 8e6),
        name="prepare",
    )(position, base_bank, snapshot.reshape(1, elements), geometry, diff_r, diff_s, stiffness, upper, lower)


def face_of(ref, side):
    rows, elements = ref.shape
    return ref.reshape(rows // LINE, LINE, elements).at[:, LINE - 1 if side == 0 else 0, :]


def gather_faces(side, fields, gather_ref, mask_ref):
    lines = mask_ref.shape[1]
    high, low = split(jnp.concatenate(fields, axis=0))
    rows = high.shape[0]
    both = dot(jnp.concatenate([high, low], axis=0), gather_ref[side])
    picked = both[:rows] + both[rows:]
    shared = picked.shape[1]
    return jnp.sum(picked.reshape(rows // lines, lines, shared) * mask_ref[side][None], axis=1)


def scatter_faces(side, values, scatter_ref, mask_ref):
    mask = mask_ref[side]
    coefs, shared = values.shape
    spread = (values[:, None, :] * mask[None]).reshape(coefs * mask.shape[0], shared)
    high, low = split(spread)
    rows = high.shape[0]
    both = dot(jnp.concatenate([high, low], axis=0), scatter_ref[side])
    return both[:rows] + both[rows:]


def local_sweep(pot, source, inverse, spack):
    applied = dot(spack, pack_field(pot))
    return (1.0 - RELAXATION) * pot + inverse * (source - applied)


def coef_block(coefs):
    return 8 if coefs % 8 == 0 else coefs


def start_kernel(
    block, count, pos_ref, geo_ref, diag_ref, dpack_ref, spack_ref, gather_ref, mask_ref, *refs
):
    z_refs, x_refs = refs[:count], refs[count : 2 * count]
    source_ref, inverse_ref, local_ref, up_ref, lo_ref, pot_ref = refs[2 * count :]
    nodes, elements = diag_ref.shape[1:]
    beta = 4.0 / PLANES
    first = pos_ref[0] * (block * pl.num_programs(0)) + pl.program_id(0) * block
    rx = geo_ref[0:1, :]
    mass = 1.0 / (rx * geo_ref[1:2, :])
    diag = diag_ref[0]
    drpack = dpack_ref[:nodes]
    spack = spack_ref[...]
    for c in range(block):
        index = first + c
        wave = beta * (index // 2).astype(F32)
        shift = beta * jnp.where(index == 1, PLANES // 2, index // 2).astype(F32)
        shift = shift * shift
        z = slab(z_refs, c)
        other = slab(x_refs, c + 1 if c % 2 == 0 else c - 1)
        turned = (wave if c % 2 == 0 else -wave) * other
        source = turned - rx * dot(drpack, pack_field(z))
        inverse = RELAXATION / (diag + shift * mass)
        pot = inverse * source
        rows = pl.ds(c * nodes, nodes)
        source_ref[rows, :] = source
        inverse_ref[rows, :] = inverse
        pot_ref[rows, :] = pot
        local_ref[rows, :] = local_sweep(pot, source, inverse, spack)
    for side, out in ((0, up_ref), (1, lo_ref)):
        fields = [face_of(ref, side)[...] for ref in (pot_ref, local_ref, inverse_ref)]
        picked = gather_faces(side, fields, gather_ref, mask_ref)
        for k in range(3):
            out[k] = picked[k * block : (k + 1) * block]


def whole(shape):
    return pl.BlockSpec(shape, lambda *i: (0,) * len(shape))


def start_solve(position, z, x, geometry, coef, dpack, spack, gather, mask):
    coefs, part, elements = z[0].shape
    nodes = len(z) * part
    shared = gather.shape[2]
    block = coef_block(coefs)
    field = [pl.BlockSpec((block, part, elements), lambda i: (i, 0, 0))] * len(z)
    flat = pl.BlockSpec((block * nodes, elements), lambda i: (i, 0))
    face = pl.BlockSpec((3, block, shared), lambda i: (0, i, 0))
    size = coefs * nodes * elements
    return pl.pallas_call(
        functools.partial(start_kernel, block, len(z)),
        out_shape=[jax.ShapeDtypeStruct((coefs * nodes, elements), F32)] * 3
        + [jax.ShapeDtypeStruct((3, coefs, shared), F32)] * 2,
        grid=(coefs // block,),
        in_specs=[
            SMEM_SPEC, whole(geometry.shape),
            pl.BlockSpec((1, nodes, elements), lambda i: (DIAG, 0, 0)),
            whole(dpack.shape), whole(spack.shape), whole(gather.shape), whole(mask.shape),
            *field, *field,
        ],
        out_specs=[flat, flat, flat, face, face],
        scratch_shapes=[pltpu.VMEM((block * nodes, elements), F32)],
        compiler_params=params(),
        cost_estimate=cost(12 * nodes * size, 20 * size),
        name="start_solve",
    )(position, geometry, coef, dpack, spack, gather, mask, *z, *x)


def sweeps_kernel(
    block, keep, local_ref, source_ref, inverse_ref, own_up_ref, own_lo_ref,
    got_up_ref, got_lo_ref, inv_up_ref, inv_lo_ref, spack_ref, gather_ref, scatter_ref, mask_ref,
    next_ref, up_ref, lo_ref, pot_ref,
):
    nodes = spack_ref.shape[0]
    spack = spack_ref[...]
    lines = block * (nodes // LINE)
    partners = []
    for side, own, got, inv in (
        (0, own_up_ref, got_up_ref, inv_up_ref),
        (1, own_lo_ref, got_lo_ref, inv_lo_ref),
    ):
        now = got[0]
        later = got[1] + PENALTY * inv[0] * own[0]
        both = scatter_faces(side, jnp.concatenate([now, later], axis=0), scatter_ref, mask_ref)
        scale = PENALTY * face_of(inverse_ref, side)[...]
        partners.append((scale * both[:lines], scale * both[lines:]))
    pot_ref[...] = local_ref[...]
    for side in range(2):
        face = face_of(pot_ref, side)
        face[...] = face[...] + partners[side][0]
    for c in range(block):
        rows = pl.ds(c * nodes, nodes)
        pot_ref[rows, :] = local_sweep(pot_ref[rows, :], source_ref[rows, :], inverse_ref[rows, :], spack)
    for side in range(2):
        face = face_of(pot_ref, side)
        face[...] = face[...] + partners[side][1]
    for c in range(block):
        rows = pl.ds(c * nodes, nodes)
        next_ref[rows, :] = local_sweep(pot_ref[rows, :], source_ref[rows, :], inverse_ref[rows, :], spack)
    for side, out in ((0, up_ref), (1, lo_ref)):
        fields = [face_of(ref, side)[...] for ref in (pot_ref, next_ref)[:keep]]
        picked = gather_faces(side, fields, gather_ref, mask_ref)
        for k in range(keep):
            out[k] = picked[k * block : (k + 1) * block]


def two_sweeps(keep, local, source, inverse, own, got, inv, spack, gather, scatter, mask):
    nodes = spack.shape[0]
    elements = local.shape[1]
    coefs = local.shape[0] // nodes
    shared = gather.shape[2]
    block = coef_block(coefs)
    flat = pl.BlockSpec((block * nodes, elements), lambda i: (i, 0))
    one = pl.BlockSpec((1, block, shared), lambda i: (0, i, 0))
    two = pl.BlockSpec((2, block, shared), lambda i: (0, i, 0))
    third = pl.BlockSpec((1, block, shared), lambda i: (2, i, 0))
    face = pl.BlockSpec((keep, block, shared), lambda i: (0, i, 0))
    size = coefs * nodes * elements
    return pl.pallas_call(
        functools.partial(sweeps_kernel, block, keep),
        out_shape=[jax.ShapeDtypeStruct(local.shape, F32)]
        + [jax.ShapeDtypeStruct((keep, coefs, shared), F32)] * 2,
        grid=(coefs // block,),
        in_specs=[
            flat, flat, flat, one, one, two, two, third, third,
            whole(spack.shape), whole(gather.shape), whole(scatter.shape), whole(mask.shape),
        ],
        out_specs=[flat, face, face],
        scratch_shapes=[pltpu.VMEM((block * nodes, elements), F32)],
        compiler_params=params(),
        cost_estimate=cost(12 * nodes * size, 16 * size),
        name="two_sweeps",
    )(local, source, inverse, *own, *got, *inv, spack, gather, scatter, mask)


def store_own(ref, me, value, *lead):
    for d in range(value.shape[0] // LINE):
        ref[(*lead, line_of(me, d), slice(None))] = value[d * LINE : (d + 1) * LINE]


def partial_kernel(block, count, pos_ref, coef_ref, dpack_ref, *refs):
    z_refs, x_refs, o_ref = refs[:count], refs[count : 2 * count], refs[2 * count]
    nodes = coef_ref.shape[1]
    dpack = dpack_ref[...]
    me = pos_ref[1]
    for c in range(block):
        z = slab(z_refs, c)
        slopes = dot(dpack, pack_field(z))
        moved = coef_ref[BXR] * slopes[:nodes] + coef_ref[BYS] * slopes[nodes:]
        store_own(o_ref, me, z - TIME_STEP * (moved + INTERACTION * z), 2, c)
        x = slab(x_refs, c)
        slopes = dot(dpack, pack_field(x))
        moved = coef_ref[BXR] * slopes[:nodes] + coef_ref[BYS] * slopes[nodes:]
        store_own(o_ref, me, x + TIME_STEP * (x * coef_ref[DXBX] - moved - INTERACTION * x), 0, c)
        store_own(o_ref, me, TIME_STEP * (x * coef_ref[DYBX]), 1, c)


def partial_update(position, z, x, coef, dpack):
    coefs, part, elements = z[0].shape
    nodes = len(z) * part
    block = coef_block(coefs)
    field = [pl.BlockSpec((block, part, elements), lambda i: (i, 0, 0))] * len(z)
    size = coefs * nodes * elements
    return pl.pallas_call(
        functools.partial(partial_kernel, block, len(z)),
        out_shape=jax.ShapeDtypeStruct((3, coefs, nodes, elements), F32),
        grid=(coefs // block,),
        in_specs=[SMEM_SPEC, whole(coef.shape), whole(dpack.shape), *field, *field],
        out_specs=pl.BlockSpec((3, block, nodes, elements), lambda i: (0, i, 0, 0)),
        compiler_params=params(),
        cost_estimate=cost(24 * nodes * size, 20 * size),
        name="partial_update",
    )(position, coef, dpack, *z, *x)


def force_kernel(
    block, pos_ref, local_ref, inverse_ref, got_up_ref, got_lo_ref, geo_ref, dpack_ref, scatter_ref,
    mask_ref, part_ref, o_ref, pot_ref,
):
    nodes = dpack_ref.shape[0] // 2
    scale = TIME_STEP * INTERACTION
    which = pl.program_id(1)
    me = pos_ref[1]

    @pl.when(which == 0)
    def _():
        pot_ref[...] = local_ref[...]
        for side, got in ((0, got_up_ref), (1, got_lo_ref)):
            face = face_of(pot_ref, side)
            partner = scatter_faces(side, got[0], scatter_ref, mask_ref)
            face[...] = face[...] + PENALTY * face_of(inverse_ref, side)[...] * partner
        first = pos_ref[0] * (block * pl.num_programs(0)) + pl.program_id(0) * block
        for c in range(block):
            wave = (4.0 / PLANES) * ((first + c) // 2).astype(F32)
            factor = scale * (wave if c % 2 == 0 else -wave)
            other = c + 1 if c % 2 == 0 else c - 1
            turned = factor * pot_ref[pl.ds(other * nodes, nodes), :]
            store_own(o_ref, me, own_order(part_ref, me, 0, c) + turned, 0, c)

    @pl.when(which == 1)
    def _():
        drpack = dpack_ref[:nodes]
        factor = scale * geo_ref[0:1, :]
        for c in range(block):
            slope = dot(drpack, pack_field(pot_ref[pl.ds(c * nodes, nodes), :]))
            store_own(o_ref, me, own_order(part_ref, me, 0, c) - factor * slope, 0, c)


def add_force(position, local, inverse, got, geometry, dpack, scatter, mask, partial):
    _, coefs, nodes, elements = partial.shape
    shared = scatter.shape[1]
    block = coef_block(coefs)
    flat = pl.BlockSpec((block * nodes, elements), lambda i, j: (i, 0))
    one = pl.BlockSpec((1, block, shared), lambda i, j: (0, i, 0))
    comp = pl.BlockSpec((1, block, nodes, elements), lambda i, j: (2 * j, i, 0, 0))
    size = coefs * nodes * elements
    return pl.pallas_call(
        functools.partial(force_kernel, block),
        out_shape=jax.ShapeDtypeStruct(partial.shape, F32),
        grid=(coefs // block, 2),
        in_specs=[
            SMEM_SPEC, flat, flat, one, one, whole(geometry.shape), whole(dpack.shape),
            whole(scatter.shape), whole(mask.shape), comp,
        ],
        out_specs=comp,
        scratch_shapes=[pltpu.VMEM((block * nodes, elements), F32)],
        input_output_aliases={9: 0},
        compiler_params=params(),
        cost_estimate=cost(6 * nodes * size, 24 * size),
        name="add_force",
    )(position, local, inverse, *got, geometry, dpack, scatter, mask, partial)


def finish_kernel(block, count, pos_ref, coef_ref, dpack_ref, part_ref, *refs):
    y_refs, o_ref = refs[:count], refs[count]
    nodes = coef_ref.shape[1]
    which = pl.program_id(1)
    me = pos_ref[1]

    @pl.when(which == 0)
    def _():
        for c in range(block):
            y = slab([ref.at[0] for ref in y_refs], c)
            store_own(o_ref, me, own_order(part_ref, me, 0, c) + TIME_STEP * (y * coef_ref[DXBY]), 0, c)

    @pl.when(which == 1)
    def _():
        dpack = dpack_ref[...]
        for c in range(block):
            y = slab([ref.at[0] for ref in y_refs], c)
            slopes = dot(dpack, pack_field(y))
            moved = coef_ref[BXR] * slopes[:nodes] + coef_ref[BYS] * slopes[nodes:]
            change = y + TIME_STEP * (y * coef_ref[DYBY] - moved)
            store_own(o_ref, me, own_order(part_ref, me, 0, c) + change, 0, c)


def finish(position, y, coef, dpack, partial):
    lines, coefs, part, elements = y.shape
    nodes = lines * part
    block = coef_block(coefs)

    def source(d):
        return pl.BlockSpec((1, block, part, elements), lambda i, j, pos: (pos[1] ^ d, i, 0, 0))

    comp = pl.BlockSpec((1, block, nodes, elements), lambda i, j, pos: (j, i, 0, 0))
    size = coefs * nodes * elements
    return pl.pallas_call(
        functools.partial(finish_kernel, block, lines),
        out_shape=jax.ShapeDtypeStruct(partial.shape, F32),
        grid_spec=pltpu.PrefetchScalarGridSpec(
            num_scalar_prefetch=1,
            grid=(coefs // block, 2),
            in_specs=[whole(coef.shape), whole(dpack.shape), comp] + [source(d) for d in range(lines)],
            out_specs=comp,
        ),
        input_output_aliases={3: 0},
        compiler_params=params(),
        cost_estimate=cost(12 * nodes * size, 20 * size),
        name="finish",
    )(position, coef, dpack, partial, *[y] * lines)


def to_all(blocks):
    return lax.all_to_all(blocks, "four", split_axis=0, concat_axis=0, tiled=True)


def swap_faces(up, lo):
    peers = lax.axis_size("dom")
    up_way = [(i, (i + 1) % peers) for i in range(peers)]
    down_way = [(j, i) for i, j in up_way]
    return lax.ppermute(lo, "dom", down_way), lax.ppermute(up, "dom", up_way)


def per_device(
    adjoint, base_bank, snapshot, geometry, diff_r, diff_s, stiffness, upper_list, lower_list
):
    _, per, nodes, elements = adjoint.shape
    peers = lax.axis_size("four")
    lines = nodes // LINE
    direct = peers == lines
    place = lax.axis_index("four").astype(jnp.int32)
    position = jnp.stack([place, place if direct else jnp.zeros_like(place)])
    natural = jnp.asarray(coef_table(PLANES))
    table = permuted_table(position, natural, lines)
    flight = []

    def exchange(blocks):
        first = len(flight)
        order = sorted(range(1, peers), key=lambda d: (d < 2, d % 2, d))
        for d in order:
            block = blocks[d]
            if len(flight) >= IN_FLIGHT:
                block, flight[-IN_FLIGHT] = lax.optimization_barrier((block, flight[-IN_FLIGHT]))
            flight.append(lax.ppermute(block, "four", [(i, i ^ d) for i in range(peers)]))

        def received():
            got = {d: flight[first + k] for k, d in enumerate(order)}
            return [blocks[0]] + [got[d] for d in range(1, peers)]

        return received

    def columns(comp):
        if direct:
            return pack(position, adjoint, comp, peers)
        return [pack_joined(adjoint, comp, peers)]

    def spread(blocks):
        if direct:
            return exchange(blocks)
        got = [to_all(blocks[0])]
        return lambda: got

    def collect(blocks):
        if direct:
            return exchange(blocks)
        got = by_line(to_all(blocks[0]))
        return lambda: [got[d] for d in range(lines)]

    def by_line(got):
        if peers == lines:
            return got
        got = jnp.moveaxis(got, 0, 1).reshape(per, lines, LINE, elements)
        return jnp.moveaxis(got, 1, 0)

    z_blocks = columns(2)
    z_columns = spread(z_blocks)
    x_blocks = columns(0)
    x_columns = spread(x_blocks)
    constants = prepare(
        position, base_bank, snapshot, geometry, diff_r, diff_s, stiffness, upper_list, lower_list
    )
    y_sent = pack_joined(adjoint, 1, peers)
    z_got, constants, y_sent, table = lax.optimization_barrier((z_columns(), constants, y_sent, table))
    coef, dpack, spack, gather, scatter, mask = constants
    z_coefs = transform(z_got, table)
    z_later = collect(z_coefs)
    x_coefs = transform(x_columns(), table)
    x_later = collect(x_coefs)
    z = z_later()
    x = x_later()
    x[2], y_sent = lax.optimization_barrier((x[2], y_sent))
    y_columns = to_all(y_sent)
    source, inverse, local, up, lo = start_solve(
        position, z, x, geometry, coef, dpack, spack, gather, mask
    )
    got = swap_faces(up, lo)
    inv = got
    partial = partial_update(position, z, x, coef, dpack)
    local, up, lo = two_sweeps(
        2, local, source, inverse, (up, lo), got, inv, spack, gather, scatter, mask
    )
    y_columns, local = lax.optimization_barrier((y_columns, local))
    got = swap_faces(up, lo)
    y = by_line(to_all(transform([y_columns], natural)[0]))
    local, up, lo = two_sweeps(
        1, local, source, inverse, (up, lo), got, inv, spack, gather, scatter, mask
    )
    got = swap_faces(up, lo)
    partial = add_force(position, local, inverse, got, geometry, dpack, scatter, mask, partial)
    return finish(position, y, coef, dpack, partial)


def solution(mesh):
    in_specs = (
        P(None, "four", None, "dom"),
        P(None, None, None, "dom"),
        P("dom"),
        P(None, "dom"),
        P(),
        P(),
        P(),
        P("dom", None),
        P("dom", None),
    )
    out_specs = P(None, "four", None, "dom")
    return jax.shard_map(
        per_device, mesh=mesh, in_specs=in_specs, out_specs=out_specs, check_vma=False
    )
```

```python
import functools
import math

import jax
import jax.numpy as jnp
import ml_dtypes
import numpy as np
from jax import lax
from jax.experimental import pallas as pl
from jax.experimental.pallas import tpu as pltpu
from jax.sharding import PartitionSpec as P

PLANES = 256
PENALTY = 0.5
RELAXATION = 0.8
TIME_STEP = 0.2
INTERACTION = 2.0
LINE = 8
IN_FLIGHT = 5

F32 = jnp.float32
BF16 = jnp.bfloat16
VMEM_LIMIT = 24 * 1024 * 1024
SMEM_SPEC = pl.BlockSpec(memory_space=pltpu.SMEM)


def params():
    return pltpu.CompilerParams(vmem_limit_bytes=VMEM_LIMIT)


def cost(flops, moved):
    return pl.CostEstimate(flops=int(flops), bytes_accessed=int(moved), transcendentals=0)


def split(x):
    high = x.astype(BF16)
    low = (x - high.astype(F32)).astype(BF16)
    return high, low


def dot(a, b):
    return lax.dot_general(a, b, (((1,), (0,)), ((), ())), preferred_element_type=F32)


def pack_matrix(m):
    high, low = split(m)
    return jnp.concatenate([high, low, high], axis=1)


def slab(refs, c):
    return jnp.concatenate([ref[c] for ref in refs], axis=0)


def pack_field(v):
    high, low = split(v)
    return jnp.concatenate([high, high, low], axis=0)


def coef_table(length):
    c = np.arange(length)[:, None]
    j = np.arange(length)[None, :]
    angle = ((c // 2) * j % length) * (2.0 * math.pi / length)
    table = np.where(c % 2 == 1, np.sin(angle), np.cos(angle)) * math.sqrt(2.0 / length)
    table[0] = 1.0 / math.sqrt(length)
    table[1] = np.where(np.arange(length) % 2 == 0, 1.0, -1.0) / math.sqrt(length)
    high = table.astype(ml_dtypes.bfloat16)
    low = (table - high.astype(np.float64)).astype(ml_dtypes.bfloat16)
    return np.concatenate([high, low], axis=0)


def permute_kernel(peers, pos_ref, table_ref, o_ref):
    planes = table_ref.shape[1]
    per = planes // peers
    me = pos_ref[1]
    row = lax.broadcasted_iota(jnp.int32, (planes, planes), 0)
    col = lax.broadcasted_iota(jnp.int32, (planes, planes), 1)
    swap = jnp.where(row == ((col // per) ^ me) * per + col % per, 1.0, 0.0).astype(BF16)
    for half in range(2):
        rows = pl.ds(half * planes, planes)
        turned = dot(swap, table_ref[rows, :]).astype(BF16)
        o_ref[rows, :] = dot(turned, swap).astype(BF16)


def permuted_table(position, table, peers):
    return pl.pallas_call(
        functools.partial(permute_kernel, peers),
        out_shape=jax.ShapeDtypeStruct(table.shape, BF16),
        in_specs=[SMEM_SPEC, pl.BlockSpec(memory_space=pltpu.VMEM)],
        compiler_params=params(),
        cost_estimate=cost(1e8, 4e6),
        name="permuted_table",
    )(position, table)


def transform_kernel(count, pos_ref, table_ref, *refs):
    planes = table_ref.shape[1]
    both = table_ref[...]
    high_table = both[:planes]
    width = refs[0].shape[-1]
    nodes = refs[0].shape[-2]
    per = planes // count
    outs = refs[count:]
    if len(outs) < count:
        outs = [outs[0].at[pos_ref[1] ^ d] for d in range(count)]
    flat = [ref.reshape(per * nodes, width) for ref in refs[:count]]
    outs = [ref.reshape(per * nodes, width) for ref in outs]
    for n in range(nodes):
        rows = pl.ds(n, per, stride=nodes) if nodes > 1 else pl.ds(0, per)
        high, low = split(jnp.concatenate([ref[rows, :] for ref in flat], axis=0))
        wide = dot(both, high)
        result = wide[:planes] + (wide[planes:] + dot(high_table, low))
        for d, ref in enumerate(outs):
            ref[rows, :] = result[d * per : (d + 1) * per]


def transform(position, blocks, table, join=False):
    per, nodes, elements = blocks[0].shape
    count = len(blocks)
    width = 128
    block = pl.BlockSpec((per, nodes, width), lambda i: (0, 0, i))
    out_shape = [jax.ShapeDtypeStruct(v.shape, F32) for v in blocks]
    out_specs = [block] * count
    if join:
        out_shape = jax.ShapeDtypeStruct((count, per, nodes, elements), F32)
        out_specs = pl.BlockSpec((count, per, nodes, width), lambda i: (0, 0, 0, i))
    size = count * blocks[0].size
    return pl.pallas_call(
        functools.partial(transform_kernel, count),
        out_shape=out_shape,
        grid=(elements // width,),
        in_specs=[SMEM_SPEC, pl.BlockSpec(table.shape, lambda i: (0, 0))] + [block] * count,
        out_specs=out_specs,
        compiler_params=params(),
        cost_estimate=cost(6 * PLANES * size, 8 * size),
        name="transform",
    )(position, table, *blocks)


def pack_kernel(pos_ref, *refs):
    count = len(refs) // 2
    for source, target in zip(refs[:count], refs[count:]):
        target[...] = source[0]


def pack(position, adjoint, comp, peers):
    _, per, nodes, elements = adjoint.shape
    part = nodes // peers
    block = per // 2

    def source(d):
        return pl.BlockSpec((1, block, part, elements), lambda i, pos: (comp, i, pos[1] ^ d, 0))

    size = per * nodes * elements
    return pl.pallas_call(
        pack_kernel,
        out_shape=[jax.ShapeDtypeStruct((per, part, elements), F32)] * peers,
        grid_spec=pltpu.PrefetchScalarGridSpec(
            num_scalar_prefetch=1,
            grid=(per // block,),
            in_specs=[source(d) for d in range(peers)],
            out_specs=[pl.BlockSpec((block, part, elements), lambda i, pos: (i, 0, 0))] * peers,
        ),
        compiler_params=params(),
        cost_estimate=cost(0, 16 * size),
        name="pack",
    )(position, *[adjoint] * peers)


BXR, BYS, DXBX, DXBY, DYBX, DYBY, DIAG = range(7)


def line_of(me, d):
    return pl.ds(pl.multiple_of((me ^ d) * LINE, LINE), LINE)


def own_order(ref, me, *lead):
    lines = ref.shape[-2] // LINE
    return jnp.concatenate([ref[(*lead, line_of(me, d), slice(None))] for d in range(lines)], axis=0)


def prep_kernel(
    pos_ref, bank_ref, snap_ref, geo_ref, dr_ref, ds_ref, st_ref, up_ref, lo_ref,
    coef_ref, dpack_ref, spack_ref, gather_ref, scatter_ref, mask_ref,
):
    elements = geo_ref.shape[1]
    nodes = dr_ref.shape[0]
    lines = nodes // LINE
    me = pos_ref[1]
    row = lax.broadcasted_iota(jnp.int32, (nodes, nodes), 0)
    col = lax.broadcasted_iota(jnp.int32, (nodes, nodes), 1)
    swap = jnp.where(row == ((col // LINE) ^ me) * LINE + col % LINE, 1.0, 0.0).astype(BF16)

    def permuted(ref):
        high, low = split(own_order(ref, me))
        return dot(high, swap) + dot(low, swap)

    snap = snap_ref[...]
    base = [
        sum(
            jnp.where(snap == k, own_order(bank_ref, me, k, i), 0.0)
            for k in range(bank_ref.shape[0])
        )
        for i in range(2)
    ]
    rx = geo_ref[0:1, :]
    sy = geo_ref[1:2, :]
    dpack = pack_matrix(jnp.concatenate([permuted(dr_ref), permuted(ds_ref)], axis=0))
    dpack_ref[...] = dpack
    bx = dot(dpack, pack_field(base[0]))
    by = dot(dpack, pack_field(base[1]))
    coef_ref[BXR] = base[0] * rx
    coef_ref[BYS] = base[1] * sy
    coef_ref[DXBX] = rx * bx[:nodes]
    coef_ref[DXBY] = rx * by[:nodes]
    coef_ref[DYBX] = sy * bx[nodes:]
    coef_ref[DYBY] = sy * by[nodes:]
    diag = jnp.sum(jnp.where(row == col, st_ref[...], 0.0), axis=0, keepdims=True)
    own = ((row // LINE) ^ me) * LINE + row % LINE == col
    diag = jnp.sum(jnp.where(own, diag, 0.0), axis=1, keepdims=True)
    spack_ref[...] = pack_matrix(jnp.where(row == col, 0.0, permuted(st_ref)))
    coef_ref[DIAG] = jnp.broadcast_to(diag, (nodes, elements))
    shared = up_ref.shape[1]
    for side, (ref, first) in enumerate(((up_ref, LINE - 1), (lo_ref, 0))):
        index = ref[...]
        node = index // elements
        element = index - node * elements
        hot = lax.broadcasted_iota(jnp.int32, (elements, shared), 0) == element
        hot = jnp.where(hot, 1.0, 0.0)
        gather_ref[side] = hot.astype(BF16)
        back = hot.T.astype(BF16)
        scatter_ref[side] = back
        mask = (lax.broadcasted_iota(jnp.int32, (lines, shared), 0) ^ me) == node // LINE
        mask = jnp.where(mask, 1.0, 0.0)
        mask_ref[side] = mask
        count = dot(mask.astype(BF16), back)
        for s in range(lines):
            n = s * LINE + first
            coef_ref[DIAG, n : n + 1, :] = coef_ref[DIAG, n : n + 1, :] + PENALTY * count[s : s + 1]


def prepare(position, base_bank, snapshot, geometry, diff_r, diff_s, stiffness, upper, lower):
    nodes = diff_r.shape[0]
    elements = geometry.shape[1]
    shared = upper.shape[1]
    return pl.pallas_call(
        prep_kernel,
        out_shape=[
            jax.ShapeDtypeStruct((7, nodes, elements), F32),
            jax.ShapeDtypeStruct((2 * nodes, 3 * nodes), BF16),
            jax.ShapeDtypeStruct((nodes, 3 * nodes), BF16),
            jax.ShapeDtypeStruct((2, elements, shared), BF16),
            jax.ShapeDtypeStruct((2, shared, elements), BF16),
            jax.ShapeDtypeStruct((2, nodes // LINE, shared), F32),
        ],
        in_specs=[SMEM_SPEC] + [pl.BlockSpec(memory_space=pltpu.VMEM)] * 8,
        compiler_params=params(),
        cost_estimate=cost(1e7, 8e6),
        name="prepare",
    )(position, base_bank, snapshot.reshape(1, elements), geometry, diff_r, diff_s, stiffness, upper, lower)


def face_of(ref, side):
    rows, elements = ref.shape
    return ref.reshape(rows // LINE, LINE, elements).at[:, LINE - 1 if side == 0 else 0, :]


def gather_faces(side, fields, gather_ref, mask_ref):
    lines = mask_ref.shape[1]
    high, low = split(jnp.concatenate(fields, axis=0))
    rows = high.shape[0]
    both = dot(jnp.concatenate([high, low], axis=0), gather_ref[side])
    picked = both[:rows] + both[rows:]
    shared = picked.shape[1]
    return jnp.sum(picked.reshape(rows // lines, lines, shared) * mask_ref[side][None], axis=1)


def scatter_faces(side, values, scatter_ref, mask_ref):
    mask = mask_ref[side]
    coefs, shared = values.shape
    spread = (values[:, None, :] * mask[None]).reshape(coefs * mask.shape[0], shared)
    high, low = split(spread)
    rows = high.shape[0]
    both = dot(jnp.concatenate([high, low], axis=0), scatter_ref[side])
    return both[:rows] + both[rows:]


def local_sweep(pot, source, inverse, spack):
    applied = dot(spack, pack_field(pot))
    return (1.0 - RELAXATION) * pot + inverse * (source - applied)


def coef_block(coefs):
    return 8 if coefs % 8 == 0 else coefs


def start_kernel(
    block, count, pos_ref, geo_ref, diag_ref, dpack_ref, spack_ref, gather_ref, mask_ref, *refs
):
    z_refs, x_refs = refs[:count], refs[count : 2 * count]
    source_ref, inverse_ref, local_ref, up_ref, lo_ref, pot_ref = refs[2 * count :]
    nodes, elements = diag_ref.shape[1:]
    beta = 4.0 / PLANES
    first = pos_ref[0] * (block * pl.num_programs(0)) + pl.program_id(0) * block
    rx = geo_ref[0:1, :]
    mass = 1.0 / (rx * geo_ref[1:2, :])
    diag = diag_ref[0]
    drpack = dpack_ref[:nodes]
    spack = spack_ref[...]
    for c in range(block):
        index = first + c
        wave = beta * (index // 2).astype(F32)
        shift = beta * jnp.where(index == 1, PLANES // 2, index // 2).astype(F32)
        shift = shift * shift
        z = slab(z_refs, c)
        other = slab(x_refs, c + 1 if c % 2 == 0 else c - 1)
        turned = (wave if c % 2 == 0 else -wave) * other
        source = turned - rx * dot(drpack, pack_field(z))
        inverse = RELAXATION / (diag + shift * mass)
        pot = inverse * source
        rows = pl.ds(c * nodes, nodes)
        source_ref[rows, :] = source
        inverse_ref[rows, :] = inverse
        pot_ref[rows, :] = pot
        local_ref[rows, :] = local_sweep(pot, source, inverse, spack)
    for side, out in ((0, up_ref), (1, lo_ref)):
        fields = [face_of(ref, side)[...] for ref in (pot_ref, local_ref, inverse_ref)]
        picked = gather_faces(side, fields, gather_ref, mask_ref)
        for k in range(3):
            out[k] = picked[k * block : (k + 1) * block]


def whole(shape):
    return pl.BlockSpec(shape, lambda *i: (0,) * len(shape))


def start_solve(position, z, x, geometry, coef, dpack, spack, gather, mask):
    coefs, part, elements = z[0].shape
    nodes = len(z) * part
    shared = gather.shape[2]
    block = coef_block(coefs)
    field = [pl.BlockSpec((block, part, elements), lambda i: (i, 0, 0))] * len(z)
    flat = pl.BlockSpec((block * nodes, elements), lambda i: (i, 0))
    face = pl.BlockSpec((3, block, shared), lambda i: (0, i, 0))
    size = coefs * nodes * elements
    return pl.pallas_call(
        functools.partial(start_kernel, block, len(z)),
        out_shape=[jax.ShapeDtypeStruct((coefs * nodes, elements), F32)] * 3
        + [jax.ShapeDtypeStruct((3, coefs, shared), F32)] * 2,
        grid=(coefs // block,),
        in_specs=[
            SMEM_SPEC, whole(geometry.shape),
            pl.BlockSpec((1, nodes, elements), lambda i: (DIAG, 0, 0)),
            whole(dpack.shape), whole(spack.shape), whole(gather.shape), whole(mask.shape),
            *field, *field,
        ],
        out_specs=[flat, flat, flat, face, face],
        scratch_shapes=[pltpu.VMEM((block * nodes, elements), F32)],
        compiler_params=params(),
        cost_estimate=cost(12 * nodes * size, 20 * size),
        name="start_solve",
    )(position, geometry, coef, dpack, spack, gather, mask, *z, *x)


def sweeps_kernel(
    block, keep, local_ref, source_ref, inverse_ref, own_up_ref, own_lo_ref,
    own_inv_up_ref, own_inv_lo_ref, got_up_ref, got_lo_ref, inv_up_ref, inv_lo_ref, spack_ref, gather_ref, scatter_ref, mask_ref,
    next_ref, up_ref, lo_ref, pot_ref,
):
    nodes = spack_ref.shape[0]
    spack = spack_ref[...]
    lines = block * (nodes // LINE)
    partners = []
    for side, own, own_inv, got, inv in (
        (0, own_up_ref, own_inv_up_ref, got_up_ref, inv_up_ref),
        (1, own_lo_ref, own_inv_lo_ref, got_lo_ref, inv_lo_ref),
    ):
        scale = PENALTY * own_inv[0]
        now = scale * got[0]
        later = scale * (got[1] + PENALTY * inv[0] * own[0])
        both = scatter_faces(side, jnp.concatenate([now, later], axis=0), scatter_ref, mask_ref)
        partners.append((both[:lines], both[lines:]))
    pot_ref[...] = local_ref[...]
    for side in range(2):
        face = face_of(pot_ref, side)
        face[...] = face[...] + partners[side][0]
    for c in range(block):
        rows = pl.ds(c * nodes, nodes)
        pot_ref[rows, :] = local_sweep(pot_ref[rows, :], source_ref[rows, :], inverse_ref[rows, :], spack)
    for side in range(2):
        face = face_of(pot_ref, side)
        face[...] = face[...] + partners[side][1]
    for c in range(block):
        rows = pl.ds(c * nodes, nodes)
        next_ref[rows, :] = local_sweep(pot_ref[rows, :], source_ref[rows, :], inverse_ref[rows, :], spack)
    for side, out in ((0, up_ref), (1, lo_ref)):
        fields = [face_of(ref, side)[...] for ref in (pot_ref, next_ref)[:keep]]
        picked = gather_faces(side, fields, gather_ref, mask_ref)
        for k in range(keep):
            out[k] = picked[k * block : (k + 1) * block]


def two_sweeps(keep, local, source, inverse, own, own_inv, got, inv, spack, gather, scatter, mask):
    nodes = spack.shape[0]
    elements = local.shape[1]
    coefs = local.shape[0] // nodes
    shared = gather.shape[2]
    block = coef_block(coefs)
    flat = pl.BlockSpec((block * nodes, elements), lambda i: (i, 0))
    one = pl.BlockSpec((1, block, shared), lambda i: (0, i, 0))
    two = pl.BlockSpec((2, block, shared), lambda i: (0, i, 0))
    third = pl.BlockSpec((1, block, shared), lambda i: (2, i, 0))
    face = pl.BlockSpec((keep, block, shared), lambda i: (0, i, 0))
    size = coefs * nodes * elements
    return pl.pallas_call(
        functools.partial(sweeps_kernel, block, keep),
        out_shape=[jax.ShapeDtypeStruct(local.shape, F32)]
        + [jax.ShapeDtypeStruct((keep, coefs, shared), F32)] * 2,
        grid=(coefs // block,),
        in_specs=[
            flat, flat, flat, one, one, third, third, two, two, third, third,
            whole(spack.shape), whole(gather.shape), whole(scatter.shape), whole(mask.shape),
        ],
        out_specs=[flat, face, face],
        scratch_shapes=[pltpu.VMEM((block * nodes, elements), F32)],
        compiler_params=params(),
        cost_estimate=cost(12 * nodes * size, 16 * size),
        name="two_sweeps",
    )(local, source, inverse, *own, *own_inv, *got, *inv, spack, gather, scatter, mask)


def store_own(ref, me, value, *lead):
    for d in range(value.shape[0] // LINE):
        ref[(*lead, line_of(me, d), slice(None))] = value[d * LINE : (d + 1) * LINE]


def partial_kernel(block, count, pos_ref, coef_ref, dpack_ref, *refs):
    z_refs, x_refs, o_ref = refs[:count], refs[count : 2 * count], refs[2 * count]
    nodes = coef_ref.shape[1]
    dpack = dpack_ref[...]
    me = pos_ref[1]
    for c in range(block):
        z = slab(z_refs, c)
        slopes = dot(dpack, pack_field(z))
        moved = coef_ref[BXR] * slopes[:nodes] + coef_ref[BYS] * slopes[nodes:]
        store_own(o_ref, me, z - TIME_STEP * (moved + INTERACTION * z), 2, c)
        x = slab(x_refs, c)
        slopes = dot(dpack, pack_field(x))
        moved = coef_ref[BXR] * slopes[:nodes] + coef_ref[BYS] * slopes[nodes:]
        store_own(o_ref, me, x + TIME_STEP * (x * coef_ref[DXBX] - moved - INTERACTION * x), 0, c)
        store_own(o_ref, me, TIME_STEP * (x * coef_ref[DYBX]), 1, c)


def partial_update(position, z, x, coef, dpack):
    coefs, part, elements = z[0].shape
    nodes = len(z) * part
    block = coef_block(coefs)
    field = [pl.BlockSpec((block, part, elements), lambda i: (i, 0, 0))] * len(z)
    size = coefs * nodes * elements
    return pl.pallas_call(
        functools.partial(partial_kernel, block, len(z)),
        out_shape=jax.ShapeDtypeStruct((3, coefs, nodes, elements), F32),
        grid=(coefs // block,),
        in_specs=[SMEM_SPEC, whole(coef.shape), whole(dpack.shape), *field, *field],
        out_specs=pl.BlockSpec((3, block, nodes, elements), lambda i: (0, i, 0, 0)),
        compiler_params=params(),
        cost_estimate=cost(24 * nodes * size, 20 * size),
        name="partial_update",
    )(position, coef, dpack, *z, *x)


def force_kernel(
    block, pos_ref, local_ref, inv_up_ref, inv_lo_ref, got_up_ref, got_lo_ref, geo_ref, dpack_ref,
    scatter_ref, mask_ref, part_ref, o_ref, pot_ref,
):
    nodes = dpack_ref.shape[0] // 2
    scale = TIME_STEP * INTERACTION
    which = pl.program_id(1)
    me = pos_ref[1]

    @pl.when(which == 0)
    def _():
        pot_ref[...] = local_ref[...]
        for side, inv, got in ((0, inv_up_ref, got_up_ref), (1, inv_lo_ref, got_lo_ref)):
            face = face_of(pot_ref, side)
            partner = PENALTY * inv[0] * got[0]
            face[...] = face[...] + scatter_faces(side, partner, scatter_ref, mask_ref)
        first = pos_ref[0] * (block * pl.num_programs(0)) + pl.program_id(0) * block
        for c in range(block):
            wave = (4.0 / PLANES) * ((first + c) // 2).astype(F32)
            factor = scale * (wave if c % 2 == 0 else -wave)
            other = c + 1 if c % 2 == 0 else c - 1
            turned = factor * pot_ref[pl.ds(other * nodes, nodes), :]
            store_own(o_ref, me, own_order(part_ref, me, 0, c) + turned, 0, c)

    @pl.when(which == 1)
    def _():
        drpack = dpack_ref[:nodes]
        factor = scale * geo_ref[0:1, :]
        for c in range(block):
            slope = dot(drpack, pack_field(pot_ref[pl.ds(c * nodes, nodes), :]))
            store_own(o_ref, me, own_order(part_ref, me, 0, c) - factor * slope, 0, c)


def add_force(position, local, own_inv, got, geometry, dpack, scatter, mask, partial):
    _, coefs, nodes, elements = partial.shape
    shared = scatter.shape[1]
    block = coef_block(coefs)
    flat = pl.BlockSpec((block * nodes, elements), lambda i, j: (i, 0))
    one = pl.BlockSpec((1, block, shared), lambda i, j: (0, i, 0))
    third = pl.BlockSpec((1, block, shared), lambda i, j: (2, i, 0))
    comp = pl.BlockSpec((1, block, nodes, elements), lambda i, j: (2 * j, i, 0, 0))
    size = coefs * nodes * elements
    return pl.pallas_call(
        functools.partial(force_kernel, block),
        out_shape=jax.ShapeDtypeStruct(partial.shape, F32),
        grid=(coefs // block, 2),
        in_specs=[
            SMEM_SPEC, flat, third, third, one, one, whole(geometry.shape), whole(dpack.shape),
            whole(scatter.shape), whole(mask.shape), comp,
        ],
        out_specs=comp,
        scratch_shapes=[pltpu.VMEM((block * nodes, elements), F32)],
        input_output_aliases={10: 0},
        compiler_params=params(),
        cost_estimate=cost(6 * nodes * size, 24 * size),
        name="add_force",
    )(position, local, *own_inv, *got, geometry, dpack, scatter, mask, partial)


def finish_kernel(block, count, pos_ref, coef_ref, dpack_ref, part_ref, *refs):
    y_refs, o_ref = [ref.at[0] for ref in refs[:count]], refs[count]
    nodes = coef_ref.shape[1]
    me = pos_ref[1]
    dpack = dpack_ref[...]
    for c in range(block):
        y = slab(y_refs, c)
        slopes = dot(dpack, pack_field(y))
        moved = coef_ref[BXR] * slopes[:nodes] + coef_ref[BYS] * slopes[nodes:]
        change = y + TIME_STEP * (y * coef_ref[DYBY] - moved)
        store_own(o_ref, me, own_order(part_ref, me, 1, c) + change, 1, c)
        change = TIME_STEP * (y * coef_ref[DXBY])
        store_own(o_ref, me, own_order(part_ref, me, 0, c) + change, 0, c)


def finish(position, y, coef, dpack, partial):
    lines, coefs, part, elements = y.shape
    nodes = lines * part
    block = coef_block(coefs)

    def source(d):
        return pl.BlockSpec((1, block, part, elements), lambda i, pos: (pos[1] ^ d, i, 0, 0))

    comp = pl.BlockSpec((2, block, nodes, elements), lambda i, pos: (0, i, 0, 0))
    size = coefs * nodes * elements
    return pl.pallas_call(
        functools.partial(finish_kernel, block, lines),
        out_shape=jax.ShapeDtypeStruct(partial.shape, F32),
        grid_spec=pltpu.PrefetchScalarGridSpec(
            num_scalar_prefetch=1,
            grid=(coefs // block,),
            in_specs=[whole(coef.shape), whole(dpack.shape), comp] + [source(d) for d in range(lines)],
            out_specs=comp,
        ),
        input_output_aliases={3: 0},
        compiler_params=params(),
        cost_estimate=cost(12 * nodes * size, 20 * size),
        name="finish",
    )(position, coef, dpack, partial, *[y] * lines)


def to_all(blocks):
    return lax.all_to_all(blocks, "four", split_axis=0, concat_axis=0, tiled=True)


def swap_faces(up, lo):
    peers = lax.axis_size("dom")
    up_way = [(i, (i + 1) % peers) for i in range(peers)]
    down_way = [(j, i) for i, j in up_way]
    return lax.ppermute(lo, "dom", down_way), lax.ppermute(up, "dom", up_way)


def tie(blocks, value):
    blocks = list(blocks)
    first = min(2, len(blocks) - 1)
    blocks[first], value = lax.optimization_barrier((blocks[first], value))
    return blocks, value


def per_device(
    adjoint, base_bank, snapshot, geometry, diff_r, diff_s, stiffness, upper_list, lower_list
):
    _, per, nodes, elements = adjoint.shape
    peers = lax.axis_size("four")
    lines = nodes // LINE
    direct = peers == lines
    place = lax.axis_index("four").astype(jnp.int32)
    position = jnp.stack([place, place if direct else jnp.zeros_like(place)])
    natural = jnp.asarray(coef_table(PLANES))
    table = permuted_table(position, natural, lines)
    flight = []

    def exchange(blocks):
        first = len(flight)
        order = sorted(range(1, peers), key=lambda d: (d < 2, d % 2, d))
        for d in order:
            block = blocks[d]
            if len(flight) >= IN_FLIGHT:
                block, flight[-IN_FLIGHT] = lax.optimization_barrier((block, flight[-IN_FLIGHT]))
            flight.append(lax.ppermute(block, "four", [(i, i ^ d) for i in range(peers)]))

        def received():
            got = {d: flight[first + k] for k, d in enumerate(order)}
            return [blocks[0]] + [got[d] for d in range(1, peers)]

        return received

    def columns(comp):
        if direct:
            return pack(position, adjoint, comp, peers)
        return [jnp.moveaxis(adjoint[comp].reshape(per, peers, nodes // peers, elements), 1, 0)]

    def spread(blocks):
        if direct:
            return exchange(blocks)
        got = [to_all(blocks[0]).reshape(PLANES, nodes // peers, elements)]
        return lambda: got

    def by_line(joined):
        if direct:
            return to_all(joined)
        got = to_all(joined.reshape(peers, per, nodes // peers, elements))
        got = jnp.moveaxis(got, 0, 1).reshape(per, lines, LINE, elements)
        return jnp.moveaxis(got, 1, 0)

    def collect(blocks):
        if direct:
            return exchange(blocks)
        got = by_line(blocks[0])
        return lambda: [got[d] for d in range(lines)]

    z_blocks = columns(2)
    z_columns = spread(z_blocks)
    x_blocks = columns(0)
    x_blocks, table = tie(x_blocks, table)
    x_columns = spread(x_blocks)
    constants = prepare(
        position, base_bank, snapshot, geometry, diff_r, diff_s, stiffness, upper_list, lower_list
    )
    z_coefs = transform(position, z_columns(), table)
    z_coefs, constants = tie(z_coefs, constants)
    coef, dpack, spack, gather, scatter, mask = constants
    z_later = collect(z_coefs)
    y_blocks = columns(1)
    x_coefs = transform(position, x_columns(), table)
    x_coefs, y_blocks = tie(x_coefs, y_blocks)
    x_later = collect(x_coefs)
    y_columns = spread(y_blocks)
    z = z_later()
    x = x_later()
    source, inverse, local, up, lo = start_solve(
        position, z, x, geometry, coef, dpack, spack, gather, mask
    )
    own_inv = (up, lo)
    got = swap_faces(up, lo)
    inv = got
    partial = partial_update(position, z, x, coef, dpack)
    local, up, lo = two_sweeps(
        2, local, source, inverse, (up, lo), own_inv, got, inv, spack, gather, scatter, mask
    )
    y_got = y_columns()
    y_got[0], local = lax.optimization_barrier((y_got[0], local))
    got = swap_faces(up, lo)
    y = by_line(transform(position, y_got, table, join=True))
    local, up, lo = two_sweeps(
        1, local, source, inverse, (up, lo), own_inv, got, inv, spack, gather, scatter, mask
    )
    got = swap_faces(up, lo)
    partial = add_force(position, local, own_inv, got, geometry, dpack, scatter, mask, partial)
    return finish(position, y, coef, dpack, partial)


def solution(mesh):
    in_specs = (
        P(None, "four", None, "dom"),
        P(None, None, None, "dom"),
        P("dom"),
        P(None, "dom"),
        P(),
        P(),
        P(),
        P("dom", None),
        P("dom", None),
    )
    out_specs = P(None, "four", None, "dom")
    return jax.shard_map(
        per_device, mesh=mesh, in_specs=in_specs, out_specs=out_specs, check_vma=False
    )
```

```python
import functools
import math

import jax
import jax.numpy as jnp
import ml_dtypes
import numpy as np
from jax import lax
from jax.experimental import pallas as pl
from jax.experimental.pallas import tpu as pltpu
from jax.sharding import PartitionSpec as P

PLANES = 256
PENALTY = 0.5
RELAXATION = 0.8
TIME_STEP = 0.2
INTERACTION = 2.0
LINE = 8
IN_FLIGHT = 5

F32 = jnp.float32
BF16 = jnp.bfloat16
VMEM_LIMIT = 20 * 1024 * 1024
LARGE_LIMIT = 56 * 1024 * 1024
SMEM_SPEC = pl.BlockSpec(memory_space=pltpu.SMEM)


def params(limit=VMEM_LIMIT):
    return pltpu.CompilerParams(vmem_limit_bytes=limit)


SHORT = pl.CostEstimate(flops=10**6, bytes_accessed=10**5, transcendentals=0)


def cost(flops, moved):
    return pl.CostEstimate(flops=int(flops), bytes_accessed=int(moved), transcendentals=0)


def split(x):
    high = x.astype(BF16)
    low = (x - high.astype(F32)).astype(BF16)
    return high, low


def dot(a, b):
    return lax.dot_general(a, b, (((1,), (0,)), ((), ())), preferred_element_type=F32)


def pack_matrix(m):
    high, low = split(m)
    return jnp.concatenate([high, low, high], axis=1)


def slab(refs, c):
    return jnp.concatenate([ref[c] for ref in refs], axis=0)


def pack_field(v):
    high, low = split(v)
    return jnp.concatenate([high, high, low], axis=0)


def coef_table(length):
    c = np.arange(length)[:, None]
    j = np.arange(length)[None, :]
    angle = ((c // 2) * j % length) * (2.0 * math.pi / length)
    table = np.where(c % 2 == 1, np.sin(angle), np.cos(angle)) * math.sqrt(2.0 / length)
    table[0] = 1.0 / math.sqrt(length)
    table[1] = np.where(np.arange(length) % 2 == 0, 1.0, -1.0) / math.sqrt(length)
    high = table.astype(ml_dtypes.bfloat16)
    low = (table - high.astype(np.float64)).astype(ml_dtypes.bfloat16)
    return np.concatenate([high, low], axis=0)


def permute_kernel(peers, pos_ref, table_ref, o_ref):
    planes = table_ref.shape[1]
    per = planes // peers
    me = pos_ref[1]
    row = lax.broadcasted_iota(jnp.int32, (planes, planes), 0)
    col = lax.broadcasted_iota(jnp.int32, (planes, planes), 1)
    swap = jnp.where(row == ((col // per) ^ me) * per + col % per, 1.0, 0.0).astype(BF16)
    for half in range(2):
        rows = pl.ds(half * planes, planes)
        turned = dot(swap, table_ref[rows, :]).astype(BF16)
        o_ref[rows, :] = dot(turned, swap).astype(BF16)


def permuted_table(position, table, peers):
    return pl.pallas_call(
        functools.partial(permute_kernel, peers),
        out_shape=jax.ShapeDtypeStruct(table.shape, BF16),
        in_specs=[SMEM_SPEC, pl.BlockSpec(memory_space=pltpu.VMEM)],
        compiler_params=params(),
        cost_estimate=cost(1e8, 4e6),
        name="permuted_table",
    )(position, table)


def transform_kernel(count, table_ref, *refs):
    planes = table_ref.shape[1]
    both = table_ref[...]
    high_table = both[:planes]
    width = refs[0].shape[-1]
    nodes = refs[0].shape[-2]
    per = planes // count
    flat = [ref.reshape(per * nodes, width) for ref in refs]
    for n in range(nodes):
        rows = pl.ds(n, per, stride=nodes) if nodes > 1 else pl.ds(0, per)
        high, low = split(jnp.concatenate([ref[rows, :] for ref in flat[:count]], axis=0))
        wide = dot(both, high)
        result = wide[:planes] + (wide[planes:] + dot(high_table, low))
        for d, ref in enumerate(flat[count:]):
            ref[rows, :] = result[d * per : (d + 1) * per]


def transform(blocks, table):
    per, nodes, elements = blocks[0].shape
    count = len(blocks)
    width = 128
    block = pl.BlockSpec((per, nodes, width), lambda i: (0, 0, i))
    size = count * blocks[0].size
    return pl.pallas_call(
        functools.partial(transform_kernel, count),
        out_shape=[jax.ShapeDtypeStruct(v.shape, F32) for v in blocks],
        grid=(elements // width,),
        in_specs=[pl.BlockSpec(table.shape, lambda i: (0, 0))] + [block] * count,
        out_specs=[block] * count,
        compiler_params=params(),
        cost_estimate=cost(6 * PLANES * size, 8 * size),
        name="transform",
    )(table, *blocks)


def pack_kernel(comp, pos_ref, x_ref, *refs):
    outs, sems = refs[:-1], refs[-1]
    copies = [
        pltpu.make_async_copy(x_ref.at[comp, :, line_of(pos_ref[1], d), :], out, sems.at[d])
        for d, out in enumerate(outs)
    ]
    for copy in copies:
        copy.start()
    for copy in copies:
        copy.wait()


def pack(position, adjoint, comp, limit):
    _, per, nodes, elements = adjoint.shape
    lines = nodes // LINE
    size = per * nodes * elements
    return pl.pallas_call(
        functools.partial(pack_kernel, comp),
        out_shape=[jax.ShapeDtypeStruct((per, LINE, elements), F32)] * lines,
        in_specs=[SMEM_SPEC, pl.BlockSpec(memory_space=pltpu.HBM)],
        out_specs=[pl.BlockSpec(memory_space=pl.ANY)] * lines,
        scratch_shapes=[pltpu.SemaphoreType.DMA((lines,))],
        compiler_params=params(limit),
        cost_estimate=cost(0, 8 * size),
        name="pack",
    )(position, adjoint)


BXR, BYS, DXBX, DXBY, DYBX, DYBY, DIAG = range(7)


def line_of(me, d):
    return pl.ds(pl.multiple_of((me ^ d) * LINE, LINE), LINE)


def own_order(ref, me, *lead):
    lines = ref.shape[-2] // LINE
    return jnp.concatenate([ref[(*lead, line_of(me, d), slice(None))] for d in range(lines)], axis=0)


def prep_kernel(
    pos_ref, bank_ref, snap_ref, geo_ref, dr_ref, ds_ref, st_ref, up_ref, lo_ref,
    coef_ref, dpack_ref, spack_ref, gather_ref, scatter_ref, mask_ref,
):
    elements = geo_ref.shape[1]
    nodes = dr_ref.shape[0]
    lines = nodes // LINE
    me = pos_ref[1]
    row = lax.broadcasted_iota(jnp.int32, (nodes, nodes), 0)
    col = lax.broadcasted_iota(jnp.int32, (nodes, nodes), 1)
    swap = jnp.where(row == ((col // LINE) ^ me) * LINE + col % LINE, 1.0, 0.0).astype(BF16)

    def permuted(ref):
        high, low = split(own_order(ref, me))
        return dot(high, swap) + dot(low, swap)

    snap = snap_ref[...]
    base = [
        sum(
            jnp.where(snap == k, own_order(bank_ref, me, k, i), 0.0)
            for k in range(bank_ref.shape[0])
        )
        for i in range(2)
    ]
    rx = geo_ref[0:1, :]
    sy = geo_ref[1:2, :]
    dpack = pack_matrix(jnp.concatenate([permuted(dr_ref), permuted(ds_ref)], axis=0))
    dpack_ref[...] = dpack
    bx = dot(dpack, pack_field(base[0]))
    by = dot(dpack, pack_field(base[1]))
    coef_ref[BXR] = base[0] * rx
    coef_ref[BYS] = base[1] * sy
    coef_ref[DXBX] = rx * bx[:nodes]
    coef_ref[DXBY] = rx * by[:nodes]
    coef_ref[DYBX] = sy * bx[nodes:]
    coef_ref[DYBY] = sy * by[nodes:]
    diag = jnp.sum(jnp.where(row == col, st_ref[...], 0.0), axis=0, keepdims=True)
    own = ((row // LINE) ^ me) * LINE + row % LINE == col
    diag = jnp.sum(jnp.where(own, diag, 0.0), axis=1, keepdims=True)
    spack_ref[...] = pack_matrix(jnp.where(row == col, 0.0, permuted(st_ref)))
    coef_ref[DIAG] = jnp.broadcast_to(diag, (nodes, elements))
    shared = up_ref.shape[1]
    for side, (ref, first) in enumerate(((up_ref, LINE - 1), (lo_ref, 0))):
        index = ref[...]
        node = index // elements
        element = index - node * elements
        hot = lax.broadcasted_iota(jnp.int32, (elements, shared), 0) == element
        hot = jnp.where(hot, 1.0, 0.0)
        gather_ref[side] = hot.astype(BF16)
        back = hot.T.astype(BF16)
        scatter_ref[side] = back
        mask = (lax.broadcasted_iota(jnp.int32, (lines, shared), 0) ^ me) == node // LINE
        mask = jnp.where(mask, 1.0, 0.0)
        mask_ref[side] = mask
        count = dot(mask.astype(BF16), back)
        for s in range(lines):
            n = s * LINE + first
            coef_ref[DIAG, n : n + 1, :] = coef_ref[DIAG, n : n + 1, :] + PENALTY * count[s : s + 1]


def prepare(position, base_bank, snapshot, geometry, diff_r, diff_s, stiffness, upper, lower):
    nodes = diff_r.shape[0]
    elements = geometry.shape[1]
    shared = upper.shape[1]
    return pl.pallas_call(
        prep_kernel,
        out_shape=[
            jax.ShapeDtypeStruct((7, nodes, elements), F32),
            jax.ShapeDtypeStruct((2 * nodes, 3 * nodes), BF16),
            jax.ShapeDtypeStruct((nodes, 3 * nodes), BF16),
            jax.ShapeDtypeStruct((2, elements, shared), BF16),
            jax.ShapeDtypeStruct((2, shared, elements), BF16),
            jax.ShapeDtypeStruct((2, nodes // LINE, shared), F32),
        ],
        in_specs=[SMEM_SPEC] + [pl.BlockSpec(memory_space=pltpu.VMEM)] * 8,
        compiler_params=params(),
        cost_estimate=cost(1e7, 8e6),
        name="prepare",
    )(position, base_bank, snapshot.reshape(1, elements), geometry, diff_r, diff_s, stiffness, upper, lower)


def face_of(ref, side):
    rows, elements = ref.shape
    return ref.reshape(rows // LINE, LINE, elements).at[:, LINE - 1 if side == 0 else 0, :]


def gather_faces(side, fields, gather_ref, mask_ref):
    lines = mask_ref.shape[1]
    high, low = split(jnp.concatenate(fields, axis=0))
    rows = high.shape[0]
    both = dot(jnp.concatenate([high, low], axis=0), gather_ref[side])
    picked = both[:rows] + both[rows:]
    shared = picked.shape[1]
    return jnp.sum(picked.reshape(rows // lines, lines, shared) * mask_ref[side][None], axis=1)


def scatter_faces(side, values, scatter_ref, mask_ref):
    mask = mask_ref[side]
    coefs, shared = values.shape
    spread = (values[:, None, :] * mask[None]).reshape(coefs * mask.shape[0], shared)
    high, low = split(spread)
    rows = high.shape[0]
    both = dot(jnp.concatenate([high, low], axis=0), scatter_ref[side])
    return both[:rows] + both[rows:]


def local_sweep(pot, source, inverse, spack):
    applied = dot(spack, pack_field(pot))
    return (1.0 - RELAXATION) * pot + inverse * (source - applied)


def coef_block(coefs):
    return 8 if coefs % 8 == 0 else coefs


def start_kernel(
    block, count, pos_ref, geo_ref, diag_ref, dpack_ref, spack_ref, gather_ref, mask_ref, *refs
):
    z_refs, x_refs = refs[:count], refs[count : 2 * count]
    source_ref, inverse_ref, local_ref, up_ref, lo_ref, pot_ref = refs[2 * count :]
    nodes, elements = diag_ref.shape[1:]
    beta = 4.0 / PLANES
    first = pos_ref[0] * (block * pl.num_programs(0)) + pl.program_id(0) * block
    rx = geo_ref[0:1, :]
    mass = 1.0 / (rx * geo_ref[1:2, :])
    diag = diag_ref[0]
    drpack = dpack_ref[:nodes]
    spack = spack_ref[...]
    for c in range(block):
        index = first + c
        wave = beta * (index // 2).astype(F32)
        shift = beta * jnp.where(index == 1, PLANES // 2, index // 2).astype(F32)
        shift = shift * shift
        z = slab(z_refs, c)
        other = slab(x_refs, c + 1 if c % 2 == 0 else c - 1)
        turned = (wave if c % 2 == 0 else -wave) * other
        source = turned - rx * dot(drpack, pack_field(z))
        inverse = RELAXATION / (diag + shift * mass)
        pot = inverse * source
        rows = pl.ds(c * nodes, nodes)
        source_ref[rows, :] = source
        inverse_ref[rows, :] = inverse
        pot_ref[rows, :] = pot
        local_ref[rows, :] = local_sweep(pot, source, inverse, spack)
    for side, out in ((0, up_ref), (1, lo_ref)):
        fields = [face_of(ref, side)[...] for ref in (pot_ref, local_ref, inverse_ref)]
        picked = gather_faces(side, fields, gather_ref, mask_ref)
        for k in range(3):
            out[k] = picked[k * block : (k + 1) * block]


def whole(shape):
    return pl.BlockSpec(shape, lambda *i: (0,) * len(shape))


def start_solve(position, z, x, geometry, coef, dpack, spack, gather, mask):
    coefs, part, elements = z[0].shape
    nodes = len(z) * part
    shared = gather.shape[2]
    block = coef_block(coefs)
    field = [pl.BlockSpec((block, part, elements), lambda i: (i, 0, 0))] * len(z)
    flat = pl.BlockSpec((block * nodes, elements), lambda i: (i, 0))
    face = pl.BlockSpec((3, block, shared), lambda i: (0, i, 0))
    size = coefs * nodes * elements
    return pl.pallas_call(
        functools.partial(start_kernel, block, len(z)),
        out_shape=[jax.ShapeDtypeStruct((coefs * nodes, elements), F32)] * 3
        + [jax.ShapeDtypeStruct((3, coefs, shared), F32)] * 2,
        grid=(coefs // block,),
        in_specs=[
            SMEM_SPEC, whole(geometry.shape),
            pl.BlockSpec((1, nodes, elements), lambda i: (DIAG, 0, 0)),
            whole(dpack.shape), whole(spack.shape), whole(gather.shape), whole(mask.shape),
            *field, *field,
        ],
        out_specs=[flat, flat, flat, face, face],
        scratch_shapes=[pltpu.VMEM((block * nodes, elements), F32)],
        compiler_params=params(),
        cost_estimate=SHORT,
        name="start_solve",
    )(position, geometry, coef, dpack, spack, gather, mask, *z, *x)


def sweeps_kernel(
    block, keep, local_ref, source_ref, inverse_ref, own_up_ref, own_lo_ref,
    own_inv_up_ref, own_inv_lo_ref, got_up_ref, got_lo_ref, inv_up_ref, inv_lo_ref, spack_ref, gather_ref, scatter_ref, mask_ref,
    next_ref, up_ref, lo_ref, pot_ref,
):
    nodes = spack_ref.shape[0]
    spack = spack_ref[...]
    lines = block * (nodes // LINE)
    partners = []
    for side, own, own_inv, got, inv in (
        (0, own_up_ref, own_inv_up_ref, got_up_ref, inv_up_ref),
        (1, own_lo_ref, own_inv_lo_ref, got_lo_ref, inv_lo_ref),
    ):
        scale = PENALTY * own_inv[0]
        now = scale * got[0]
        later = scale * (got[1] + PENALTY * inv[0] * own[0])
        both = scatter_faces(side, jnp.concatenate([now, later], axis=0), scatter_ref, mask_ref)
        partners.append((both[:lines], both[lines:]))
    pot_ref[...] = local_ref[...]
    for side in range(2):
        face = face_of(pot_ref, side)
        face[...] = face[...] + partners[side][0]
    for c in range(block):
        rows = pl.ds(c * nodes, nodes)
        pot_ref[rows, :] = local_sweep(pot_ref[rows, :], source_ref[rows, :], inverse_ref[rows, :], spack)
    for side in range(2):
        face = face_of(pot_ref, side)
        face[...] = face[...] + partners[side][1]
    for c in range(block):
        rows = pl.ds(c * nodes, nodes)
        next_ref[rows, :] = local_sweep(pot_ref[rows, :], source_ref[rows, :], inverse_ref[rows, :], spack)
    for side, out in ((0, up_ref), (1, lo_ref)):
        fields = [face_of(ref, side)[...] for ref in (pot_ref, next_ref)[:keep]]
        picked = gather_faces(side, fields, gather_ref, mask_ref)
        for k in range(keep):
            out[k] = picked[k * block : (k + 1) * block]


def two_sweeps(keep, local, source, inverse, own, own_inv, got, inv, spack, gather, scatter, mask):
    nodes = spack.shape[0]
    elements = local.shape[1]
    coefs = local.shape[0] // nodes
    shared = gather.shape[2]
    block = coef_block(coefs)
    flat = pl.BlockSpec((block * nodes, elements), lambda i: (i, 0))
    one = pl.BlockSpec((1, block, shared), lambda i: (0, i, 0))
    two = pl.BlockSpec((2, block, shared), lambda i: (0, i, 0))
    third = pl.BlockSpec((1, block, shared), lambda i: (2, i, 0))
    face = pl.BlockSpec((keep, block, shared), lambda i: (0, i, 0))
    size = coefs * nodes * elements
    return pl.pallas_call(
        functools.partial(sweeps_kernel, block, keep),
        out_shape=[jax.ShapeDtypeStruct(local.shape, F32)]
        + [jax.ShapeDtypeStruct((keep, coefs, shared), F32)] * 2,
        grid=(coefs // block,),
        in_specs=[
            flat, flat, flat, one, one, third, third, two, two, third, third,
            whole(spack.shape), whole(gather.shape), whole(scatter.shape), whole(mask.shape),
        ],
        out_specs=[flat, face, face],
        scratch_shapes=[pltpu.VMEM((block * nodes, elements), F32)],
        compiler_params=params(),
        cost_estimate=SHORT,
        name="two_sweeps",
    )(local, source, inverse, *own, *own_inv, *got, *inv, spack, gather, scatter, mask)


def store_own(ref, me, value, *lead):
    for d in range(value.shape[0] // LINE):
        ref[(*lead, line_of(me, d), slice(None))] = value[d * LINE : (d + 1) * LINE]


def partial_kernel(block, count, coef_ref, dpack_ref, *refs):
    z_refs, x_refs = refs[:count], refs[count : 2 * count]
    px_ref, py_ref, pz_ref = refs[2 * count :]
    nodes = coef_ref.shape[1]
    dpack = dpack_ref[...]
    for c in range(block):
        z = slab(z_refs, c)
        slopes = dot(dpack, pack_field(z))
        moved = coef_ref[BXR] * slopes[:nodes] + coef_ref[BYS] * slopes[nodes:]
        pz_ref[c] = z - TIME_STEP * (moved + INTERACTION * z)
        x = slab(x_refs, c)
        slopes = dot(dpack, pack_field(x))
        moved = coef_ref[BXR] * slopes[:nodes] + coef_ref[BYS] * slopes[nodes:]
        px_ref[c] = x + TIME_STEP * (x * coef_ref[DXBX] - moved - INTERACTION * x)
        py_ref[c] = TIME_STEP * (x * coef_ref[DYBX])


def partial_update(z, x, coef, dpack):
    coefs, part, elements = z[0].shape
    nodes = len(z) * part
    block = coef_block(coefs)
    field = [pl.BlockSpec((block, part, elements), lambda i: (i, 0, 0))] * len(z)
    out = pl.BlockSpec((block, nodes, elements), lambda i: (i, 0, 0))
    return pl.pallas_call(
        functools.partial(partial_kernel, block, len(z)),
        out_shape=[jax.ShapeDtypeStruct((coefs, nodes, elements), F32)] * 3,
        grid=(coefs // block,),
        in_specs=[whole(coef.shape), whole(dpack.shape), *field, *field],
        out_specs=[out] * 3,
        compiler_params=params(),
        cost_estimate=SHORT,
        name="partial_update",
    )(coef, dpack, *z, *x)


def force_kernel(
    block, pos_ref, local_ref, inv_up_ref, inv_lo_ref, got_up_ref, got_lo_ref, geo_ref, dpack_ref,
    scatter_ref, mask_ref, px_ref, pz_ref, o_ref, x_ref, pot_ref,
):
    nodes = dpack_ref.shape[0] // 2
    scale = TIME_STEP * INTERACTION
    me = pos_ref[1]
    pot_ref[...] = local_ref[...]
    for side, inv, got in ((0, inv_up_ref, got_up_ref), (1, inv_lo_ref, got_lo_ref)):
        face = face_of(pot_ref, side)
        partner = PENALTY * inv[0] * got[0]
        face[...] = face[...] + scatter_faces(side, partner, scatter_ref, mask_ref)
    first = pos_ref[0] * (block * pl.num_programs(0)) + pl.program_id(0) * block
    drpack = dpack_ref[:nodes]
    slope_scale = scale * geo_ref[0:1, :]
    for c in range(block):
        pot = pot_ref[pl.ds(c * nodes, nodes), :]
        slope = dot(drpack, pack_field(pot))
        store_own(o_ref, me, pz_ref[c] - slope_scale * slope, 0, c)
        wave = (4.0 / PLANES) * ((first + c) // 2).astype(F32)
        factor = scale * (wave if c % 2 else -wave)
        other = c - 1 if c % 2 else c + 1
        x_ref[other] = px_ref[other] + factor * pot


def add_force(position, local, own_inv, got, geometry, dpack, scatter, mask, px, pz):
    coefs, nodes, elements = px.shape
    shared = scatter.shape[1]
    block = coef_block(coefs)
    flat = pl.BlockSpec((block * nodes, elements), lambda i: (i, 0))
    one = pl.BlockSpec((1, block, shared), lambda i: (0, i, 0))
    third = pl.BlockSpec((1, block, shared), lambda i: (2, i, 0))
    part = pl.BlockSpec((block, nodes, elements), lambda i: (i, 0, 0))
    return pl.pallas_call(
        functools.partial(force_kernel, block),
        out_shape=[
            jax.ShapeDtypeStruct((3, coefs, nodes, elements), F32),
            jax.ShapeDtypeStruct(px.shape, F32),
        ],
        grid=(coefs // block,),
        in_specs=[
            SMEM_SPEC, flat, third, third, one, one, whole(geometry.shape), whole(dpack.shape),
            whole(scatter.shape), whole(mask.shape), part, part,
        ],
        out_specs=[pl.BlockSpec((1, block, nodes, elements), lambda i: (2, i, 0, 0)), part],
        scratch_shapes=[pltpu.VMEM((block * nodes, elements), F32)],
        compiler_params=params(),
        cost_estimate=SHORT,
        name="add_force",
    )(position, local, *own_inv, *got, geometry, dpack, scatter, mask, px, pz)


def finish_kernel(block, count, pos_ref, coef_ref, dpack_ref, px_ref, py_ref, filled_ref, *refs):
    del filled_ref
    y_refs, o_ref = refs[:count], refs[count]
    nodes = coef_ref.shape[1]
    me = pos_ref[1]
    dpack = dpack_ref[...]
    for c in range(block):
        y = slab(y_refs, c)
        slopes = dot(dpack, pack_field(y))
        moved = coef_ref[BXR] * slopes[:nodes] + coef_ref[BYS] * slopes[nodes:]
        change = y + TIME_STEP * (y * coef_ref[DYBY] - moved)
        store_own(o_ref, me, py_ref[c] + change, 1, c)
        store_own(o_ref, me, px_ref[c] + TIME_STEP * (y * coef_ref[DXBY]), 0, c)


def finish(position, y, coef, dpack, px, py, filled):
    coefs, part, elements = y[0].shape
    nodes = len(y) * part
    block = coef_block(coefs)
    field = pl.BlockSpec((block, part, elements), lambda i: (i, 0, 0))
    own = pl.BlockSpec((block, nodes, elements), lambda i: (i, 0, 0))
    return pl.pallas_call(
        functools.partial(finish_kernel, block, len(y)),
        out_shape=jax.ShapeDtypeStruct(filled.shape, F32),
        grid=(coefs // block,),
        in_specs=[
            SMEM_SPEC, whole(coef.shape), whole(dpack.shape), own, own,
            pl.BlockSpec(memory_space=pl.ANY), *[field] * len(y),
        ],
        out_specs=pl.BlockSpec((2, block, nodes, elements), lambda i: (0, i, 0, 0)),
        input_output_aliases={5: 0},
        compiler_params=params(),
        cost_estimate=SHORT,
        name="finish",
    )(position, coef, dpack, px, py, filled, *y)


def to_all(blocks):
    return lax.all_to_all(blocks, "four", split_axis=0, concat_axis=0, tiled=True)


def swap_faces(up, lo):
    peers = lax.axis_size("dom")
    up_way = [(i, (i + 1) % peers) for i in range(peers)]
    down_way = [(j, i) for i, j in up_way]
    return lax.ppermute(lo, "dom", down_way), lax.ppermute(up, "dom", up_way)


def tie(blocks, value):
    blocks = list(blocks)
    first = min(2, len(blocks) - 1)
    blocks[first], value = lax.optimization_barrier((blocks[first], value))
    return blocks, value


def per_device(
    adjoint, base_bank, snapshot, geometry, diff_r, diff_s, stiffness, upper_list, lower_list
):
    _, per, nodes, elements = adjoint.shape
    peers = lax.axis_size("four")
    lines = nodes // LINE
    direct = peers == lines
    place = lax.axis_index("four").astype(jnp.int32)
    position = jnp.stack([place, place if direct else jnp.zeros_like(place)])
    natural = jnp.asarray(coef_table(PLANES))
    table = permuted_table(position, natural, lines)
    flight = []

    def exchange(blocks):
        first = len(flight)
        order = sorted(range(1, peers), key=lambda d: (d < 2, d % 2, d))
        for d in order:
            block = blocks[d]
            if len(flight) >= IN_FLIGHT:
                block, flight[-IN_FLIGHT] = lax.optimization_barrier((block, flight[-IN_FLIGHT]))
            flight.append(lax.ppermute(block, "four", [(i, i ^ d) for i in range(peers)]))

        def received():
            got = {d: flight[first + k] for k, d in enumerate(order)}
            return [blocks[0]] + [got[d] for d in range(1, peers)]

        return received

    def columns(comp):
        if direct:
            return pack(position, adjoint, comp, LARGE_LIMIT if comp == 2 else VMEM_LIMIT)
        return [jnp.moveaxis(adjoint[comp].reshape(per, peers, nodes // peers, elements), 1, 0)]

    def spread(blocks):
        if direct:
            return exchange(blocks)
        got = [to_all(blocks[0]).reshape(PLANES, nodes // peers, elements)]
        return lambda: got

    def collect(blocks):
        if direct:
            return exchange(blocks)
        got = to_all(blocks[0].reshape(peers, per, nodes // peers, elements))
        got = jnp.moveaxis(got, 0, 1).reshape(per, lines, LINE, elements)
        return lambda: [got[:, d] for d in range(lines)]

    z_blocks = columns(2)
    z_columns = spread(z_blocks)
    x_blocks = columns(0)
    x_blocks, table = tie(x_blocks, table)
    x_columns = spread(x_blocks)
    constants = prepare(
        position, base_bank, snapshot, geometry, diff_r, diff_s, stiffness, upper_list, lower_list
    )
    z_coefs = transform(z_columns(), table)
    z_coefs, constants = tie(z_coefs, constants)
    coef, dpack, spack, gather, scatter, mask = constants
    z_later = collect(z_coefs)
    y_blocks = columns(1)
    x_coefs = transform(x_columns(), table)
    x_coefs, y_blocks = tie(x_coefs, y_blocks)
    x_later = collect(x_coefs)
    y_columns = spread(y_blocks)
    z = z_later()
    x = x_later()
    source, inverse, local, up, lo = start_solve(
        position, z, x, geometry, coef, dpack, spack, gather, mask
    )
    own_inv = (up, lo)
    got = swap_faces(up, lo)
    inv = got
    px, py, pz = partial_update(z, x, coef, dpack)
    local, up, lo = two_sweeps(
        2, local, source, inverse, (up, lo), own_inv, got, inv, spack, gather, scatter, mask
    )
    y_got = y_columns()
    y_got[0], local = lax.optimization_barrier((y_got[0], local))
    got = swap_faces(up, lo)
    y_later = collect(transform(y_got, table))
    local, up, lo = two_sweeps(
        1, local, source, inverse, (up, lo), own_inv, got, inv, spack, gather, scatter, mask
    )
    got = swap_faces(up, lo)
    filled, px = add_force(position, local, own_inv, got, geometry, dpack, scatter, mask, px, pz)
    return finish(position, y_later(), coef, dpack, px, py, filled)


def solution(mesh):
    in_specs = (
        P(None, "four", None, "dom"),
        P(None, None, None, "dom"),
        P("dom"),
        P(None, "dom"),
        P(),
        P(),
        P(),
        P("dom", None),
        P("dom", None),
    )
    out_specs = P(None, "four", None, "dom")
    return jax.shard_map(
        per_device, mesh=mesh, in_specs=in_specs, out_specs=out_specs, check_vma=False
    )
```

```python
import functools
import math

import jax
import jax.numpy as jnp
import ml_dtypes
import numpy as np
from jax import lax
from jax.experimental import pallas as pl
from jax.experimental.pallas import tpu as pltpu
from jax.sharding import PartitionSpec as P

PLANES = 256
PENALTY = 0.5
RELAXATION = 0.8
TIME_STEP = 0.2
INTERACTION = 2.0
LINE = 8
IN_FLIGHT = 5

F32 = jnp.float32
BF16 = jnp.bfloat16
VMEM_LIMIT = 20 * 1024 * 1024
LARGE_LIMIT = 55 * 1024 * 1024
SMEM_SPEC = pl.BlockSpec(memory_space=pltpu.SMEM)


def params(limit=VMEM_LIMIT):
    return pltpu.CompilerParams(vmem_limit_bytes=limit)


SHORT = pl.CostEstimate(flops=10**6, bytes_accessed=10**5, transcendentals=0)


def cost(flops, moved):
    return pl.CostEstimate(flops=int(flops), bytes_accessed=int(moved), transcendentals=0)


def split(x):
    high = x.astype(BF16)
    low = (x - high.astype(F32)).astype(BF16)
    return high, low


def dot(a, b):
    return lax.dot_general(a, b, (((1,), (0,)), ((), ())), preferred_element_type=F32)


def pack_matrix(m):
    high, low = split(m)
    return jnp.concatenate([high, low, high], axis=1)


def slab(refs, c):
    return jnp.concatenate([ref[c] for ref in refs], axis=0)


def pack_field(v):
    high, low = split(v)
    return jnp.concatenate([high, high, low], axis=0)


def coef_table(length):
    c = np.arange(length)[:, None]
    j = np.arange(length)[None, :]
    angle = ((c // 2) * j % length) * (2.0 * math.pi / length)
    table = np.where(c % 2 == 1, np.sin(angle), np.cos(angle)) * math.sqrt(2.0 / length)
    table[0] = 1.0 / math.sqrt(length)
    table[1] = np.where(np.arange(length) % 2 == 0, 1.0, -1.0) / math.sqrt(length)
    high = table.astype(ml_dtypes.bfloat16)
    low = (table - high.astype(np.float64)).astype(ml_dtypes.bfloat16)
    return np.concatenate([high, low], axis=0)


def permute_kernel(peers, pos_ref, table_ref, o_ref):
    planes = table_ref.shape[1]
    per = planes // peers
    me = pos_ref[1]
    row = lax.broadcasted_iota(jnp.int32, (planes, planes), 0)
    col = lax.broadcasted_iota(jnp.int32, (planes, planes), 1)
    swap = jnp.where(row == ((col // per) ^ me) * per + col % per, 1.0, 0.0).astype(BF16)
    for half in range(2):
        rows = pl.ds(half * planes, planes)
        turned = dot(swap, table_ref[rows, :]).astype(BF16)
        o_ref[rows, :] = dot(turned, swap).astype(BF16)


def permuted_table(position, table, peers):
    return pl.pallas_call(
        functools.partial(permute_kernel, peers),
        out_shape=jax.ShapeDtypeStruct(table.shape, BF16),
        in_specs=[SMEM_SPEC, pl.BlockSpec(memory_space=pltpu.VMEM)],
        compiler_params=params(),
        cost_estimate=cost(1e8, 4e6),
        name="permuted_table",
    )(position, table)


def transform_kernel(count, table_ref, *refs):
    planes = table_ref.shape[1]
    both = table_ref[...]
    high_table = both[:planes]
    width = refs[0].shape[-1]
    nodes = refs[0].shape[-2]
    per = planes // count
    flat = [ref.reshape(per * nodes, width) for ref in refs]
    for n in range(nodes):
        rows = pl.ds(n, per, stride=nodes) if nodes > 1 else pl.ds(0, per)
        high, low = split(jnp.concatenate([ref[rows, :] for ref in flat[:count]], axis=0))
        wide = dot(both, high)
        result = wide[:planes] + (wide[planes:] + dot(high_table, low))
        for d, ref in enumerate(flat[count:]):
            ref[rows, :] = result[d * per : (d + 1) * per]


def transform(blocks, table):
    per, nodes, elements = blocks[0].shape
    count = len(blocks)
    width = 128
    block = pl.BlockSpec((per, nodes, width), lambda i: (0, 0, i))
    size = count * blocks[0].size
    return pl.pallas_call(
        functools.partial(transform_kernel, count),
        out_shape=[jax.ShapeDtypeStruct(v.shape, F32) for v in blocks],
        grid=(elements // width,),
        in_specs=[pl.BlockSpec(table.shape, lambda i: (0, 0))] + [block] * count,
        out_specs=[block] * count,
        compiler_params=params(),
        cost_estimate=cost(6 * PLANES * size, 8 * size),
        name="transform",
    )(table, *blocks)


def pack_kernel(pos_ref, *refs):
    count = len(refs) // 2
    for source, target in zip(refs[:count], refs[count:]):
        target[...] = source[0]


def pack(position, adjoint, comp, limit):
    _, per, nodes, elements = adjoint.shape
    lines = nodes // LINE
    block = per // 2

    def source(d):
        return pl.BlockSpec((1, block, LINE, elements), lambda i, pos: (comp, i, pos[1] ^ d, 0))

    size = per * nodes * elements
    return pl.pallas_call(
        pack_kernel,
        out_shape=[jax.ShapeDtypeStruct((per, LINE, elements), F32)] * lines,
        grid_spec=pltpu.PrefetchScalarGridSpec(
            num_scalar_prefetch=1,
            grid=(per // block,),
            in_specs=[source(d) for d in range(lines)],
            out_specs=[pl.BlockSpec((block, LINE, elements), lambda i, pos: (i, 0, 0))] * lines,
        ),
        compiler_params=params(limit),
        cost_estimate=cost(0, 8 * size),
        name="pack",
    )(position, *[adjoint] * lines)


BXR, BYS, DXBX, DXBY, DYBX, DYBY, DIAG = range(7)


def line_of(me, d):
    return pl.ds(pl.multiple_of((me ^ d) * LINE, LINE), LINE)


def own_order(ref, me, *lead):
    lines = ref.shape[-2] // LINE
    return jnp.concatenate([ref[(*lead, line_of(me, d), slice(None))] for d in range(lines)], axis=0)


def prep_kernel(
    pos_ref, bank_ref, snap_ref, geo_ref, dr_ref, ds_ref, st_ref, up_ref, lo_ref,
    coef_ref, dpack_ref, spack_ref, gather_ref, scatter_ref, mask_ref, face_ref,
):
    elements = geo_ref.shape[1]
    nodes = dr_ref.shape[0]
    lines = nodes // LINE
    me = pos_ref[1]
    row = lax.broadcasted_iota(jnp.int32, (nodes, nodes), 0)
    col = lax.broadcasted_iota(jnp.int32, (nodes, nodes), 1)
    swap = jnp.where(row == ((col // LINE) ^ me) * LINE + col % LINE, 1.0, 0.0).astype(BF16)

    def permuted(ref):
        high, low = split(own_order(ref, me))
        return dot(high, swap) + dot(low, swap)

    snap = snap_ref[...]
    base = [
        sum(
            jnp.where(snap == k, own_order(bank_ref, me, k, i), 0.0)
            for k in range(bank_ref.shape[0])
        )
        for i in range(2)
    ]
    rx = geo_ref[0:1, :]
    sy = geo_ref[1:2, :]
    dpack = pack_matrix(jnp.concatenate([permuted(dr_ref), permuted(ds_ref)], axis=0))
    dpack_ref[...] = dpack
    bx = dot(dpack, pack_field(base[0]))
    by = dot(dpack, pack_field(base[1]))
    coef_ref[BXR] = base[0] * rx
    coef_ref[BYS] = base[1] * sy
    coef_ref[DXBX] = rx * bx[:nodes]
    coef_ref[DXBY] = rx * by[:nodes]
    coef_ref[DYBX] = sy * bx[nodes:]
    coef_ref[DYBY] = sy * by[nodes:]
    diag = jnp.sum(jnp.where(row == col, st_ref[...], 0.0), axis=0, keepdims=True)
    own = ((row // LINE) ^ me) * LINE + row % LINE == col
    diag = jnp.sum(jnp.where(own, diag, 0.0), axis=1, keepdims=True)
    spack_ref[...] = pack_matrix(jnp.where(row == col, 0.0, permuted(st_ref)))
    coef_ref[DIAG] = jnp.broadcast_to(diag, (nodes, elements))
    shared = up_ref.shape[1]
    mass = jnp.broadcast_to(1.0 / (rx * sy), (16, elements))
    for side, (ref, first) in enumerate(((up_ref, LINE - 1), (lo_ref, 0))):
        index = ref[...]
        node = index // elements
        element = index - node * elements
        hot = lax.broadcasted_iota(jnp.int32, (elements, shared), 0) == element
        hot = jnp.where(hot, 1.0, 0.0)
        gather_ref[side] = hot.astype(BF16)
        back = hot.T.astype(BF16)
        scatter_ref[side] = back
        mask = (lax.broadcasted_iota(jnp.int32, (lines, shared), 0) ^ me) == node // LINE
        mask = jnp.where(mask, 1.0, 0.0)
        mask_ref[side] = mask
        high, low = split(mass)
        rest = (mass - high.astype(F32) - low.astype(F32)).astype(BF16)
        at_face = sum(dot(part, gather_ref[side])[:1] for part in (high, low, rest))
        face_ref[side, 0:1, :] = at_face
        lead = jnp.concatenate([diag[s * LINE + first : s * LINE + first + 1] for s in range(lines)], axis=0)
        face_ref[side, 1:2, :] = PENALTY + jnp.sum(mask * lead, axis=0, keepdims=True)
        count = dot(mask.astype(BF16), back)
        for s in range(lines):
            n = s * LINE + first
            coef_ref[DIAG, n : n + 1, :] = coef_ref[DIAG, n : n + 1, :] + PENALTY * count[s : s + 1]


def prepare(position, base_bank, snapshot, geometry, diff_r, diff_s, stiffness, upper, lower):
    nodes = diff_r.shape[0]
    elements = geometry.shape[1]
    shared = upper.shape[1]
    return pl.pallas_call(
        prep_kernel,
        out_shape=[
            jax.ShapeDtypeStruct((7, nodes, elements), F32),
            jax.ShapeDtypeStruct((2 * nodes, 3 * nodes), BF16),
            jax.ShapeDtypeStruct((nodes, 3 * nodes), BF16),
            jax.ShapeDtypeStruct((2, elements, shared), BF16),
            jax.ShapeDtypeStruct((2, shared, elements), BF16),
            jax.ShapeDtypeStruct((2, nodes // LINE, shared), F32),
            jax.ShapeDtypeStruct((2, 2, shared), F32),
        ],
        in_specs=[SMEM_SPEC] + [pl.BlockSpec(memory_space=pltpu.VMEM)] * 8,
        compiler_params=params(),
        cost_estimate=cost(1e7, 8e6),
        name="prepare",
    )(position, base_bank, snapshot.reshape(1, elements), geometry, diff_r, diff_s, stiffness, upper, lower)


def face_of(ref, side):
    rows, elements = ref.shape
    return ref.reshape(rows // LINE, LINE, elements).at[:, LINE - 1 if side == 0 else 0, :]


def gather_faces(side, fields, gather_ref, mask_ref):
    lines = mask_ref.shape[1]
    high, low = split(jnp.concatenate(fields, axis=0))
    rows = high.shape[0]
    both = dot(jnp.concatenate([high, low], axis=0), gather_ref[side])
    picked = both[:rows] + both[rows:]
    shared = picked.shape[1]
    return jnp.sum(picked.reshape(rows // lines, lines, shared) * mask_ref[side][None], axis=1)


def scatter_faces(side, values, scatter_ref, mask_ref):
    mask = mask_ref[side]
    coefs, shared = values.shape
    spread = (values[:, None, :] * mask[None]).reshape(coefs * mask.shape[0], shared)
    high, low = split(spread)
    rows = high.shape[0]
    both = dot(jnp.concatenate([high, low], axis=0), scatter_ref[side])
    return both[:rows] + both[rows:]


def local_sweep(pot, source, inverse, spack):
    applied = dot(spack, pack_field(pot))
    return (1.0 - RELAXATION) * pot + inverse * (source - applied)


def coef_block(coefs):
    return 8 if coefs % 8 == 0 else coefs


def start_kernel(
    block, count, pos_ref, geo_ref, diag_ref, dpack_ref, spack_ref, gather_ref, mask_ref, *refs
):
    z_refs, x_refs = refs[:count], refs[count : 2 * count]
    source_ref, inverse_ref, local_ref, up_ref, lo_ref, pot_ref = refs[2 * count :]
    nodes, elements = diag_ref.shape[1:]
    beta = 4.0 / PLANES
    first = pos_ref[0] * (block * pl.num_programs(0)) + pl.program_id(0) * block
    rx = geo_ref[0:1, :]
    mass = 1.0 / (rx * geo_ref[1:2, :])
    diag = diag_ref[0]
    drpack = dpack_ref[:nodes]
    spack = spack_ref[...]
    for c in range(block):
        index = first + c
        wave = beta * (index // 2).astype(F32)
        shift = beta * jnp.where(index == 1, PLANES // 2, index // 2).astype(F32)
        shift = shift * shift
        z = slab(z_refs, c)
        other = slab(x_refs, c + 1 if c % 2 == 0 else c - 1)
        turned = (wave if c % 2 == 0 else -wave) * other
        source = turned - rx * dot(drpack, pack_field(z))
        inverse = RELAXATION / (diag + shift * mass)
        pot = inverse * source
        rows = pl.ds(c * nodes, nodes)
        source_ref[rows, :] = source
        inverse_ref[rows, :] = inverse
        pot_ref[rows, :] = pot
        local_ref[rows, :] = local_sweep(pot, source, inverse, spack)
    for side, out in ((0, up_ref), (1, lo_ref)):
        fields = [face_of(ref, side)[...] for ref in (pot_ref, local_ref)]
        picked = gather_faces(side, fields, gather_ref, mask_ref)
        for k in range(2):
            out[k] = picked[k * block : (k + 1) * block]


def whole(shape):
    return pl.BlockSpec(shape, lambda *i: (0,) * len(shape))


def start_solve(position, z, x, geometry, coef, dpack, spack, gather, mask):
    coefs, part, elements = z[0].shape
    nodes = len(z) * part
    shared = gather.shape[2]
    block = coef_block(coefs)
    field = [pl.BlockSpec((block, part, elements), lambda i: (i, 0, 0))] * len(z)
    flat = pl.BlockSpec((block * nodes, elements), lambda i: (i, 0))
    face = pl.BlockSpec((2, block, shared), lambda i: (0, i, 0))
    size = coefs * nodes * elements
    return pl.pallas_call(
        functools.partial(start_kernel, block, len(z)),
        out_shape=[jax.ShapeDtypeStruct((coefs * nodes, elements), F32)] * 3
        + [jax.ShapeDtypeStruct((2, coefs, shared), F32)] * 2,
        grid=(coefs // block,),
        in_specs=[
            SMEM_SPEC, whole(geometry.shape),
            pl.BlockSpec((1, nodes, elements), lambda i: (DIAG, 0, 0)),
            whole(dpack.shape), whole(spack.shape), whole(gather.shape), whole(mask.shape),
            *field, *field,
        ],
        out_specs=[flat, flat, flat, face, face],
        scratch_shapes=[pltpu.VMEM((block * nodes, elements), F32)],
        compiler_params=params(),
        cost_estimate=SHORT,
        name="start_solve",
    )(position, geometry, coef, dpack, spack, gather, mask, *z, *x)


def face_inverse(face, first, coefs):
    index = first + lax.broadcasted_iota(jnp.int32, (coefs, 1), 0)
    wave = jnp.where(index == 1, PLANES // 2, index // 2).astype(F32)
    shift = (4.0 / PLANES) * wave
    shift = shift * shift
    return RELAXATION / (face[1:2] + shift * face[0:1])


def sweeps_kernel(
    block, keep, pos_ref, local_ref, source_ref, inverse_ref, own_up_ref, own_lo_ref,
    got_up_ref, got_lo_ref, face_ref, far_up_ref, far_lo_ref, spack_ref, gather_ref, scatter_ref,
    mask_ref, next_ref, up_ref, lo_ref, pot_ref,
):
    nodes = spack_ref.shape[0]
    spack = spack_ref[...]
    lines = block * (nodes // LINE)
    first = pos_ref[0] * (block * pl.num_programs(0)) + pl.program_id(0) * block
    partners = []
    for side, own, got, far in ((0, own_up_ref, got_up_ref, far_up_ref), (1, own_lo_ref, got_lo_ref, far_lo_ref)):
        scale = PENALTY * face_inverse(face_ref[side], first, block)
        now = scale * got[0]
        later = scale * (got[1] + PENALTY * face_inverse(far[...], first, block) * own[0])
        both = scatter_faces(side, jnp.concatenate([now, later], axis=0), scatter_ref, mask_ref)
        partners.append((both[:lines], both[lines:]))
    pot_ref[...] = local_ref[...]
    for side in range(2):
        face = face_of(pot_ref, side)
        face[...] = face[...] + partners[side][0]
    for c in range(block):
        rows = pl.ds(c * nodes, nodes)
        pot_ref[rows, :] = local_sweep(pot_ref[rows, :], source_ref[rows, :], inverse_ref[rows, :], spack)
    for side in range(2):
        face = face_of(pot_ref, side)
        face[...] = face[...] + partners[side][1]
    for c in range(block):
        rows = pl.ds(c * nodes, nodes)
        next_ref[rows, :] = local_sweep(pot_ref[rows, :], source_ref[rows, :], inverse_ref[rows, :], spack)
    for side, out in ((0, up_ref), (1, lo_ref)):
        fields = [face_of(ref, side)[...] for ref in (pot_ref, next_ref)[:keep]]
        picked = gather_faces(side, fields, gather_ref, mask_ref)
        for k in range(keep):
            out[k] = picked[k * block : (k + 1) * block]


def two_sweeps(keep, position, local, source, inverse, own, got, face, far, spack, gather, scatter, mask):
    nodes = spack.shape[0]
    elements = local.shape[1]
    coefs = local.shape[0] // nodes
    shared = gather.shape[2]
    block = coef_block(coefs)
    flat = pl.BlockSpec((block * nodes, elements), lambda i: (i, 0))
    one = pl.BlockSpec((1, block, shared), lambda i: (0, i, 0))
    two = pl.BlockSpec((2, block, shared), lambda i: (0, i, 0))
    kept = pl.BlockSpec((keep, block, shared), lambda i: (0, i, 0))
    size = coefs * nodes * elements
    return pl.pallas_call(
        functools.partial(sweeps_kernel, block, keep),
        out_shape=[jax.ShapeDtypeStruct(local.shape, F32)]
        + [jax.ShapeDtypeStruct((keep, coefs, shared), F32)] * 2,
        grid=(coefs // block,),
        in_specs=[
            SMEM_SPEC, flat, flat, flat, one, one, two, two,
            whole(face.shape), whole(far[0].shape), whole(far[1].shape),
            whole(spack.shape), whole(gather.shape), whole(scatter.shape), whole(mask.shape),
        ],
        out_specs=[flat, kept, kept],
        scratch_shapes=[pltpu.VMEM((block * nodes, elements), F32)],
        compiler_params=params(),
        cost_estimate=SHORT,
        name="two_sweeps",
    )(position, local, source, inverse, *own, *got, face, *far, spack, gather, scatter, mask)


def store_own(ref, me, value, *lead):
    for d in range(value.shape[0] // LINE):
        ref[(*lead, line_of(me, d), slice(None))] = value[d * LINE : (d + 1) * LINE]


def partial_kernel(block, count, coef_ref, dpack_ref, *refs):
    z_refs, x_refs = refs[:count], refs[count : 2 * count]
    px_ref, py_ref, pz_ref = refs[2 * count :]
    nodes = coef_ref.shape[1]
    dpack = dpack_ref[...]
    for c in range(block):
        z = slab(z_refs, c)
        slopes = dot(dpack, pack_field(z))
        moved = coef_ref[BXR] * slopes[:nodes] + coef_ref[BYS] * slopes[nodes:]
        pz_ref[c] = z - TIME_STEP * (moved + INTERACTION * z)
        x = slab(x_refs, c)
        slopes = dot(dpack, pack_field(x))
        moved = coef_ref[BXR] * slopes[:nodes] + coef_ref[BYS] * slopes[nodes:]
        px_ref[c] = x + TIME_STEP * (x * coef_ref[DXBX] - moved - INTERACTION * x)
        py_ref[c] = TIME_STEP * (x * coef_ref[DYBX])


def partial_update(z, x, coef, dpack):
    coefs, part, elements = z[0].shape
    nodes = len(z) * part
    block = coef_block(coefs)
    field = [pl.BlockSpec((block, part, elements), lambda i: (i, 0, 0))] * len(z)
    out = pl.BlockSpec((block, nodes, elements), lambda i: (i, 0, 0))
    return pl.pallas_call(
        functools.partial(partial_kernel, block, len(z)),
        out_shape=[jax.ShapeDtypeStruct((coefs, nodes, elements), F32)] * 3,
        grid=(coefs // block,),
        in_specs=[whole(coef.shape), whole(dpack.shape), *field, *field],
        out_specs=[out] * 3,
        compiler_params=params(),
        cost_estimate=SHORT,
        name="partial_update",
    )(coef, dpack, *z, *x)


def force_kernel(
    block, pos_ref, local_ref, got_up_ref, got_lo_ref, face_ref, geo_ref, dpack_ref,
    scatter_ref, mask_ref, px_ref, pz_ref, o_ref, x_ref, pot_ref,
):
    nodes = dpack_ref.shape[0] // 2
    scale = TIME_STEP * INTERACTION
    me = pos_ref[1]
    pot_ref[...] = local_ref[...]
    first = pos_ref[0] * (block * pl.num_programs(0)) + pl.program_id(0) * block
    for side, got in ((0, got_up_ref), (1, got_lo_ref)):
        face = face_of(pot_ref, side)
        partner = PENALTY * face_inverse(face_ref[side], first, block) * got[0]
        face[...] = face[...] + scatter_faces(side, partner, scatter_ref, mask_ref)
    drpack = dpack_ref[:nodes]
    slope_scale = scale * geo_ref[0:1, :]
    for c in range(block):
        pot = pot_ref[pl.ds(c * nodes, nodes), :]
        slope = dot(drpack, pack_field(pot))
        store_own(o_ref, me, pz_ref[c] - slope_scale * slope, 0, c)
        wave = (4.0 / PLANES) * ((first + c) // 2).astype(F32)
        factor = scale * (wave if c % 2 else -wave)
        other = c - 1 if c % 2 else c + 1
        x_ref[other] = px_ref[other] + factor * pot


def add_force(position, local, got, face, geometry, dpack, scatter, mask, px, pz):
    coefs, nodes, elements = px.shape
    shared = scatter.shape[1]
    block = coef_block(coefs)
    flat = pl.BlockSpec((block * nodes, elements), lambda i: (i, 0))
    one = pl.BlockSpec((1, block, shared), lambda i: (0, i, 0))
    part = pl.BlockSpec((block, nodes, elements), lambda i: (i, 0, 0))
    return pl.pallas_call(
        functools.partial(force_kernel, block),
        out_shape=[
            jax.ShapeDtypeStruct((3, coefs, nodes, elements), F32),
            jax.ShapeDtypeStruct(px.shape, F32),
        ],
        grid=(coefs // block,),
        in_specs=[
            SMEM_SPEC, flat, one, one, whole(face.shape), whole(geometry.shape), whole(dpack.shape),
            whole(scatter.shape), whole(mask.shape), part, part,
        ],
        out_specs=[pl.BlockSpec((1, block, nodes, elements), lambda i: (2, i, 0, 0)), part],
        scratch_shapes=[pltpu.VMEM((block * nodes, elements), F32)],
        compiler_params=params(),
        cost_estimate=SHORT,
        name="add_force",
    )(position, local, *got, face, geometry, dpack, scatter, mask, px, pz)


def finish_kernel(block, count, pos_ref, coef_ref, dpack_ref, px_ref, py_ref, filled_ref, *refs):
    del filled_ref
    y_refs, o_ref = refs[:count], refs[count]
    nodes = coef_ref.shape[1]
    me = pos_ref[1]
    dpack = dpack_ref[...]
    for c in range(block):
        y = slab(y_refs, c)
        slopes = dot(dpack, pack_field(y))
        moved = coef_ref[BXR] * slopes[:nodes] + coef_ref[BYS] * slopes[nodes:]
        change = y + TIME_STEP * (y * coef_ref[DYBY] - moved)
        store_own(o_ref, me, py_ref[c] + change, 1, c)
        store_own(o_ref, me, px_ref[c] + TIME_STEP * (y * coef_ref[DXBY]), 0, c)


def finish(position, y, coef, dpack, px, py, filled):
    coefs, part, elements = y[0].shape
    nodes = len(y) * part
    block = coef_block(coefs)
    field = pl.BlockSpec((block, part, elements), lambda i: (i, 0, 0))
    own = pl.BlockSpec((block, nodes, elements), lambda i: (i, 0, 0))
    return pl.pallas_call(
        functools.partial(finish_kernel, block, len(y)),
        out_shape=jax.ShapeDtypeStruct(filled.shape, F32),
        grid=(coefs // block,),
        in_specs=[
            SMEM_SPEC, whole(coef.shape), whole(dpack.shape), own, own,
            pl.BlockSpec(memory_space=pl.ANY), *[field] * len(y),
        ],
        out_specs=pl.BlockSpec((2, block, nodes, elements), lambda i: (0, i, 0, 0)),
        input_output_aliases={5: 0},
        compiler_params=params(),
        cost_estimate=SHORT,
        name="finish",
    )(position, coef, dpack, px, py, filled, *y)


def to_all(blocks):
    return lax.all_to_all(blocks, "four", split_axis=0, concat_axis=0, tiled=True)


def swap_faces(up, lo):
    peers = lax.axis_size("dom")
    up_way = [(i, (i + 1) % peers) for i in range(peers)]
    down_way = [(j, i) for i, j in up_way]
    return lax.ppermute(lo, "dom", down_way), lax.ppermute(up, "dom", up_way)


def tie(blocks, value):
    blocks = list(blocks)
    first = min(2, len(blocks) - 1)
    blocks[first], value = lax.optimization_barrier((blocks[first], value))
    return blocks, value


def per_device(
    adjoint, base_bank, snapshot, geometry, diff_r, diff_s, stiffness, upper_list, lower_list
):
    _, per, nodes, elements = adjoint.shape
    peers = lax.axis_size("four")
    lines = nodes // LINE
    direct = peers == lines
    place = lax.axis_index("four").astype(jnp.int32)
    position = jnp.stack([place, place if direct else jnp.zeros_like(place)])
    natural = jnp.asarray(coef_table(PLANES))
    table = permuted_table(position, natural, lines)
    flight = []

    def exchange(blocks):
        first = len(flight)
        order = sorted(range(1, peers), key=lambda d: (d < 2, d % 2, d))
        for d in order:
            block = blocks[d]
            if len(flight) >= IN_FLIGHT:
                block, flight[-IN_FLIGHT] = lax.optimization_barrier((block, flight[-IN_FLIGHT]))
            flight.append(lax.ppermute(block, "four", [(i, i ^ d) for i in range(peers)]))

        def received():
            got = {d: flight[first + k] for k, d in enumerate(order)}
            return [blocks[0]] + [got[d] for d in range(1, peers)]

        return received

    def columns(comp):
        if direct:
            return pack(position, adjoint, comp, LARGE_LIMIT if comp == 2 else VMEM_LIMIT)
        return [jnp.moveaxis(adjoint[comp].reshape(per, peers, nodes // peers, elements), 1, 0)]

    def spread(blocks):
        if direct:
            return exchange(blocks)
        got = [to_all(blocks[0]).reshape(PLANES, nodes // peers, elements)]
        return lambda: got

    def collect(blocks):
        if direct:
            return exchange(blocks)
        got = to_all(blocks[0].reshape(peers, per, nodes // peers, elements))
        got = jnp.moveaxis(got, 0, 1).reshape(per, lines, LINE, elements)
        return lambda: [got[:, d] for d in range(lines)]

    z_blocks = columns(2)
    z_columns = spread(z_blocks)
    x_blocks = columns(0)
    x_blocks, table = tie(x_blocks, table)
    x_columns = spread(x_blocks)
    constants = prepare(
        position, base_bank, snapshot, geometry, diff_r, diff_s, stiffness, upper_list, lower_list
    )
    z_coefs = transform(z_columns(), table)
    z_coefs, constants = tie(z_coefs, constants)
    coef, dpack, spack, gather, scatter, mask, face = constants
    far = swap_faces(face[0], face[1])
    z_later = collect(z_coefs)
    y_blocks = columns(1)
    x_coefs = transform(x_columns(), table)
    x_coefs, (y_blocks, far) = tie(x_coefs, (y_blocks, far))
    x_later = collect(x_coefs)
    y_columns = spread(y_blocks)
    z = z_later()
    x = x_later()
    source, inverse, local, up, lo = start_solve(
        position, z, x, geometry, coef, dpack, spack, gather, mask
    )
    got = swap_faces(up, lo)
    parts = partial_update(z, x, coef, dpack)
    local, (px, py, pz) = lax.optimization_barrier((local, parts))
    local, up, lo = two_sweeps(
        2, position, local, source, inverse, (up, lo), got, face, far, spack, gather, scatter, mask
    )
    y_got = y_columns()
    y_got[0], local = lax.optimization_barrier((y_got[0], local))
    got = swap_faces(up, lo)
    begun = len(flight)
    y_later = collect(transform(y_got, table))

    def after(value, first, last):
        here = slice(begun + first, begun + last)
        value, flight[here] = lax.optimization_barrier((value, flight[here]))
        return value

    local = after(local, 0, 2)
    local, up, lo = two_sweeps(
        1, position, local, source, inverse, (up, lo), got, face, far, spack, gather, scatter, mask
    )
    up, lo = after((up, lo), 2, 4)
    got = swap_faces(up, lo)
    local = after(local, 4, 5)
    filled, px = add_force(position, local, got, face, geometry, dpack, scatter, mask, px, pz)
    return finish(position, y_later(), coef, dpack, px, py, filled)


def solution(mesh):
    in_specs = (
        P(None, "four", None, "dom"),
        P(None, None, None, "dom"),
        P("dom"),
        P(None, "dom"),
        P(),
        P(),
        P(),
        P("dom", None),
        P("dom", None),
    )
    out_specs = P(None, "four", None, "dom")
    return jax.shard_map(
        per_device, mesh=mesh, in_specs=in_specs, out_specs=out_specs, check_vma=False
    )
```

```python
import functools
import math

import jax
import jax.numpy as jnp
import ml_dtypes
import numpy as np
from jax import lax
from jax.experimental import pallas as pl
from jax.experimental.pallas import tpu as pltpu
from jax.sharding import PartitionSpec as P

PLANES = 256
PENALTY = 0.5
RELAXATION = 0.8
TIME_STEP = 0.2
INTERACTION = 2.0
LINE = 8
IN_FLIGHT = 5

F32 = jnp.float32
BF16 = jnp.bfloat16
VMEM_LIMIT = 20 * 1024 * 1024
LARGE_LIMIT = 48 * 1024 * 1024
SMEM_SPEC = pl.BlockSpec(memory_space=pltpu.SMEM)


def params(limit=VMEM_LIMIT):
    return pltpu.CompilerParams(vmem_limit_bytes=limit)


SHORT = pl.CostEstimate(flops=10**6, bytes_accessed=10**5, transcendentals=0)


def cost(flops, moved):
    return pl.CostEstimate(flops=int(flops), bytes_accessed=int(moved), transcendentals=0)


def split(x):
    high = x.astype(BF16)
    low = (x - high.astype(F32)).astype(BF16)
    return high, low


def dot(a, b):
    return lax.dot_general(a, b, (((1,), (0,)), ((), ())), preferred_element_type=F32)


def pack_matrix(m):
    high, low = split(m)
    return jnp.concatenate([high, low, high], axis=1)


def slab(refs, c):
    return jnp.concatenate([ref[c] for ref in refs], axis=0)


def pack_field(v):
    high, low = split(v)
    return jnp.concatenate([high, high, low], axis=0)


def coef_table(length):
    c = np.arange(length)[:, None]
    j = np.arange(length)[None, :]
    angle = ((c // 2) * j % length) * (2.0 * math.pi / length)
    table = np.where(c % 2 == 1, np.sin(angle), np.cos(angle)) * math.sqrt(2.0 / length)
    table[0] = 1.0 / math.sqrt(length)
    table[1] = np.where(np.arange(length) % 2 == 0, 1.0, -1.0) / math.sqrt(length)
    high = table.astype(ml_dtypes.bfloat16)
    low = (table - high.astype(np.float64)).astype(ml_dtypes.bfloat16)
    return np.concatenate([high, low], axis=0)


def permute_kernel(peers, pos_ref, table_ref, o_ref):
    planes = table_ref.shape[1]
    per = planes // peers
    me = pos_ref[1]
    row = lax.broadcasted_iota(jnp.int32, (planes, planes), 0)
    col = lax.broadcasted_iota(jnp.int32, (planes, planes), 1)
    swap = jnp.where(row == ((col // per) ^ me) * per + col % per, 1.0, 0.0).astype(BF16)
    for half in range(2):
        rows = pl.ds(half * planes, planes)
        turned = dot(swap, table_ref[rows, :]).astype(BF16)
        o_ref[rows, :] = dot(turned, swap).astype(BF16)


def permuted_table(position, table, peers):
    return pl.pallas_call(
        functools.partial(permute_kernel, peers),
        out_shape=jax.ShapeDtypeStruct(table.shape, BF16),
        in_specs=[SMEM_SPEC, pl.BlockSpec(memory_space=pltpu.VMEM)],
        compiler_params=params(),
        cost_estimate=cost(1e8, 4e6),
        name="permuted_table",
    )(position, table)


def transform_kernel(count, table_ref, *refs):
    planes = table_ref.shape[1]
    both = table_ref[...]
    high_table = both[:planes]
    width = refs[0].shape[-1]
    nodes = refs[0].shape[-2]
    per = planes // count
    flat = [ref.reshape(per * nodes, width) for ref in refs]
    for n in range(nodes):
        rows = pl.ds(n, per, stride=nodes) if nodes > 1 else pl.ds(0, per)
        high, low = split(jnp.concatenate([ref[rows, :] for ref in flat[:count]], axis=0))
        wide = dot(both, high)
        result = wide[:planes] + (wide[planes:] + dot(high_table, low))
        for d, ref in enumerate(flat[count:]):
            ref[rows, :] = result[d * per : (d + 1) * per]


def transform(blocks, table):
    per, nodes, elements = blocks[0].shape
    count = len(blocks)
    width = 128
    block = pl.BlockSpec((per, nodes, width), lambda i: (0, 0, i))
    size = count * blocks[0].size
    return pl.pallas_call(
        functools.partial(transform_kernel, count),
        out_shape=[jax.ShapeDtypeStruct(v.shape, F32) for v in blocks],
        grid=(elements // width,),
        in_specs=[pl.BlockSpec(table.shape, lambda i: (0, 0))] + [block] * count,
        out_specs=[block] * count,
        compiler_params=params(),
        cost_estimate=cost(6 * PLANES * size, 8 * size),
        name="transform",
    )(table, *blocks)


def pack_kernel(pos_ref, *refs):
    count = len(refs) // 2
    for source, target in zip(refs[:count], refs[count:]):
        target[...] = source[0]


def pack(position, adjoint, comp, limit):
    _, per, nodes, elements = adjoint.shape
    lines = nodes // LINE
    block = per // 2

    def source(d):
        return pl.BlockSpec((1, block, LINE, elements), lambda i, pos: (comp, i, pos[1] ^ d, 0))

    size = per * nodes * elements
    return pl.pallas_call(
        pack_kernel,
        out_shape=[jax.ShapeDtypeStruct((per, LINE, elements), F32)] * lines,
        grid_spec=pltpu.PrefetchScalarGridSpec(
            num_scalar_prefetch=1,
            grid=(per // block,),
            in_specs=[source(d) for d in range(lines)],
            out_specs=[pl.BlockSpec((block, LINE, elements), lambda i, pos: (i, 0, 0))] * lines,
        ),
        compiler_params=params(limit),
        cost_estimate=cost(0, 8 * size),
        name="pack",
    )(position, *[adjoint] * lines)


BXR, BYS, DXBX, DXBY, DYBX, DYBY, DIAG = range(7)


def line_of(me, d):
    return pl.ds(pl.multiple_of((me ^ d) * LINE, LINE), LINE)


def own_order(ref, me, *lead):
    lines = ref.shape[-2] // LINE
    return jnp.concatenate([ref[(*lead, line_of(me, d), slice(None))] for d in range(lines)], axis=0)


def prep_kernel(
    pos_ref, bank_ref, snap_ref, geo_ref, dr_ref, ds_ref, st_ref, up_ref, lo_ref,
    coef_ref, dpack_ref, spack_ref, gather_ref, scatter_ref, mask_ref, face_ref,
):
    elements = geo_ref.shape[1]
    nodes = dr_ref.shape[0]
    lines = nodes // LINE
    me = pos_ref[1]
    row = lax.broadcasted_iota(jnp.int32, (nodes, nodes), 0)
    col = lax.broadcasted_iota(jnp.int32, (nodes, nodes), 1)
    swap = jnp.where(row == ((col // LINE) ^ me) * LINE + col % LINE, 1.0, 0.0).astype(BF16)

    def permuted(ref):
        high, low = split(own_order(ref, me))
        return dot(high, swap) + dot(low, swap)

    snap = snap_ref[...]
    base = [
        sum(
            jnp.where(snap == k, own_order(bank_ref, me, k, i), 0.0)
            for k in range(bank_ref.shape[0])
        )
        for i in range(2)
    ]
    rx = geo_ref[0:1, :]
    sy = geo_ref[1:2, :]
    dpack = pack_matrix(jnp.concatenate([permuted(dr_ref), permuted(ds_ref)], axis=0))
    dpack_ref[...] = dpack
    bx = dot(dpack, pack_field(base[0]))
    by = dot(dpack, pack_field(base[1]))
    coef_ref[BXR] = base[0] * rx
    coef_ref[BYS] = base[1] * sy
    coef_ref[DXBX] = rx * bx[:nodes]
    coef_ref[DXBY] = rx * by[:nodes]
    coef_ref[DYBX] = sy * bx[nodes:]
    coef_ref[DYBY] = sy * by[nodes:]
    diag = jnp.sum(jnp.where(row == col, st_ref[...], 0.0), axis=0, keepdims=True)
    own = ((row // LINE) ^ me) * LINE + row % LINE == col
    diag = jnp.sum(jnp.where(own, diag, 0.0), axis=1, keepdims=True)
    spack_ref[...] = pack_matrix(jnp.where(row == col, 0.0, permuted(st_ref)))
    coef_ref[DIAG] = jnp.broadcast_to(diag, (nodes, elements))
    shared = up_ref.shape[1]
    mass = jnp.broadcast_to(1.0 / (rx * sy), (16, elements))
    for side, (ref, first) in enumerate(((up_ref, LINE - 1), (lo_ref, 0))):
        index = ref[...]
        node = index // elements
        element = index - node * elements
        hot = lax.broadcasted_iota(jnp.int32, (elements, shared), 0) == element
        hot = jnp.where(hot, 1.0, 0.0)
        gather_ref[side] = hot.astype(BF16)
        back = hot.T.astype(BF16)
        scatter_ref[side] = back
        mask = (lax.broadcasted_iota(jnp.int32, (lines, shared), 0) ^ me) == node // LINE
        mask = jnp.where(mask, 1.0, 0.0)
        mask_ref[side] = mask
        high, low = split(mass)
        rest = (mass - high.astype(F32) - low.astype(F32)).astype(BF16)
        at_face = sum(dot(part, gather_ref[side])[:1] for part in (high, low, rest))
        face_ref[side, 0:1, :] = at_face
        lead = jnp.concatenate([diag[s * LINE + first : s * LINE + first + 1] for s in range(lines)], axis=0)
        face_ref[side, 1:2, :] = PENALTY + jnp.sum(mask * lead, axis=0, keepdims=True)
        count = dot(mask.astype(BF16), back)
        for s in range(lines):
            n = s * LINE + first
            coef_ref[DIAG, n : n + 1, :] = coef_ref[DIAG, n : n + 1, :] + PENALTY * count[s : s + 1]


def prepare(position, base_bank, snapshot, geometry, diff_r, diff_s, stiffness, upper, lower):
    nodes = diff_r.shape[0]
    elements = geometry.shape[1]
    shared = upper.shape[1]
    return pl.pallas_call(
        prep_kernel,
        out_shape=[
            jax.ShapeDtypeStruct((7, nodes, elements), F32),
            jax.ShapeDtypeStruct((2 * nodes, 3 * nodes), BF16),
            jax.ShapeDtypeStruct((nodes, 3 * nodes), BF16),
            jax.ShapeDtypeStruct((2, elements, shared), BF16),
            jax.ShapeDtypeStruct((2, shared, elements), BF16),
            jax.ShapeDtypeStruct((2, nodes // LINE, shared), F32),
            jax.ShapeDtypeStruct((2, 2, shared), F32),
        ],
        in_specs=[SMEM_SPEC] + [pl.BlockSpec(memory_space=pltpu.VMEM)] * 8,
        compiler_params=params(),
        cost_estimate=cost(1e7, 8e6),
        name="prepare",
    )(position, base_bank, snapshot.reshape(1, elements), geometry, diff_r, diff_s, stiffness, upper, lower)


def face_of(ref, side):
    rows, elements = ref.shape
    return ref.reshape(rows // LINE, LINE, elements).at[:, LINE - 1 if side == 0 else 0, :]


def gather_faces(side, fields, gather_ref, mask_ref):
    lines = mask_ref.shape[1]
    high, low = split(jnp.concatenate(fields, axis=0))
    rows = high.shape[0]
    both = dot(jnp.concatenate([high, low], axis=0), gather_ref[side])
    picked = both[:rows] + both[rows:]
    shared = picked.shape[1]
    return jnp.sum(picked.reshape(rows // lines, lines, shared) * mask_ref[side][None], axis=1)


def scatter_faces(side, values, scatter_ref, mask_ref):
    mask = mask_ref[side]
    coefs, shared = values.shape
    spread = (values[:, None, :] * mask[None]).reshape(coefs * mask.shape[0], shared)
    high, low = split(spread)
    rows = high.shape[0]
    both = dot(jnp.concatenate([high, low], axis=0), scatter_ref[side])
    return both[:rows] + both[rows:]


def local_sweep(pot, source, inverse, spack):
    applied = dot(spack, pack_field(pot))
    return (1.0 - RELAXATION) * pot + inverse * (source - applied)


def coef_block(coefs):
    return 8 if coefs % 8 == 0 else coefs


def start_kernel(
    block, count, pos_ref, geo_ref, diag_ref, dpack_ref, spack_ref, gather_ref, mask_ref, *refs
):
    z_refs, x_refs = refs[:count], refs[count : 2 * count]
    source_ref, inverse_ref, local_ref, up_ref, lo_ref, pot_ref = refs[2 * count :]
    nodes, elements = diag_ref.shape[1:]
    beta = 4.0 / PLANES
    first = pos_ref[0] * (block * pl.num_programs(0)) + pl.program_id(0) * block
    rx = geo_ref[0:1, :]
    mass = 1.0 / (rx * geo_ref[1:2, :])
    diag = diag_ref[0]
    drpack = dpack_ref[:nodes]
    spack = spack_ref[...]
    for c in range(block):
        index = first + c
        wave = beta * (index // 2).astype(F32)
        shift = beta * jnp.where(index == 1, PLANES // 2, index // 2).astype(F32)
        shift = shift * shift
        z = slab(z_refs, c)
        other = slab(x_refs, c + 1 if c % 2 == 0 else c - 1)
        turned = (wave if c % 2 == 0 else -wave) * other
        source = turned - rx * dot(drpack, pack_field(z))
        inverse = RELAXATION / (diag + shift * mass)
        pot = inverse * source
        rows = pl.ds(c * nodes, nodes)
        source_ref[rows, :] = source
        inverse_ref[rows, :] = inverse
        pot_ref[rows, :] = pot
        local_ref[rows, :] = local_sweep(pot, source, inverse, spack)
    for side, out in ((0, up_ref), (1, lo_ref)):
        fields = [face_of(ref, side)[...] for ref in (pot_ref, local_ref)]
        picked = gather_faces(side, fields, gather_ref, mask_ref)
        for k in range(2):
            out[k] = picked[k * block : (k + 1) * block]


def whole(shape):
    return pl.BlockSpec(shape, lambda *i: (0,) * len(shape))


def start_solve(position, z, x, geometry, coef, dpack, spack, gather, mask):
    coefs, part, elements = z[0].shape
    nodes = len(z) * part
    shared = gather.shape[2]
    block = coef_block(coefs)
    field = [pl.BlockSpec((block, part, elements), lambda i: (i, 0, 0))] * len(z)
    flat = pl.BlockSpec((block * nodes, elements), lambda i: (i, 0))
    face = pl.BlockSpec((2, block, shared), lambda i: (0, i, 0))
    size = coefs * nodes * elements
    return pl.pallas_call(
        functools.partial(start_kernel, block, len(z)),
        out_shape=[jax.ShapeDtypeStruct((coefs * nodes, elements), F32)] * 3
        + [jax.ShapeDtypeStruct((2, coefs, shared), F32)] * 2,
        grid=(coefs // block,),
        in_specs=[
            SMEM_SPEC, whole(geometry.shape),
            pl.BlockSpec((1, nodes, elements), lambda i: (DIAG, 0, 0)),
            whole(dpack.shape), whole(spack.shape), whole(gather.shape), whole(mask.shape),
            *field, *field,
        ],
        out_specs=[flat, flat, flat, face, face],
        scratch_shapes=[pltpu.VMEM((block * nodes, elements), F32)],
        compiler_params=params(),
        cost_estimate=SHORT,
        name="start_solve",
    )(position, geometry, coef, dpack, spack, gather, mask, *z, *x)


def face_inverse(face, first, coefs):
    index = first + lax.broadcasted_iota(jnp.int32, (coefs, 1), 0)
    wave = jnp.where(index == 1, PLANES // 2, index // 2).astype(F32)
    shift = (4.0 / PLANES) * wave
    shift = shift * shift
    return RELAXATION / (face[1:2] + shift * face[0:1])


def sweeps_kernel(
    block, keep, pos_ref, local_ref, source_ref, inverse_ref, own_up_ref, own_lo_ref,
    got_up_ref, got_lo_ref, face_ref, far_up_ref, far_lo_ref, spack_ref, gather_ref, scatter_ref,
    mask_ref, next_ref, up_ref, lo_ref, pot_ref,
):
    nodes = spack_ref.shape[0]
    spack = spack_ref[...]
    lines = block * (nodes // LINE)
    first = pos_ref[0] * (block * pl.num_programs(0)) + pl.program_id(0) * block
    partners = []
    for side, own, got, far in ((0, own_up_ref, got_up_ref, far_up_ref), (1, own_lo_ref, got_lo_ref, far_lo_ref)):
        scale = PENALTY * face_inverse(face_ref[side], first, block)
        now = scale * got[0]
        later = scale * (got[1] + PENALTY * face_inverse(far[...], first, block) * own[0])
        both = scatter_faces(side, jnp.concatenate([now, later], axis=0), scatter_ref, mask_ref)
        partners.append((both[:lines], both[lines:]))
    pot_ref[...] = local_ref[...]
    for side in range(2):
        face = face_of(pot_ref, side)
        face[...] = face[...] + partners[side][0]
    for c in range(block):
        rows = pl.ds(c * nodes, nodes)
        pot_ref[rows, :] = local_sweep(pot_ref[rows, :], source_ref[rows, :], inverse_ref[rows, :], spack)
    for side in range(2):
        face = face_of(pot_ref, side)
        face[...] = face[...] + partners[side][1]
    for c in range(block):
        rows = pl.ds(c * nodes, nodes)
        next_ref[rows, :] = local_sweep(pot_ref[rows, :], source_ref[rows, :], inverse_ref[rows, :], spack)
    for side, out in ((0, up_ref), (1, lo_ref)):
        fields = [face_of(ref, side)[...] for ref in (pot_ref, next_ref)[:keep]]
        picked = gather_faces(side, fields, gather_ref, mask_ref)
        for k in range(keep):
            out[k] = picked[k * block : (k + 1) * block]


def two_sweeps(keep, position, local, source, inverse, own, got, face, far, spack, gather, scatter, mask):
    nodes = spack.shape[0]
    elements = local.shape[1]
    coefs = local.shape[0] // nodes
    shared = gather.shape[2]
    block = coef_block(coefs)
    flat = pl.BlockSpec((block * nodes, elements), lambda i: (i, 0))
    one = pl.BlockSpec((1, block, shared), lambda i: (0, i, 0))
    two = pl.BlockSpec((2, block, shared), lambda i: (0, i, 0))
    kept = pl.BlockSpec((keep, block, shared), lambda i: (0, i, 0))
    size = coefs * nodes * elements
    return pl.pallas_call(
        functools.partial(sweeps_kernel, block, keep),
        out_shape=[jax.ShapeDtypeStruct(local.shape, F32)]
        + [jax.ShapeDtypeStruct((keep, coefs, shared), F32)] * 2,
        grid=(coefs // block,),
        in_specs=[
            SMEM_SPEC, flat, flat, flat, one, one, two, two,
            whole(face.shape), whole(far[0].shape), whole(far[1].shape),
            whole(spack.shape), whole(gather.shape), whole(scatter.shape), whole(mask.shape),
        ],
        out_specs=[flat, kept, kept],
        scratch_shapes=[pltpu.VMEM((block * nodes, elements), F32)],
        compiler_params=params(),
        cost_estimate=SHORT,
        name="two_sweeps",
    )(position, local, source, inverse, *own, *got, face, *far, spack, gather, scatter, mask)


def store_own(ref, me, value, *lead):
    for d in range(value.shape[0] // LINE):
        ref[(*lead, line_of(me, d), slice(None))] = value[d * LINE : (d + 1) * LINE]


def partial_kernel(block, count, coef_ref, dpack_ref, *refs):
    z_refs, x_refs = refs[:count], refs[count : 2 * count]
    px_ref, py_ref, pz_ref = refs[2 * count :]
    nodes = coef_ref.shape[1]
    dpack = dpack_ref[...]
    for c in range(block):
        z = slab(z_refs, c)
        slopes = dot(dpack, pack_field(z))
        moved = coef_ref[BXR] * slopes[:nodes] + coef_ref[BYS] * slopes[nodes:]
        pz_ref[c] = z - TIME_STEP * (moved + INTERACTION * z)
        x = slab(x_refs, c)
        slopes = dot(dpack, pack_field(x))
        moved = coef_ref[BXR] * slopes[:nodes] + coef_ref[BYS] * slopes[nodes:]
        px_ref[c] = x + TIME_STEP * (x * coef_ref[DXBX] - moved - INTERACTION * x)
        py_ref[c] = TIME_STEP * (x * coef_ref[DYBX])


def partial_update(z, x, coef, dpack):
    coefs, part, elements = z[0].shape
    nodes = len(z) * part
    block = coef_block(coefs)
    field = [pl.BlockSpec((block, part, elements), lambda i: (i, 0, 0))] * len(z)
    out = pl.BlockSpec((block, nodes, elements), lambda i: (i, 0, 0))
    return pl.pallas_call(
        functools.partial(partial_kernel, block, len(z)),
        out_shape=[jax.ShapeDtypeStruct((coefs, nodes, elements), F32)] * 3,
        grid=(coefs // block,),
        in_specs=[whole(coef.shape), whole(dpack.shape), *field, *field],
        out_specs=[out] * 3,
        compiler_params=params(),
        cost_estimate=SHORT,
        name="partial_update",
    )(coef, dpack, *z, *x)


def force_kernel(
    block, pos_ref, local_ref, got_up_ref, got_lo_ref, face_ref, geo_ref, dpack_ref,
    scatter_ref, mask_ref, px_ref, pz_ref, o_ref, x_ref, pot_ref,
):
    nodes = dpack_ref.shape[0] // 2
    scale = TIME_STEP * INTERACTION
    me = pos_ref[1]
    pot_ref[...] = local_ref[...]
    first = pos_ref[0] * (block * pl.num_programs(0)) + pl.program_id(0) * block
    for side, got in ((0, got_up_ref), (1, got_lo_ref)):
        face = face_of(pot_ref, side)
        partner = PENALTY * face_inverse(face_ref[side], first, block) * got[0]
        face[...] = face[...] + scatter_faces(side, partner, scatter_ref, mask_ref)
    drpack = dpack_ref[:nodes]
    slope_scale = scale * geo_ref[0:1, :]
    for c in range(block):
        pot = pot_ref[pl.ds(c * nodes, nodes), :]
        slope = dot(drpack, pack_field(pot))
        store_own(o_ref, me, pz_ref[c] - slope_scale * slope, 0, c)
        wave = (4.0 / PLANES) * ((first + c) // 2).astype(F32)
        factor = scale * (wave if c % 2 else -wave)
        other = c - 1 if c % 2 else c + 1
        x_ref[other] = px_ref[other] + factor * pot


def add_force(position, local, got, face, geometry, dpack, scatter, mask, px, pz):
    coefs, nodes, elements = px.shape
    shared = scatter.shape[1]
    block = coef_block(coefs)
    flat = pl.BlockSpec((block * nodes, elements), lambda i: (i, 0))
    one = pl.BlockSpec((1, block, shared), lambda i: (0, i, 0))
    part = pl.BlockSpec((block, nodes, elements), lambda i: (i, 0, 0))
    return pl.pallas_call(
        functools.partial(force_kernel, block),
        out_shape=[
            jax.ShapeDtypeStruct((3, coefs, nodes, elements), F32),
            jax.ShapeDtypeStruct(px.shape, F32),
        ],
        grid=(coefs // block,),
        in_specs=[
            SMEM_SPEC, flat, one, one, whole(face.shape), whole(geometry.shape), whole(dpack.shape),
            whole(scatter.shape), whole(mask.shape), part, part,
        ],
        out_specs=[pl.BlockSpec((1, block, nodes, elements), lambda i: (2, i, 0, 0)), part],
        scratch_shapes=[pltpu.VMEM((block * nodes, elements), F32)],
        compiler_params=params(),
        cost_estimate=SHORT,
        name="add_force",
    )(position, local, *got, face, geometry, dpack, scatter, mask, px, pz)


def finish_kernel(block, count, pos_ref, coef_ref, dpack_ref, px_ref, py_ref, filled_ref, *refs):
    del filled_ref
    y_refs, o_ref = refs[:count], refs[count]
    nodes = coef_ref.shape[1]
    me = pos_ref[1]
    dpack = dpack_ref[...]
    for c in range(block):
        y = slab(y_refs, c)
        slopes = dot(dpack, pack_field(y))
        moved = coef_ref[BXR] * slopes[:nodes] + coef_ref[BYS] * slopes[nodes:]
        change = y + TIME_STEP * (y * coef_ref[DYBY] - moved)
        store_own(o_ref, me, py_ref[c] + change, 1, c)
        store_own(o_ref, me, px_ref[c] + TIME_STEP * (y * coef_ref[DXBY]), 0, c)


def finish(position, y, coef, dpack, px, py, filled):
    coefs, part, elements = y[0].shape
    nodes = len(y) * part
    block = coef_block(coefs)
    field = pl.BlockSpec((block, part, elements), lambda i: (i, 0, 0))
    own = pl.BlockSpec((block, nodes, elements), lambda i: (i, 0, 0))
    return pl.pallas_call(
        functools.partial(finish_kernel, block, len(y)),
        out_shape=jax.ShapeDtypeStruct(filled.shape, F32),
        grid=(coefs // block,),
        in_specs=[
            SMEM_SPEC, whole(coef.shape), whole(dpack.shape), own, own,
            pl.BlockSpec(memory_space=pl.ANY), *[field] * len(y),
        ],
        out_specs=pl.BlockSpec((2, block, nodes, elements), lambda i: (0, i, 0, 0)),
        input_output_aliases={5: 0},
        compiler_params=params(),
        cost_estimate=SHORT,
        name="finish",
    )(position, coef, dpack, px, py, filled, *y)


def to_all(blocks):
    return lax.all_to_all(blocks, "four", split_axis=0, concat_axis=0, tiled=True)


def swap_faces(up, lo):
    peers = lax.axis_size("dom")
    up_way = [(i, (i + 1) % peers) for i in range(peers)]
    down_way = [(j, i) for i, j in up_way]
    return lax.ppermute(lo, "dom", down_way), lax.ppermute(up, "dom", up_way)


class Exchange:
    def __init__(self, blocks, flight):
        self.blocks = list(blocks)
        self.flight = flight
        self.places = {}
        self.order = sorted(range(1, len(self.blocks)), key=lambda d: (-bin(d >> 1).count("1"), d % 2, d))

    def hold(self, value):
        if len(self.places) < len(self.order):
            d = self.order[len(self.places)]
            self.blocks[d], value = lax.optimization_barrier((self.blocks[d], value))
        return value

    def send(self, count):
        for d in self.order[len(self.places) :][:count]:
            block = self.blocks[d]
            if len(self.flight) >= IN_FLIGHT:
                block, self.flight[-IN_FLIGHT] = lax.optimization_barrier((block, self.flight[-IN_FLIGHT]))
            pairs = [(i, i ^ d) for i in range(len(self.blocks))]
            self.places[d] = len(self.flight)
            self.flight.append(lax.ppermute(block, "four", pairs))

    def after(self, value, first, last):
        for d in self.order[first:last]:
            place = self.places[d]
            value, self.flight[place] = lax.optimization_barrier((value, self.flight[place]))
        return value

    def got(self):
        return [self.blocks[0]] + [self.flight[self.places[d]] for d in range(1, len(self.blocks))]


class Whole(Exchange):
    def __init__(self, blocks, exchange):
        super().__init__(blocks[:1], [])
        self.exchange = exchange

    def got(self):
        return self.exchange(self.blocks[0])


def per_device(
    adjoint, base_bank, snapshot, geometry, diff_r, diff_s, stiffness, upper_list, lower_list
):
    _, per, nodes, elements = adjoint.shape
    peers = lax.axis_size("four")
    lines = nodes // LINE
    direct = peers == lines
    place = lax.axis_index("four").astype(jnp.int32)
    position = jnp.stack([place, place if direct else jnp.zeros_like(place)])
    natural = jnp.asarray(coef_table(PLANES))
    table = permuted_table(position, natural, lines)
    flight = []
    share = nodes // peers

    def columns(comp):
        if direct:
            return pack(position, adjoint, comp, LARGE_LIMIT if comp == 2 else VMEM_LIMIT)
        return [jnp.moveaxis(adjoint[comp].reshape(per, peers, share, elements), 1, 0)]

    def gather_planes(block):
        return [to_all(block).reshape(PLANES, share, elements)]

    def gather_lines(block):
        got = jnp.moveaxis(to_all(block.reshape(peers, per, share, elements)), 0, 1)
        got = got.reshape(per, lines, LINE, elements)
        return [got[:, d] for d in range(lines)]

    def spread(blocks):
        return Exchange(blocks, flight) if direct else Whole(blocks, gather_planes)

    def collect(blocks):
        return Exchange(blocks, flight) if direct else Whole(blocks, gather_lines)

    z_out = spread(columns(2))
    z_out.send(3)
    *constants, face = prepare(
        position, base_bank, snapshot, geometry, diff_r, diff_s, stiffness, upper_list, lower_list
    )
    coef, dpack, spack, gather, scatter, mask = constants
    far = z_out.hold(swap_faces(face[0], face[1]))
    z_out.send(4)
    x_out = spread(columns(0))
    table = x_out.hold(table)
    x_out.send(5)
    z_coefs = x_out.hold(transform(z_out.got(), table))
    x_out.send(2)
    y_blocks = columns(1)
    z_back = collect(z_coefs)
    z_back.send(5)
    x_coefs, y_blocks = z_back.hold((transform(x_out.got(), table), y_blocks))
    z_back.send(2)
    x_back = collect(x_coefs)
    x_back.send(7)
    y_out = spread(y_blocks)
    y_out.send(7)
    z = z_back.got()
    x = x_back.got()
    source, inverse, local, up, lo = start_solve(
        position, z, x, geometry, coef, dpack, spack, gather, mask
    )
    got = swap_faces(up, lo)
    parts = partial_update(z, x, coef, dpack)
    local, (px, py, pz) = lax.optimization_barrier((local, parts))
    local = y_out.after(local, 2, 3)
    local, up, lo = two_sweeps(
        2, position, local, source, inverse, (up, lo), got, face, far, spack, gather, scatter, mask
    )
    y_got = list(y_out.got())
    y_got[0], local = lax.optimization_barrier((y_got[0], local))
    got = swap_faces(up, lo)
    y_back = collect(transform(y_got, table))
    y_back.send(7)
    local = y_back.after(local, 0, 1)
    local, up, lo = two_sweeps(
        1, position, local, source, inverse, (up, lo), got, face, far, spack, gather, scatter, mask
    )
    up, lo = y_back.after((up, lo), 1, 3)
    got = swap_faces(up, lo)
    local = y_back.after(local, 3, 5)
    filled, px = add_force(position, local, got, face, geometry, dpack, scatter, mask, px, pz)
    return finish(position, y_back.got(), coef, dpack, px, py, filled)


def solution(mesh):
    in_specs = (
        P(None, "four", None, "dom"),
        P(None, None, None, "dom"),
        P("dom"),
        P(None, "dom"),
        P(),
        P(),
        P(),
        P("dom", None),
        P("dom", None),
    )
    out_specs = P(None, "four", None, "dom")
    return jax.shard_map(
        per_device, mesh=mesh, in_specs=in_specs, out_specs=out_specs, check_vma=False
    )
```

```python
import functools
import math

import jax
import jax.numpy as jnp
import ml_dtypes
import numpy as np
from jax import lax
from jax.experimental import pallas as pl
from jax.experimental.pallas import tpu as pltpu
from jax.sharding import PartitionSpec as P

PLANES = 256
PENALTY = 0.5
RELAXATION = 0.8
TIME_STEP = 0.2
INTERACTION = 2.0
LINE = 8
IN_FLIGHT = 5

F32 = jnp.float32
BF16 = jnp.bfloat16
VMEM_LIMIT = 20 * 1024 * 1024
LARGE_LIMIT = 48 * 1024 * 1024
SMEM_SPEC = pl.BlockSpec(memory_space=pltpu.SMEM)


def params(limit=VMEM_LIMIT):
    return pltpu.CompilerParams(vmem_limit_bytes=limit)


SHORT = pl.CostEstimate(flops=10**6, bytes_accessed=10**5, transcendentals=0)


def cost(flops, moved):
    return pl.CostEstimate(flops=int(flops), bytes_accessed=int(moved), transcendentals=0)


def split(x):
    high = x.astype(BF16)
    low = (x - high.astype(F32)).astype(BF16)
    return high, low


def dot(a, b):
    return lax.dot_general(a, b, (((1,), (0,)), ((), ())), preferred_element_type=F32)


def pack_matrix(m):
    high, low = split(m)
    return jnp.concatenate([high, low, high], axis=1)


def slab(refs, c):
    return jnp.concatenate([ref[c] for ref in refs], axis=0)


def pack_field(v):
    high, low = split(v)
    return jnp.concatenate([high, high, low], axis=0)


def coef_table(length):
    c = np.arange(length)[:, None]
    j = np.arange(length)[None, :]
    angle = ((c // 2) * j % length) * (2.0 * math.pi / length)
    table = np.where(c % 2 == 1, np.sin(angle), np.cos(angle)) * math.sqrt(2.0 / length)
    table[0] = 1.0 / math.sqrt(length)
    table[1] = np.where(np.arange(length) % 2 == 0, 1.0, -1.0) / math.sqrt(length)
    high = table.astype(ml_dtypes.bfloat16)
    low = (table - high.astype(np.float64)).astype(ml_dtypes.bfloat16)
    return np.concatenate([high, low], axis=0)


def permute_kernel(peers, pos_ref, table_ref, o_ref):
    planes = table_ref.shape[1]
    per = planes // peers
    me = pos_ref[1]
    row = lax.broadcasted_iota(jnp.int32, (planes, planes), 0)
    col = lax.broadcasted_iota(jnp.int32, (planes, planes), 1)
    swap = jnp.where(row == ((col // per) ^ me) * per + col % per, 1.0, 0.0).astype(BF16)
    for half in range(2):
        rows = pl.ds(half * planes, planes)
        turned = dot(swap, table_ref[rows, :]).astype(BF16)
        o_ref[rows, :] = dot(turned, swap).astype(BF16)


def permuted_table(position, table, peers):
    return pl.pallas_call(
        functools.partial(permute_kernel, peers),
        out_shape=jax.ShapeDtypeStruct(table.shape, BF16),
        in_specs=[SMEM_SPEC, pl.BlockSpec(memory_space=pltpu.VMEM)],
        compiler_params=params(),
        cost_estimate=cost(1e8, 4e6),
        name="permuted_table",
    )(position, table)


def transform_kernel(count, table_ref, *refs):
    planes = table_ref.shape[1]
    both = table_ref[...]
    high_table = both[:planes]
    width = refs[0].shape[-1]
    nodes = refs[0].shape[-2]
    per = planes // count
    flat = [ref.reshape(per * nodes, width) for ref in refs]
    for n in range(nodes):
        rows = pl.ds(n, per, stride=nodes) if nodes > 1 else pl.ds(0, per)
        high, low = split(jnp.concatenate([ref[rows, :] for ref in flat[:count]], axis=0))
        wide = dot(both, high)
        result = wide[:planes] + (wide[planes:] + dot(high_table, low))
        for d, ref in enumerate(flat[count:]):
            ref[rows, :] = result[d * per : (d + 1) * per]


def transform(blocks, table):
    per, nodes, elements = blocks[0].shape
    count = len(blocks)
    width = 128
    block = pl.BlockSpec((per, nodes, width), lambda i: (0, 0, i))
    size = count * blocks[0].size
    return pl.pallas_call(
        functools.partial(transform_kernel, count),
        out_shape=[jax.ShapeDtypeStruct(v.shape, F32) for v in blocks],
        grid=(elements // width,),
        in_specs=[pl.BlockSpec(table.shape, lambda i: (0, 0))] + [block] * count,
        out_specs=[block] * count,
        compiler_params=params(),
        cost_estimate=cost(6 * PLANES * size, 8 * size),
        name="transform",
    )(table, *blocks)


def pack_kernel(pos_ref, *refs):
    count = len(refs) // 2
    for source, target in zip(refs[:count], refs[count:]):
        target[...] = source[0]


def pack(position, adjoint, comp, limit):
    _, per, nodes, elements = adjoint.shape
    lines = nodes // LINE
    block = per // 2

    def source(d):
        return pl.BlockSpec((1, block, LINE, elements), lambda i, pos: (comp, i, pos[1] ^ d, 0))

    size = per * nodes * elements
    return pl.pallas_call(
        pack_kernel,
        out_shape=[jax.ShapeDtypeStruct((per, LINE, elements), F32)] * lines,
        grid_spec=pltpu.PrefetchScalarGridSpec(
            num_scalar_prefetch=1,
            grid=(per // block,),
            in_specs=[source(d) for d in range(lines)],
            out_specs=[pl.BlockSpec((block, LINE, elements), lambda i, pos: (i, 0, 0))] * lines,
        ),
        compiler_params=params(limit),
        cost_estimate=cost(0, 8 * size),
        name="pack",
    )(position, *[adjoint] * lines)


BXR, BYS, DXBX, DXBY, DYBX, DYBY, DIAG = range(7)


def line_of(me, d):
    return pl.ds(pl.multiple_of((me ^ d) * LINE, LINE), LINE)


def own_order(ref, me, *lead):
    lines = ref.shape[-2] // LINE
    return jnp.concatenate([ref[(*lead, line_of(me, d), slice(None))] for d in range(lines)], axis=0)


def prep_kernel(
    pos_ref, bank_ref, snap_ref, geo_ref, dr_ref, ds_ref, st_ref, up_ref, lo_ref,
    coef_ref, dpack_ref, spack_ref, gather_ref, scatter_ref, mask_ref, face_ref,
):
    elements = geo_ref.shape[1]
    nodes = dr_ref.shape[0]
    lines = nodes // LINE
    me = pos_ref[1]
    row = lax.broadcasted_iota(jnp.int32, (nodes, nodes), 0)
    col = lax.broadcasted_iota(jnp.int32, (nodes, nodes), 1)
    swap = jnp.where(row == ((col // LINE) ^ me) * LINE + col % LINE, 1.0, 0.0).astype(BF16)

    def permuted(ref):
        high, low = split(own_order(ref, me))
        return dot(high, swap) + dot(low, swap)

    snap = snap_ref[...]
    base = [
        sum(
            jnp.where(snap == k, own_order(bank_ref, me, k, i), 0.0)
            for k in range(bank_ref.shape[0])
        )
        for i in range(2)
    ]
    rx = geo_ref[0:1, :]
    sy = geo_ref[1:2, :]
    dpack = pack_matrix(jnp.concatenate([permuted(dr_ref), permuted(ds_ref)], axis=0))
    dpack_ref[...] = dpack
    bx = dot(dpack, pack_field(base[0]))
    by = dot(dpack, pack_field(base[1]))
    coef_ref[BXR] = base[0] * rx
    coef_ref[BYS] = base[1] * sy
    coef_ref[DXBX] = rx * bx[:nodes]
    coef_ref[DXBY] = rx * by[:nodes]
    coef_ref[DYBX] = sy * bx[nodes:]
    coef_ref[DYBY] = sy * by[nodes:]
    diag = jnp.sum(jnp.where(row == col, st_ref[...], 0.0), axis=0, keepdims=True)
    own = ((row // LINE) ^ me) * LINE + row % LINE == col
    diag = jnp.sum(jnp.where(own, diag, 0.0), axis=1, keepdims=True)
    spack_ref[...] = pack_matrix(jnp.where(row == col, 0.0, permuted(st_ref)))
    coef_ref[DIAG] = jnp.broadcast_to(diag, (nodes, elements))
    shared = up_ref.shape[1]
    mass = jnp.broadcast_to(1.0 / (rx * sy), (16, elements))
    for side, (ref, first) in enumerate(((up_ref, LINE - 1), (lo_ref, 0))):
        index = ref[...]
        node = index // elements
        element = index - node * elements
        hot = lax.broadcasted_iota(jnp.int32, (elements, shared), 0) == element
        hot = jnp.where(hot, 1.0, 0.0)
        gather_ref[side] = hot.astype(BF16)
        back = hot.T.astype(BF16)
        scatter_ref[side] = back
        mask = (lax.broadcasted_iota(jnp.int32, (lines, shared), 0) ^ me) == node // LINE
        mask = jnp.where(mask, 1.0, 0.0)
        mask_ref[side] = mask
        high, low = split(mass)
        rest = (mass - high.astype(F32) - low.astype(F32)).astype(BF16)
        at_face = sum(dot(part, gather_ref[side])[:1] for part in (high, low, rest))
        face_ref[side, 0:1, :] = at_face
        lead = jnp.concatenate([diag[s * LINE + first : s * LINE + first + 1] for s in range(lines)], axis=0)
        face_ref[side, 1:2, :] = PENALTY + jnp.sum(mask * lead, axis=0, keepdims=True)
        count = dot(mask.astype(BF16), back)
        for s in range(lines):
            n = s * LINE + first
            coef_ref[DIAG, n : n + 1, :] = coef_ref[DIAG, n : n + 1, :] + PENALTY * count[s : s + 1]


def prepare(position, base_bank, snapshot, geometry, diff_r, diff_s, stiffness, upper, lower):
    nodes = diff_r.shape[0]
    elements = geometry.shape[1]
    shared = upper.shape[1]
    return pl.pallas_call(
        prep_kernel,
        out_shape=[
            jax.ShapeDtypeStruct((7, nodes, elements), F32),
            jax.ShapeDtypeStruct((2 * nodes, 3 * nodes), BF16),
            jax.ShapeDtypeStruct((nodes, 3 * nodes), BF16),
            jax.ShapeDtypeStruct((2, elements, shared), BF16),
            jax.ShapeDtypeStruct((2, shared, elements), BF16),
            jax.ShapeDtypeStruct((2, nodes // LINE, shared), F32),
            jax.ShapeDtypeStruct((2, 2, shared), F32),
        ],
        in_specs=[SMEM_SPEC] + [pl.BlockSpec(memory_space=pltpu.VMEM)] * 8,
        compiler_params=params(),
        cost_estimate=cost(1e7, 8e6),
        name="prepare",
    )(position, base_bank, snapshot.reshape(1, elements), geometry, diff_r, diff_s, stiffness, upper, lower)


def face_of(ref, side):
    rows, elements = ref.shape
    return ref.reshape(rows // LINE, LINE, elements).at[:, LINE - 1 if side == 0 else 0, :]


def gather_faces(side, fields, gather_ref, mask_ref):
    lines = mask_ref.shape[1]
    high, low = split(jnp.concatenate(fields, axis=0))
    rows = high.shape[0]
    both = dot(jnp.concatenate([high, low], axis=0), gather_ref[side])
    picked = both[:rows] + both[rows:]
    shared = picked.shape[1]
    return jnp.sum(picked.reshape(rows // lines, lines, shared) * mask_ref[side][None], axis=1)


def scatter_faces(side, values, scatter_ref, mask_ref):
    mask = mask_ref[side]
    coefs, shared = values.shape
    spread = (values[:, None, :] * mask[None]).reshape(coefs * mask.shape[0], shared)
    high, low = split(spread)
    rows = high.shape[0]
    both = dot(jnp.concatenate([high, low], axis=0), scatter_ref[side])
    return both[:rows] + both[rows:]


def local_sweep(pot, source, inverse, spack):
    applied = dot(spack, pack_field(pot))
    return (1.0 - RELAXATION) * pot + inverse * (source - applied)


def coef_block(coefs):
    return 8 if coefs % 8 == 0 else coefs


def start_kernel(
    block, count, pos_ref, geo_ref, diag_ref, dpack_ref, spack_ref, gather_ref, mask_ref, *refs
):
    z_refs, x_refs = refs[:count], refs[count : 2 * count]
    source_ref, inverse_ref, local_ref, up_ref, lo_ref, pot_ref = refs[2 * count :]
    nodes, elements = diag_ref.shape[1:]
    beta = 4.0 / PLANES
    first = pos_ref[0] * (block * pl.num_programs(0)) + pl.program_id(0) * block
    rx = geo_ref[0:1, :]
    mass = 1.0 / (rx * geo_ref[1:2, :])
    diag = diag_ref[0]
    drpack = dpack_ref[:nodes]
    spack = spack_ref[...]
    for c in range(block):
        index = first + c
        wave = beta * (index // 2).astype(F32)
        shift = beta * jnp.where(index == 1, PLANES // 2, index // 2).astype(F32)
        shift = shift * shift
        z = slab(z_refs, c)
        other = slab(x_refs, c + 1 if c % 2 == 0 else c - 1)
        turned = (wave if c % 2 == 0 else -wave) * other
        source = turned - rx * dot(drpack, pack_field(z))
        inverse = RELAXATION / (diag + shift * mass)
        pot = inverse * source
        rows = pl.ds(c * nodes, nodes)
        source_ref[rows, :] = source
        inverse_ref[rows, :] = inverse
        pot_ref[rows, :] = pot
        local_ref[rows, :] = local_sweep(pot, source, inverse, spack)
    for side, out in ((0, up_ref), (1, lo_ref)):
        fields = [face_of(ref, side)[...] for ref in (pot_ref, local_ref)]
        picked = gather_faces(side, fields, gather_ref, mask_ref)
        for k in range(2):
            out[k] = picked[k * block : (k + 1) * block]


def whole(shape):
    return pl.BlockSpec(shape, lambda *i: (0,) * len(shape))


def start_solve(position, z, x, geometry, coef, dpack, spack, gather, mask):
    coefs, part, elements = z[0].shape
    nodes = len(z) * part
    shared = gather.shape[2]
    block = coef_block(coefs)
    field = [pl.BlockSpec((block, part, elements), lambda i: (i, 0, 0))] * len(z)
    flat = pl.BlockSpec((block * nodes, elements), lambda i: (i, 0))
    face = pl.BlockSpec((2, block, shared), lambda i: (0, i, 0))
    size = coefs * nodes * elements
    return pl.pallas_call(
        functools.partial(start_kernel, block, len(z)),
        out_shape=[jax.ShapeDtypeStruct((coefs * nodes, elements), F32)] * 3
        + [jax.ShapeDtypeStruct((2, coefs, shared), F32)] * 2,
        grid=(coefs // block,),
        in_specs=[
            SMEM_SPEC, whole(geometry.shape),
            pl.BlockSpec((1, nodes, elements), lambda i: (DIAG, 0, 0)),
            whole(dpack.shape), whole(spack.shape), whole(gather.shape), whole(mask.shape),
            *field, *field,
        ],
        out_specs=[flat, flat, flat, face, face],
        scratch_shapes=[pltpu.VMEM((block * nodes, elements), F32)],
        compiler_params=params(),
        cost_estimate=SHORT,
        name="start_solve",
    )(position, geometry, coef, dpack, spack, gather, mask, *z, *x)


def face_inverse(face, first, coefs):
    index = first + lax.broadcasted_iota(jnp.int32, (coefs, 1), 0)
    wave = jnp.where(index == 1, PLANES // 2, index // 2).astype(F32)
    shift = (4.0 / PLANES) * wave
    shift = shift * shift
    return RELAXATION / (face[1:2] + shift * face[0:1])


def sweeps_kernel(
    block, keep, pos_ref, local_ref, source_ref, inverse_ref, own_up_ref, own_lo_ref,
    got_up_ref, got_lo_ref, face_ref, far_up_ref, far_lo_ref, spack_ref, gather_ref, scatter_ref,
    mask_ref, next_ref, up_ref, lo_ref, pot_ref,
):
    nodes = spack_ref.shape[0]
    spack = spack_ref[...]
    lines = block * (nodes // LINE)
    first = pos_ref[0] * (block * pl.num_programs(0)) + pl.program_id(0) * block
    partners = []
    for side, own, got, far in ((0, own_up_ref, got_up_ref, far_up_ref), (1, own_lo_ref, got_lo_ref, far_lo_ref)):
        scale = PENALTY * face_inverse(face_ref[side], first, block)
        now = scale * got[0]
        later = scale * (got[1] + PENALTY * face_inverse(far[...], first, block) * own[0])
        both = scatter_faces(side, jnp.concatenate([now, later], axis=0), scatter_ref, mask_ref)
        partners.append((both[:lines], both[lines:]))
    pot_ref[...] = local_ref[...]
    for side in range(2):
        face = face_of(pot_ref, side)
        face[...] = face[...] + partners[side][0]
    for c in range(block):
        rows = pl.ds(c * nodes, nodes)
        pot_ref[rows, :] = local_sweep(pot_ref[rows, :], source_ref[rows, :], inverse_ref[rows, :], spack)
    for side in range(2):
        face = face_of(pot_ref, side)
        face[...] = face[...] + partners[side][1]
    for c in range(block):
        rows = pl.ds(c * nodes, nodes)
        next_ref[rows, :] = local_sweep(pot_ref[rows, :], source_ref[rows, :], inverse_ref[rows, :], spack)
    for side, out in ((0, up_ref), (1, lo_ref)):
        fields = [face_of(ref, side)[...] for ref in (pot_ref, next_ref)[:keep]]
        picked = gather_faces(side, fields, gather_ref, mask_ref)
        for k in range(keep):
            out[k] = picked[k * block : (k + 1) * block]


def two_sweeps(keep, position, local, source, inverse, own, got, face, far, spack, gather, scatter, mask):
    nodes = spack.shape[0]
    elements = local.shape[1]
    coefs = local.shape[0] // nodes
    shared = gather.shape[2]
    block = coef_block(coefs)
    flat = pl.BlockSpec((block * nodes, elements), lambda i: (i, 0))
    one = pl.BlockSpec((1, block, shared), lambda i: (0, i, 0))
    two = pl.BlockSpec((2, block, shared), lambda i: (0, i, 0))
    kept = pl.BlockSpec((keep, block, shared), lambda i: (0, i, 0))
    size = coefs * nodes * elements
    return pl.pallas_call(
        functools.partial(sweeps_kernel, block, keep),
        out_shape=[jax.ShapeDtypeStruct(local.shape, F32)]
        + [jax.ShapeDtypeStruct((keep, coefs, shared), F32)] * 2,
        grid=(coefs // block,),
        in_specs=[
            SMEM_SPEC, flat, flat, flat, one, one, two, two,
            whole(face.shape), whole(far[0].shape), whole(far[1].shape),
            whole(spack.shape), whole(gather.shape), whole(scatter.shape), whole(mask.shape),
        ],
        out_specs=[flat, kept, kept],
        scratch_shapes=[pltpu.VMEM((block * nodes, elements), F32)],
        compiler_params=params(),
        cost_estimate=SHORT,
        name="two_sweeps",
    )(position, local, source, inverse, *own, *got, face, *far, spack, gather, scatter, mask)


def store_own(ref, me, value, *lead):
    for d in range(value.shape[0] // LINE):
        ref[(*lead, line_of(me, d), slice(None))] = value[d * LINE : (d + 1) * LINE]


def partial_kernel(block, count, coef_ref, dpack_ref, *refs):
    z_refs, x_refs = refs[:count], refs[count : 2 * count]
    px_ref, py_ref, pz_ref = refs[2 * count :]
    nodes = coef_ref.shape[1]
    dpack = dpack_ref[...]
    for c in range(block):
        z = slab(z_refs, c)
        slopes = dot(dpack, pack_field(z))
        moved = coef_ref[BXR] * slopes[:nodes] + coef_ref[BYS] * slopes[nodes:]
        pz_ref[c] = z - TIME_STEP * (moved + INTERACTION * z)
        x = slab(x_refs, c)
        slopes = dot(dpack, pack_field(x))
        moved = coef_ref[BXR] * slopes[:nodes] + coef_ref[BYS] * slopes[nodes:]
        px_ref[c] = x + TIME_STEP * (x * coef_ref[DXBX] - moved - INTERACTION * x)
        py_ref[c] = TIME_STEP * (x * coef_ref[DYBX])


def partial_update(z, x, coef, dpack):
    coefs, part, elements = z[0].shape
    nodes = len(z) * part
    block = coef_block(coefs)
    field = [pl.BlockSpec((block, part, elements), lambda i: (i, 0, 0))] * len(z)
    out = pl.BlockSpec((block, nodes, elements), lambda i: (i, 0, 0))
    return pl.pallas_call(
        functools.partial(partial_kernel, block, len(z)),
        out_shape=[jax.ShapeDtypeStruct((coefs, nodes, elements), F32)] * 3,
        grid=(coefs // block,),
        in_specs=[whole(coef.shape), whole(dpack.shape), *field, *field],
        out_specs=[out] * 3,
        compiler_params=params(),
        cost_estimate=SHORT,
        name="partial_update",
    )(coef, dpack, *z, *x)


def force_kernel(
    block, pos_ref, local_ref, got_up_ref, got_lo_ref, face_ref, geo_ref, dpack_ref,
    scatter_ref, mask_ref, px_ref, pz_ref, o_ref, x_ref, pot_ref,
):
    nodes = dpack_ref.shape[0] // 2
    scale = TIME_STEP * INTERACTION
    me = pos_ref[1]
    pot_ref[...] = local_ref[...]
    first = pos_ref[0] * (block * pl.num_programs(0)) + pl.program_id(0) * block
    for side, got in ((0, got_up_ref), (1, got_lo_ref)):
        face = face_of(pot_ref, side)
        partner = PENALTY * face_inverse(face_ref[side], first, block) * got[0]
        face[...] = face[...] + scatter_faces(side, partner, scatter_ref, mask_ref)
    drpack = dpack_ref[:nodes]
    slope_scale = scale * geo_ref[0:1, :]
    for c in range(block):
        pot = pot_ref[pl.ds(c * nodes, nodes), :]
        slope = dot(drpack, pack_field(pot))
        store_own(o_ref, me, pz_ref[c] - slope_scale * slope, 0, c)
        wave = (4.0 / PLANES) * ((first + c) // 2).astype(F32)
        factor = scale * (wave if c % 2 else -wave)
        other = c - 1 if c % 2 else c + 1
        x_ref[other] = px_ref[other] + factor * pot


def add_force(position, local, got, face, geometry, dpack, scatter, mask, px, pz):
    coefs, nodes, elements = px.shape
    shared = scatter.shape[1]
    block = coef_block(coefs)
    flat = pl.BlockSpec((block * nodes, elements), lambda i: (i, 0))
    one = pl.BlockSpec((1, block, shared), lambda i: (0, i, 0))
    part = pl.BlockSpec((block, nodes, elements), lambda i: (i, 0, 0))
    return pl.pallas_call(
        functools.partial(force_kernel, block),
        out_shape=[
            jax.ShapeDtypeStruct((3, coefs, nodes, elements), F32),
            jax.ShapeDtypeStruct(px.shape, F32),
        ],
        grid=(coefs // block,),
        in_specs=[
            SMEM_SPEC, flat, one, one, whole(face.shape), whole(geometry.shape), whole(dpack.shape),
            whole(scatter.shape), whole(mask.shape), part, part,
        ],
        out_specs=[pl.BlockSpec((1, block, nodes, elements), lambda i: (2, i, 0, 0)), part],
        scratch_shapes=[pltpu.VMEM((block * nodes, elements), F32)],
        compiler_params=params(),
        cost_estimate=SHORT,
        name="add_force",
    )(position, local, *got, face, geometry, dpack, scatter, mask, px, pz)


def finish_kernel(block, count, pos_ref, coef_ref, dpack_ref, px_ref, py_ref, filled_ref, *refs):
    del filled_ref
    y_refs, o_ref = refs[:count], refs[count]
    nodes = coef_ref.shape[1]
    me = pos_ref[1]
    dpack = dpack_ref[...]
    for c in range(block):
        y = slab(y_refs, c)
        slopes = dot(dpack, pack_field(y))
        moved = coef_ref[BXR] * slopes[:nodes] + coef_ref[BYS] * slopes[nodes:]
        change = y + TIME_STEP * (y * coef_ref[DYBY] - moved)
        store_own(o_ref, me, py_ref[c] + change, 1, c)
        store_own(o_ref, me, px_ref[c] + TIME_STEP * (y * coef_ref[DXBY]), 0, c)


def finish(position, y, coef, dpack, px, py, filled):
    coefs, part, elements = y[0].shape
    nodes = len(y) * part
    block = coef_block(coefs)
    field = pl.BlockSpec((block, part, elements), lambda i: (i, 0, 0))
    own = pl.BlockSpec((block, nodes, elements), lambda i: (i, 0, 0))
    return pl.pallas_call(
        functools.partial(finish_kernel, block, len(y)),
        out_shape=jax.ShapeDtypeStruct(filled.shape, F32),
        grid=(coefs // block,),
        in_specs=[
            SMEM_SPEC, whole(coef.shape), whole(dpack.shape), own, own,
            pl.BlockSpec(memory_space=pl.ANY), *[field] * len(y),
        ],
        out_specs=pl.BlockSpec((2, block, nodes, elements), lambda i: (0, i, 0, 0)),
        input_output_aliases={5: 0},
        compiler_params=params(),
        cost_estimate=SHORT,
        name="finish",
    )(position, coef, dpack, px, py, filled, *y)


def to_all(blocks):
    return lax.all_to_all(blocks, "four", split_axis=0, concat_axis=0, tiled=True)


def swap_faces(up, lo):
    peers = lax.axis_size("dom")
    up_way = [(i, (i + 1) % peers) for i in range(peers)]
    down_way = [(j, i) for i, j in up_way]
    return lax.ppermute(lo, "dom", down_way), lax.ppermute(up, "dom", up_way)


class Exchange:
    def __init__(self, blocks, flight):
        self.blocks = list(blocks)
        self.flight = flight
        self.places = {}
        self.order = sorted(range(1, len(self.blocks)), key=lambda d: (d < 2, d % 2, d))

    def hold(self, value):
        if len(self.places) < len(self.order):
            d = self.order[len(self.places)]
            self.blocks[d], value = lax.optimization_barrier((self.blocks[d], value))
        return value

    def send(self, count):
        for d in self.order[len(self.places) :][:count]:
            block = self.blocks[d]
            if len(self.flight) >= IN_FLIGHT:
                block, self.flight[-IN_FLIGHT] = lax.optimization_barrier((block, self.flight[-IN_FLIGHT]))
            pairs = [(i, i ^ d) for i in range(len(self.blocks))]
            self.places[d] = len(self.flight)
            self.flight.append(lax.ppermute(block, "four", pairs))

    def after(self, value, first, last):
        for d in self.order[first:last]:
            place = self.places[d]
            value, self.flight[place] = lax.optimization_barrier((value, self.flight[place]))
        return value

    def got(self):
        return [self.blocks[0]] + [self.flight[self.places[d]] for d in range(1, len(self.blocks))]


class Whole(Exchange):
    def __init__(self, blocks, exchange):
        super().__init__(blocks[:1], [])
        self.exchange = exchange

    def got(self):
        return self.exchange(self.blocks[0])


def per_device(
    adjoint, base_bank, snapshot, geometry, diff_r, diff_s, stiffness, upper_list, lower_list
):
    _, per, nodes, elements = adjoint.shape
    peers = lax.axis_size("four")
    lines = nodes // LINE
    direct = peers == lines
    place = lax.axis_index("four").astype(jnp.int32)
    position = jnp.stack([place, place if direct else jnp.zeros_like(place)])
    natural = jnp.asarray(coef_table(PLANES))
    table = permuted_table(position, natural, lines)
    flight = []
    share = nodes // peers

    def columns(comp):
        if direct:
            return pack(position, adjoint, comp, LARGE_LIMIT if comp == 2 else VMEM_LIMIT)
        return [jnp.moveaxis(adjoint[comp].reshape(per, peers, share, elements), 1, 0)]

    def gather_planes(block):
        return [to_all(block).reshape(PLANES, share, elements)]

    def gather_lines(block):
        got = jnp.moveaxis(to_all(block.reshape(peers, per, share, elements)), 0, 1)
        got = got.reshape(per, lines, LINE, elements)
        return [got[:, d] for d in range(lines)]

    def spread(blocks):
        return Exchange(blocks, flight) if direct else Whole(blocks, gather_planes)

    def collect(blocks):
        return Exchange(blocks, flight) if direct else Whole(blocks, gather_lines)

    z_out = spread(columns(2))
    z_out.send(3)
    *constants, face = prepare(
        position, base_bank, snapshot, geometry, diff_r, diff_s, stiffness, upper_list, lower_list
    )
    coef, dpack, spack, gather, scatter, mask = constants
    far = z_out.hold(swap_faces(face[0], face[1]))
    z_out.send(4)
    x_out = spread(columns(0))
    table = x_out.hold(table)
    x_out.send(5)
    z_coefs = x_out.hold(transform(z_out.got(), table))
    x_out.send(2)
    y_blocks = columns(1)
    z_back = collect(z_coefs)
    z_back.send(5)
    x_coefs, y_blocks = z_back.hold((transform(x_out.got(), table), y_blocks))
    z_back.send(2)
    x_back = collect(x_coefs)
    x_back.send(7)
    y_out = spread(y_blocks)
    y_out.send(7)
    z = z_back.got()
    x = x_back.got()
    source, inverse, local, up, lo = start_solve(
        position, z, x, geometry, coef, dpack, spack, gather, mask
    )
    got = swap_faces(up, lo)
    parts = partial_update(z, x, coef, dpack)
    local, (px, py, pz) = lax.optimization_barrier((local, parts))
    local = y_out.after(local, 2, 3)
    local, up, lo = two_sweeps(
        2, position, local, source, inverse, (up, lo), got, face, far, spack, gather, scatter, mask
    )
    y_got = list(y_out.got())
    y_got[0], local = lax.optimization_barrier((y_got[0], local))
    got = swap_faces(up, lo)
    y_back = collect(transform(y_got, table))
    y_back.send(7)
    local = y_back.after(local, 0, 2)
    local, up, lo = two_sweeps(
        1, position, local, source, inverse, (up, lo), got, face, far, spack, gather, scatter, mask
    )
    up, lo = y_back.after((up, lo), 2, 4)
    got = swap_faces(up, lo)
    local = y_back.after(local, 4, 5)
    filled, px = add_force(position, local, got, face, geometry, dpack, scatter, mask, px, pz)
    return finish(position, y_back.got(), coef, dpack, px, py, filled)


def solution(mesh):
    in_specs = (
        P(None, "four", None, "dom"),
        P(None, None, None, "dom"),
        P("dom"),
        P(None, "dom"),
        P(),
        P(),
        P(),
        P("dom", None),
        P("dom", None),
    )
    out_specs = P(None, "four", None, "dom")
    return jax.shard_map(
        per_device, mesh=mesh, in_specs=in_specs, out_specs=out_specs, check_vma=False
    )
```

```python
import functools
import math

import jax
import jax.numpy as jnp
import ml_dtypes
import numpy as np
from jax import lax
from jax.experimental import pallas as pl
from jax.experimental.pallas import tpu as pltpu
from jax.sharding import PartitionSpec as P

PLANES = 256
PENALTY = 0.5
RELAXATION = 0.8
TIME_STEP = 0.2
INTERACTION = 2.0
LINE = 8
IN_FLIGHT = 5

F32 = jnp.float32
BF16 = jnp.bfloat16
VMEM_LIMIT = 20 * 1024 * 1024
LARGE_LIMIT = 48 * 1024 * 1024
SMEM_SPEC = pl.BlockSpec(memory_space=pltpu.SMEM)


def params(limit=VMEM_LIMIT):
    return pltpu.CompilerParams(vmem_limit_bytes=limit)


SHORT = pl.CostEstimate(flops=10**6, bytes_accessed=10**5, transcendentals=0)


def cost(flops, moved):
    return pl.CostEstimate(flops=int(flops), bytes_accessed=int(moved), transcendentals=0)


def split(x):
    high = x.astype(BF16)
    low = (x - high.astype(F32)).astype(BF16)
    return high, low


def dot(a, b):
    return lax.dot_general(a, b, (((1,), (0,)), ((), ())), preferred_element_type=F32)


def pack_matrix(m):
    high, low = split(m)
    return jnp.concatenate([high, low, high], axis=1)


def slab(refs, c):
    return jnp.concatenate([ref[c] for ref in refs], axis=0)


def pack_field(v):
    high, low = split(v)
    return jnp.concatenate([high, high, low], axis=0)


def coef_table(length):
    c = np.arange(length)[:, None]
    j = np.arange(length)[None, :]
    angle = ((c // 2) * j % length) * (2.0 * math.pi / length)
    table = np.where(c % 2 == 1, np.sin(angle), np.cos(angle)) * math.sqrt(2.0 / length)
    table[0] = 1.0 / math.sqrt(length)
    table[1] = np.where(np.arange(length) % 2 == 0, 1.0, -1.0) / math.sqrt(length)
    high = table.astype(ml_dtypes.bfloat16)
    low = (table - high.astype(np.float64)).astype(ml_dtypes.bfloat16)
    return np.concatenate([high, low], axis=0)


def permute_kernel(peers, pos_ref, table_ref, o_ref):
    planes = table_ref.shape[1]
    per = planes // peers
    me = pos_ref[1]
    row = lax.broadcasted_iota(jnp.int32, (planes, planes), 0)
    col = lax.broadcasted_iota(jnp.int32, (planes, planes), 1)
    swap = jnp.where(row == ((col // per) ^ me) * per + col % per, 1.0, 0.0).astype(BF16)
    for half in range(2):
        rows = pl.ds(half * planes, planes)
        turned = dot(swap, table_ref[rows, :]).astype(BF16)
        o_ref[rows, :] = dot(turned, swap).astype(BF16)


def permuted_table(position, table, peers):
    return pl.pallas_call(
        functools.partial(permute_kernel, peers),
        out_shape=jax.ShapeDtypeStruct(table.shape, BF16),
        in_specs=[SMEM_SPEC, pl.BlockSpec(memory_space=pltpu.VMEM)],
        compiler_params=params(),
        cost_estimate=cost(1e8, 4e6),
        name="permuted_table",
    )(position, table)


def transform_kernel(count, table_ref, *refs):
    planes = table_ref.shape[1]
    both = table_ref[...]
    high_table = both[:planes]
    width = refs[0].shape[-1]
    nodes = refs[0].shape[-2]
    per = planes // count
    flat = [ref.reshape(per * nodes, width) for ref in refs]
    for n in range(nodes):
        rows = pl.ds(n, per, stride=nodes) if nodes > 1 else pl.ds(0, per)
        high, low = split(jnp.concatenate([ref[rows, :] for ref in flat[:count]], axis=0))
        wide = dot(both, high)
        result = wide[:planes] + (wide[planes:] + dot(high_table, low))
        for d, ref in enumerate(flat[count:]):
            ref[rows, :] = result[d * per : (d + 1) * per]


def transform(blocks, table):
    per, nodes, elements = blocks[0].shape
    count = len(blocks)
    width = 128
    block = pl.BlockSpec((per, nodes, width), lambda i: (0, 0, i))
    size = count * blocks[0].size
    return pl.pallas_call(
        functools.partial(transform_kernel, count),
        out_shape=[jax.ShapeDtypeStruct(v.shape, F32) for v in blocks],
        grid=(elements // width,),
        in_specs=[pl.BlockSpec(table.shape, lambda i: (0, 0))] + [block] * count,
        out_specs=[block] * count,
        compiler_params=params(),
        cost_estimate=cost(6 * PLANES * size, 8 * size),
        name="transform",
    )(table, *blocks)


def pack_kernel(pos_ref, *refs):
    count = len(refs) // 2
    for source, target in zip(refs[:count], refs[count:]):
        target[...] = source[0]


def pack(position, adjoint, comp, limit):
    _, per, nodes, elements = adjoint.shape
    lines = nodes // LINE
    block = per // 2

    def source(d):
        return pl.BlockSpec((1, block, LINE, elements), lambda i, pos: (comp, i, pos[1] ^ d, 0))

    size = per * nodes * elements
    return pl.pallas_call(
        pack_kernel,
        out_shape=[jax.ShapeDtypeStruct((per, LINE, elements), F32)] * lines,
        grid_spec=pltpu.PrefetchScalarGridSpec(
            num_scalar_prefetch=1,
            grid=(per // block,),
            in_specs=[source(d) for d in range(lines)],
            out_specs=[pl.BlockSpec((block, LINE, elements), lambda i, pos: (i, 0, 0))] * lines,
        ),
        compiler_params=params(limit),
        cost_estimate=cost(0, 8 * size),
        name="pack",
    )(position, *[adjoint] * lines)


BXR, BYS, DXBX, DXBY, DYBX, DYBY, DIAG = range(7)


def line_of(me, d):
    return pl.ds(pl.multiple_of((me ^ d) * LINE, LINE), LINE)


def own_order(ref, me, *lead):
    lines = ref.shape[-2] // LINE
    return jnp.concatenate([ref[(*lead, line_of(me, d), slice(None))] for d in range(lines)], axis=0)


def prep_kernel(
    pos_ref, bank_ref, snap_ref, geo_ref, dr_ref, ds_ref, st_ref, up_ref, lo_ref,
    coef_ref, dpack_ref, spack_ref, gather_ref, scatter_ref, mask_ref, face_ref,
):
    elements = geo_ref.shape[1]
    nodes = dr_ref.shape[0]
    lines = nodes // LINE
    me = pos_ref[1]
    row = lax.broadcasted_iota(jnp.int32, (nodes, nodes), 0)
    col = lax.broadcasted_iota(jnp.int32, (nodes, nodes), 1)
    swap = jnp.where(row == ((col // LINE) ^ me) * LINE + col % LINE, 1.0, 0.0).astype(BF16)

    def permuted(ref):
        high, low = split(own_order(ref, me))
        return dot(high, swap) + dot(low, swap)

    snap = snap_ref[...]
    base = [
        sum(
            jnp.where(snap == k, own_order(bank_ref, me, k, i), 0.0)
            for k in range(bank_ref.shape[0])
        )
        for i in range(2)
    ]
    rx = geo_ref[0:1, :]
    sy = geo_ref[1:2, :]
    dpack = pack_matrix(jnp.concatenate([permuted(dr_ref), permuted(ds_ref)], axis=0))
    dpack_ref[...] = dpack
    bx = dot(dpack, pack_field(base[0]))
    by = dot(dpack, pack_field(base[1]))
    coef_ref[BXR] = base[0] * rx
    coef_ref[BYS] = base[1] * sy
    coef_ref[DXBX] = rx * bx[:nodes]
    coef_ref[DXBY] = rx * by[:nodes]
    coef_ref[DYBX] = sy * bx[nodes:]
    coef_ref[DYBY] = sy * by[nodes:]
    diag = jnp.sum(jnp.where(row == col, st_ref[...], 0.0), axis=0, keepdims=True)
    own = ((row // LINE) ^ me) * LINE + row % LINE == col
    diag = jnp.sum(jnp.where(own, diag, 0.0), axis=1, keepdims=True)
    spack_ref[...] = pack_matrix(jnp.where(row == col, 0.0, permuted(st_ref)))
    coef_ref[DIAG] = jnp.broadcast_to(diag, (nodes, elements))
    shared = up_ref.shape[1]
    mass = jnp.broadcast_to(1.0 / (rx * sy), (16, elements))
    for side, (ref, first) in enumerate(((up_ref, LINE - 1), (lo_ref, 0))):
        index = ref[...]
        node = index // elements
        element = index - node * elements
        hot = lax.broadcasted_iota(jnp.int32, (elements, shared), 0) == element
        hot = jnp.where(hot, 1.0, 0.0)
        gather_ref[side] = hot.astype(BF16)
        back = hot.T.astype(BF16)
        scatter_ref[side] = back
        mask = (lax.broadcasted_iota(jnp.int32, (lines, shared), 0) ^ me) == node // LINE
        mask = jnp.where(mask, 1.0, 0.0)
        mask_ref[side] = mask
        high, low = split(mass)
        rest = (mass - high.astype(F32) - low.astype(F32)).astype(BF16)
        at_face = sum(dot(part, gather_ref[side])[:1] for part in (high, low, rest))
        face_ref[side, 0:1, :] = at_face
        lead = jnp.concatenate([diag[s * LINE + first : s * LINE + first + 1] for s in range(lines)], axis=0)
        face_ref[side, 1:2, :] = PENALTY + jnp.sum(mask * lead, axis=0, keepdims=True)
        count = dot(mask.astype(BF16), back)
        for s in range(lines):
            n = s * LINE + first
            coef_ref[DIAG, n : n + 1, :] = coef_ref[DIAG, n : n + 1, :] + PENALTY * count[s : s + 1]


def prepare(position, base_bank, snapshot, geometry, diff_r, diff_s, stiffness, upper, lower):
    nodes = diff_r.shape[0]
    elements = geometry.shape[1]
    shared = upper.shape[1]
    return pl.pallas_call(
        prep_kernel,
        out_shape=[
            jax.ShapeDtypeStruct((7, nodes, elements), F32),
            jax.ShapeDtypeStruct((2 * nodes, 3 * nodes), BF16),
            jax.ShapeDtypeStruct((nodes, 3 * nodes), BF16),
            jax.ShapeDtypeStruct((2, elements, shared), BF16),
            jax.ShapeDtypeStruct((2, shared, elements), BF16),
            jax.ShapeDtypeStruct((2, nodes // LINE, shared), F32),
            jax.ShapeDtypeStruct((2, 2, shared), F32),
        ],
        in_specs=[SMEM_SPEC] + [pl.BlockSpec(memory_space=pltpu.VMEM)] * 8,
        compiler_params=params(),
        cost_estimate=cost(1e7, 8e6),
        name="prepare",
    )(position, base_bank, snapshot.reshape(1, elements), geometry, diff_r, diff_s, stiffness, upper, lower)


def face_of(ref, side):
    rows, elements = ref.shape
    return ref.reshape(rows // LINE, LINE, elements).at[:, LINE - 1 if side == 0 else 0, :]


def gather_faces(side, fields, gather_ref, mask_ref):
    lines = mask_ref.shape[1]
    high, low = split(jnp.concatenate(fields, axis=0))
    rows = high.shape[0]
    both = dot(jnp.concatenate([high, low], axis=0), gather_ref[side])
    picked = both[:rows] + both[rows:]
    shared = picked.shape[1]
    return jnp.sum(picked.reshape(rows // lines, lines, shared) * mask_ref[side][None], axis=1)


def scatter_faces(side, values, scatter_ref, mask_ref):
    mask = mask_ref[side]
    coefs, shared = values.shape
    spread = (values[:, None, :] * mask[None]).reshape(coefs * mask.shape[0], shared)
    high, low = split(spread)
    rows = high.shape[0]
    both = dot(jnp.concatenate([high, low], axis=0), scatter_ref[side])
    return both[:rows] + both[rows:]


def local_sweep(pot, source, inverse, spack):
    applied = dot(spack, pack_field(pot))
    return (1.0 - RELAXATION) * pot + inverse * (source - applied)


def coef_block(coefs, block=8):
    return block if coefs % block == 0 else coefs


def start_kernel(
    block, count, pos_ref, geo_ref, diag_ref, dpack_ref, spack_ref, gather_ref, mask_ref, *refs
):
    z_refs, x_refs = refs[:count], refs[count : 2 * count]
    source_ref, inverse_ref, local_ref, up_ref, lo_ref, pot_ref = refs[2 * count :]
    nodes, elements = diag_ref.shape[1:]
    beta = 4.0 / PLANES
    first = pos_ref[0] * (block * pl.num_programs(0)) + pl.program_id(0) * block
    rx = geo_ref[0:1, :]
    mass = 1.0 / (rx * geo_ref[1:2, :])
    diag = diag_ref[0]
    drpack = dpack_ref[:nodes]
    spack = spack_ref[...]
    for c in range(block):
        index = first + c
        wave = beta * (index // 2).astype(F32)
        shift = beta * jnp.where(index == 1, PLANES // 2, index // 2).astype(F32)
        shift = shift * shift
        z = slab(z_refs, c)
        other = slab(x_refs, c + 1 if c % 2 == 0 else c - 1)
        turned = (wave if c % 2 == 0 else -wave) * other
        source = turned - rx * dot(drpack, pack_field(z))
        inverse = RELAXATION / (diag + shift * mass)
        pot = inverse * source
        rows = pl.ds(c * nodes, nodes)
        source_ref[rows, :] = source
        inverse_ref[rows, :] = inverse
        pot_ref[rows, :] = pot
        local_ref[rows, :] = local_sweep(pot, source, inverse, spack)
    for side, out in ((0, up_ref), (1, lo_ref)):
        fields = [face_of(ref, side)[...] for ref in (pot_ref, local_ref)]
        picked = gather_faces(side, fields, gather_ref, mask_ref)
        for k in range(2):
            out[k] = picked[k * block : (k + 1) * block]


def whole(shape):
    return pl.BlockSpec(shape, lambda *i: (0,) * len(shape))


def start_solve(position, z, x, geometry, coef, dpack, spack, gather, mask):
    coefs, part, elements = z[0].shape
    nodes = len(z) * part
    shared = gather.shape[2]
    block = coef_block(coefs)
    field = [pl.BlockSpec((block, part, elements), lambda i: (i, 0, 0))] * len(z)
    flat = pl.BlockSpec((block * nodes, elements), lambda i: (i, 0))
    face = pl.BlockSpec((2, block, shared), lambda i: (0, i, 0))
    size = coefs * nodes * elements
    return pl.pallas_call(
        functools.partial(start_kernel, block, len(z)),
        out_shape=[jax.ShapeDtypeStruct((coefs * nodes, elements), F32)] * 3
        + [jax.ShapeDtypeStruct((2, coefs, shared), F32)] * 2,
        grid=(coefs // block,),
        in_specs=[
            SMEM_SPEC, whole(geometry.shape),
            pl.BlockSpec((1, nodes, elements), lambda i: (DIAG, 0, 0)),
            whole(dpack.shape), whole(spack.shape), whole(gather.shape), whole(mask.shape),
            *field, *field,
        ],
        out_specs=[flat, flat, flat, face, face],
        scratch_shapes=[pltpu.VMEM((block * nodes, elements), F32)],
        compiler_params=params(),
        cost_estimate=SHORT,
        name="start_solve",
    )(position, geometry, coef, dpack, spack, gather, mask, *z, *x)


def face_inverse(face, first, coefs):
    index = first + lax.broadcasted_iota(jnp.int32, (coefs, 1), 0)
    wave = jnp.where(index == 1, PLANES // 2, index // 2).astype(F32)
    shift = (4.0 / PLANES) * wave
    shift = shift * shift
    return RELAXATION / (face[1:2] + shift * face[0:1])


def sweeps_kernel(
    block, keep, pos_ref, local_ref, source_ref, inverse_ref, own_up_ref, own_lo_ref,
    got_up_ref, got_lo_ref, face_ref, far_up_ref, far_lo_ref, spack_ref, gather_ref, scatter_ref,
    mask_ref, next_ref, up_ref, lo_ref, pot_ref,
):
    nodes = spack_ref.shape[0]
    spack = spack_ref[...]
    lines = block * (nodes // LINE)
    first = pos_ref[0] * (block * pl.num_programs(0)) + pl.program_id(0) * block
    partners = []
    for side, own, got, far in ((0, own_up_ref, got_up_ref, far_up_ref), (1, own_lo_ref, got_lo_ref, far_lo_ref)):
        scale = PENALTY * face_inverse(face_ref[side], first, block)
        now = scale * got[0]
        later = scale * (got[1] + PENALTY * face_inverse(far[...], first, block) * own[0])
        both = scatter_faces(side, jnp.concatenate([now, later], axis=0), scatter_ref, mask_ref)
        partners.append((both[:lines], both[lines:]))
    pot_ref[...] = local_ref[...]
    for side in range(2):
        face = face_of(pot_ref, side)
        face[...] = face[...] + partners[side][0]
    for c in range(block):
        rows = pl.ds(c * nodes, nodes)
        pot_ref[rows, :] = local_sweep(pot_ref[rows, :], source_ref[rows, :], inverse_ref[rows, :], spack)
    for side in range(2):
        face = face_of(pot_ref, side)
        face[...] = face[...] + partners[side][1]
    for c in range(block):
        rows = pl.ds(c * nodes, nodes)
        next_ref[rows, :] = local_sweep(pot_ref[rows, :], source_ref[rows, :], inverse_ref[rows, :], spack)
    for side, out in ((0, up_ref), (1, lo_ref)):
        fields = [face_of(ref, side)[...] for ref in (pot_ref, next_ref)[:keep]]
        picked = gather_faces(side, fields, gather_ref, mask_ref)
        for k in range(keep):
            out[k] = picked[k * block : (k + 1) * block]


def two_sweeps(keep, position, local, source, inverse, own, got, face, far, spack, gather, scatter, mask):
    nodes = spack.shape[0]
    elements = local.shape[1]
    coefs = local.shape[0] // nodes
    shared = gather.shape[2]
    block = coef_block(coefs, 16)
    flat = pl.BlockSpec((block * nodes, elements), lambda i: (i, 0))
    one = pl.BlockSpec((1, block, shared), lambda i: (0, i, 0))
    two = pl.BlockSpec((2, block, shared), lambda i: (0, i, 0))
    kept = pl.BlockSpec((keep, block, shared), lambda i: (0, i, 0))
    size = coefs * nodes * elements
    return pl.pallas_call(
        functools.partial(sweeps_kernel, block, keep),
        out_shape=[jax.ShapeDtypeStruct(local.shape, F32)]
        + [jax.ShapeDtypeStruct((keep, coefs, shared), F32)] * 2,
        grid=(coefs // block,),
        in_specs=[
            SMEM_SPEC, flat, flat, flat, one, one, two, two,
            whole(face.shape), whole(far[0].shape), whole(far[1].shape),
            whole(spack.shape), whole(gather.shape), whole(scatter.shape), whole(mask.shape),
        ],
        out_specs=[flat, kept, kept],
        scratch_shapes=[pltpu.VMEM((block * nodes, elements), F32)],
        compiler_params=params(),
        cost_estimate=SHORT,
        name="two_sweeps",
    )(position, local, source, inverse, *own, *got, face, *far, spack, gather, scatter, mask)


def store_own(ref, me, value, *lead):
    for d in range(value.shape[0] // LINE):
        ref[(*lead, line_of(me, d), slice(None))] = value[d * LINE : (d + 1) * LINE]


def partial_kernel(block, count, coef_ref, dpack_ref, *refs):
    z_refs, x_refs = refs[:count], refs[count : 2 * count]
    px_ref, py_ref, pz_ref = refs[2 * count :]
    nodes = coef_ref.shape[1]
    dpack = dpack_ref[...]
    for c in range(block):
        z = slab(z_refs, c)
        slopes = dot(dpack, pack_field(z))
        moved = coef_ref[BXR] * slopes[:nodes] + coef_ref[BYS] * slopes[nodes:]
        pz_ref[c] = z - TIME_STEP * (moved + INTERACTION * z)
        x = slab(x_refs, c)
        slopes = dot(dpack, pack_field(x))
        moved = coef_ref[BXR] * slopes[:nodes] + coef_ref[BYS] * slopes[nodes:]
        px_ref[c] = x + TIME_STEP * (x * coef_ref[DXBX] - moved - INTERACTION * x)
        py_ref[c] = TIME_STEP * (x * coef_ref[DYBX])


def partial_update(z, x, coef, dpack):
    coefs, part, elements = z[0].shape
    nodes = len(z) * part
    block = coef_block(coefs)
    field = [pl.BlockSpec((block, part, elements), lambda i: (i, 0, 0))] * len(z)
    out = pl.BlockSpec((block, nodes, elements), lambda i: (i, 0, 0))
    return pl.pallas_call(
        functools.partial(partial_kernel, block, len(z)),
        out_shape=[jax.ShapeDtypeStruct((coefs, nodes, elements), F32)] * 3,
        grid=(coefs // block,),
        in_specs=[whole(coef.shape), whole(dpack.shape), *field, *field],
        out_specs=[out] * 3,
        compiler_params=params(),
        cost_estimate=SHORT,
        name="partial_update",
    )(coef, dpack, *z, *x)


def force_kernel(
    block, pos_ref, local_ref, got_up_ref, got_lo_ref, face_ref, geo_ref, dpack_ref,
    scatter_ref, mask_ref, px_ref, pz_ref, o_ref, x_ref, pot_ref,
):
    nodes = dpack_ref.shape[0] // 2
    scale = TIME_STEP * INTERACTION
    me = pos_ref[1]
    pot_ref[...] = local_ref[...]
    first = pos_ref[0] * (block * pl.num_programs(0)) + pl.program_id(0) * block
    for side, got in ((0, got_up_ref), (1, got_lo_ref)):
        face = face_of(pot_ref, side)
        partner = PENALTY * face_inverse(face_ref[side], first, block) * got[0]
        face[...] = face[...] + scatter_faces(side, partner, scatter_ref, mask_ref)
    drpack = dpack_ref[:nodes]
    slope_scale = scale * geo_ref[0:1, :]
    for c in range(block):
        pot = pot_ref[pl.ds(c * nodes, nodes), :]
        slope = dot(drpack, pack_field(pot))
        store_own(o_ref, me, pz_ref[c] - slope_scale * slope, 0, c)
        wave = (4.0 / PLANES) * ((first + c) // 2).astype(F32)
        factor = scale * (wave if c % 2 else -wave)
        other = c - 1 if c % 2 else c + 1
        x_ref[other] = px_ref[other] + factor * pot


def add_force(position, local, got, face, geometry, dpack, scatter, mask, px, pz):
    coefs, nodes, elements = px.shape
    shared = scatter.shape[1]
    block = coef_block(coefs)
    flat = pl.BlockSpec((block * nodes, elements), lambda i: (i, 0))
    one = pl.BlockSpec((1, block, shared), lambda i: (0, i, 0))
    part = pl.BlockSpec((block, nodes, elements), lambda i: (i, 0, 0))
    return pl.pallas_call(
        functools.partial(force_kernel, block),
        out_shape=[
            jax.ShapeDtypeStruct((3, coefs, nodes, elements), F32),
            jax.ShapeDtypeStruct(px.shape, F32),
        ],
        grid=(coefs // block,),
        in_specs=[
            SMEM_SPEC, flat, one, one, whole(face.shape), whole(geometry.shape), whole(dpack.shape),
            whole(scatter.shape), whole(mask.shape), part, part,
        ],
        out_specs=[pl.BlockSpec((1, block, nodes, elements), lambda i: (2, i, 0, 0)), part],
        scratch_shapes=[pltpu.VMEM((block * nodes, elements), F32)],
        compiler_params=params(),
        cost_estimate=SHORT,
        name="add_force",
    )(position, local, *got, face, geometry, dpack, scatter, mask, px, pz)


def finish_kernel(block, count, pos_ref, coef_ref, dpack_ref, px_ref, py_ref, filled_ref, *refs):
    del filled_ref
    y_refs, o_ref = refs[:count], refs[count]
    nodes = coef_ref.shape[1]
    me = pos_ref[1]
    dpack = dpack_ref[...]
    for c in range(block):
        y = slab(y_refs, c)
        slopes = dot(dpack, pack_field(y))
        moved = coef_ref[BXR] * slopes[:nodes] + coef_ref[BYS] * slopes[nodes:]
        change = y + TIME_STEP * (y * coef_ref[DYBY] - moved)
        store_own(o_ref, me, py_ref[c] + change, 1, c)
        store_own(o_ref, me, px_ref[c] + TIME_STEP * (y * coef_ref[DXBY]), 0, c)


def finish(position, y, coef, dpack, px, py, filled):
    coefs, part, elements = y[0].shape
    nodes = len(y) * part
    block = coef_block(coefs, 4)
    field = pl.BlockSpec((block, part, elements), lambda i: (i, 0, 0))
    own = pl.BlockSpec((block, nodes, elements), lambda i: (i, 0, 0))
    return pl.pallas_call(
        functools.partial(finish_kernel, block, len(y)),
        out_shape=jax.ShapeDtypeStruct(filled.shape, F32),
        grid=(coefs // block,),
        in_specs=[
            SMEM_SPEC, whole(coef.shape), whole(dpack.shape), own, own,
            pl.BlockSpec(memory_space=pl.ANY), *[field] * len(y),
        ],
        out_specs=pl.BlockSpec((2, block, nodes, elements), lambda i: (0, i, 0, 0)),
        input_output_aliases={5: 0},
        compiler_params=params(),
        cost_estimate=SHORT,
        name="finish",
    )(position, coef, dpack, px, py, filled, *y)


def to_all(blocks):
    return lax.all_to_all(blocks, "four", split_axis=0, concat_axis=0, tiled=True)


def swap_faces(up, lo):
    peers = lax.axis_size("dom")
    up_way = [(i, (i + 1) % peers) for i in range(peers)]
    down_way = [(j, i) for i, j in up_way]
    return lax.ppermute(lo, "dom", down_way), lax.ppermute(up, "dom", up_way)


class Exchange:
    def __init__(self, blocks, flight):
        self.blocks = list(blocks)
        self.flight = flight
        self.places = {}
        self.order = sorted(range(1, len(self.blocks)), key=lambda d: (d < 2, d % 2, d))

    def hold(self, value):
        if len(self.places) < len(self.order):
            d = self.order[len(self.places)]
            self.blocks[d], value = lax.optimization_barrier((self.blocks[d], value))
        return value

    def send(self, count):
        for d in self.order[len(self.places) :][:count]:
            block = self.blocks[d]
            if len(self.flight) >= IN_FLIGHT:
                block, self.flight[-IN_FLIGHT] = lax.optimization_barrier((block, self.flight[-IN_FLIGHT]))
            pairs = [(i, i ^ d) for i in range(len(self.blocks))]
            self.places[d] = len(self.flight)
            self.flight.append(lax.ppermute(block, "four", pairs))

    def after(self, value, first, last):
        for d in self.order[first:last]:
            place = self.places[d]
            value, self.flight[place] = lax.optimization_barrier((value, self.flight[place]))
        return value

    def got(self):
        return [self.blocks[0]] + [self.flight[self.places[d]] for d in range(1, len(self.blocks))]


class Whole(Exchange):
    def __init__(self, blocks, exchange):
        super().__init__(blocks[:1], [])
        self.exchange = exchange

    def got(self):
        return self.exchange(self.blocks[0])


def per_device(
    adjoint, base_bank, snapshot, geometry, diff_r, diff_s, stiffness, upper_list, lower_list
):
    _, per, nodes, elements = adjoint.shape
    peers = lax.axis_size("four")
    lines = nodes // LINE
    direct = peers == lines
    place = lax.axis_index("four").astype(jnp.int32)
    position = jnp.stack([place, place if direct else jnp.zeros_like(place)])
    natural = jnp.asarray(coef_table(PLANES))
    table = permuted_table(position, natural, lines)
    flight = []
    share = nodes // peers

    def columns(comp):
        if direct:
            return pack(position, adjoint, comp, LARGE_LIMIT if comp == 2 else VMEM_LIMIT)
        return [jnp.moveaxis(adjoint[comp].reshape(per, peers, share, elements), 1, 0)]

    def gather_planes(block):
        return [to_all(block).reshape(PLANES, share, elements)]

    def gather_lines(block):
        got = jnp.moveaxis(to_all(block.reshape(peers, per, share, elements)), 0, 1)
        got = got.reshape(per, lines, LINE, elements)
        return [got[:, d] for d in range(lines)]

    def spread(blocks):
        return Exchange(blocks, flight) if direct else Whole(blocks, gather_planes)

    def collect(blocks):
        return Exchange(blocks, flight) if direct else Whole(blocks, gather_lines)

    z_out = spread(columns(2))
    z_out.send(3)
    *constants, face = prepare(
        position, base_bank, snapshot, geometry, diff_r, diff_s, stiffness, upper_list, lower_list
    )
    coef, dpack, spack, gather, scatter, mask = constants
    far = z_out.hold(swap_faces(face[0], face[1]))
    z_out.send(4)
    x_out = spread(columns(0))
    table = x_out.hold(table)
    x_out.send(5)
    z_coefs = x_out.hold(transform(z_out.got(), table))
    x_out.send(2)
    y_blocks = columns(1)
    z_back = collect(z_coefs)
    z_back.send(5)
    x_coefs, y_blocks = z_back.hold((transform(x_out.got(), table), y_blocks))
    z_back.send(2)
    x_back = collect(x_coefs)
    x_back.send(7)
    y_out = spread(y_blocks)
    y_out.send(7)
    z = z_back.got()
    x = x_back.got()
    source, inverse, local, up, lo = start_solve(
        position, z, x, geometry, coef, dpack, spack, gather, mask
    )
    got = swap_faces(up, lo)
    parts = partial_update(z, x, coef, dpack)
    local, (px, py, pz) = lax.optimization_barrier((local, parts))
    local = y_out.after(local, 2, 3)
    local, up, lo = two_sweeps(
        2, position, local, source, inverse, (up, lo), got, face, far, spack, gather, scatter, mask
    )
    y_got = list(y_out.got())
    y_got[0], local = lax.optimization_barrier((y_got[0], local))
    got = swap_faces(up, lo)
    y_back = collect(transform(y_got, table))
    y_back.send(6)
    local = y_back.after(local, 0, 2)
    local, up, lo = two_sweeps(
        1, position, local, source, inverse, (up, lo), got, face, far, spack, gather, scatter, mask
    )
    up = y_back.hold(up)
    y_back.send(1)
    up, lo = y_back.after((up, lo), 2, 3)
    got = swap_faces(up, lo)
    local = y_back.after(local, 4, 6)
    filled, px = add_force(position, local, got, face, geometry, dpack, scatter, mask, px, pz)
    return finish(position, y_back.got(), coef, dpack, px, py, filled)


def solution(mesh):
    in_specs = (
        P(None, "four", None, "dom"),
        P(None, None, None, "dom"),
        P("dom"),
        P(None, "dom"),
        P(),
        P(),
        P(),
        P("dom", None),
        P("dom", None),
    )
    out_specs = P(None, "four", None, "dom")
    return jax.shard_map(
        per_device, mesh=mesh, in_specs=in_specs, out_specs=out_specs, check_vma=False
    )
```

```python
import functools
import math

import jax
import jax.numpy as jnp
import ml_dtypes
import numpy as np
from jax import lax
from jax.experimental import pallas as pl
from jax.experimental.pallas import tpu as pltpu
from jax.sharding import PartitionSpec as P

PLANES = 256
PENALTY = 0.5
RELAXATION = 0.8
TIME_STEP = 0.2
INTERACTION = 2.0
LINE = 8
IN_FLIGHT = 5

F32 = jnp.float32
BF16 = jnp.bfloat16
VMEM_LIMIT = 20 * 1024 * 1024
LARGE_LIMIT = 48 * 1024 * 1024
SMEM_SPEC = pl.BlockSpec(memory_space=pltpu.SMEM)


def params(limit=VMEM_LIMIT):
    return pltpu.CompilerParams(vmem_limit_bytes=limit)


SHORT = pl.CostEstimate(flops=10**6, bytes_accessed=10**5, transcendentals=0)


def cost(flops, moved):
    return pl.CostEstimate(flops=int(flops), bytes_accessed=int(moved), transcendentals=0)


def split(x):
    high = x.astype(BF16)
    low = (x - high.astype(F32)).astype(BF16)
    return high, low


def dot(a, b):
    return lax.dot_general(a, b, (((1,), (0,)), ((), ())), preferred_element_type=F32)


def pack_matrix(m):
    high, low = split(m)
    return jnp.concatenate([high, low, high], axis=1)


def slab(refs, c):
    return jnp.concatenate([ref[c] for ref in refs], axis=0)


def pack_field(v):
    high, low = split(v)
    return jnp.concatenate([high, high, low], axis=0)


def coef_table(length):
    c = np.arange(length)[:, None]
    j = np.arange(length)[None, :]
    angle = ((c // 2) * j % length) * (2.0 * math.pi / length)
    table = np.where(c % 2 == 1, np.sin(angle), np.cos(angle)) * math.sqrt(2.0 / length)
    table[0] = 1.0 / math.sqrt(length)
    table[1] = np.where(np.arange(length) % 2 == 0, 1.0, -1.0) / math.sqrt(length)
    high = table.astype(ml_dtypes.bfloat16)
    low = (table - high.astype(np.float64)).astype(ml_dtypes.bfloat16)
    return np.concatenate([high, low], axis=0)


def permute_kernel(peers, pos_ref, table_ref, o_ref):
    planes = table_ref.shape[1]
    per = planes // peers
    me = pos_ref[1]
    row = lax.broadcasted_iota(jnp.int32, (planes, planes), 0)
    col = lax.broadcasted_iota(jnp.int32, (planes, planes), 1)
    swap = jnp.where(row == ((col // per) ^ me) * per + col % per, 1.0, 0.0).astype(BF16)
    for half in range(2):
        rows = pl.ds(half * planes, planes)
        turned = dot(swap, table_ref[rows, :]).astype(BF16)
        o_ref[rows, :] = dot(turned, swap).astype(BF16)


def permuted_table(position, table, peers):
    return pl.pallas_call(
        functools.partial(permute_kernel, peers),
        out_shape=jax.ShapeDtypeStruct(table.shape, BF16),
        in_specs=[SMEM_SPEC, pl.BlockSpec(memory_space=pltpu.VMEM)],
        compiler_params=params(),
        cost_estimate=cost(1e8, 4e6),
        name="permuted_table",
    )(position, table)


def transform_kernel(count, table_ref, *refs):
    planes = table_ref.shape[1]
    both = table_ref[...]
    high_table = both[:planes]
    width = refs[0].shape[-1]
    nodes = refs[0].shape[-2]
    per = planes // count
    flat = [ref.reshape(per * nodes, width) for ref in refs]
    for n in range(nodes):
        rows = pl.ds(n, per, stride=nodes) if nodes > 1 else pl.ds(0, per)
        high, low = split(jnp.concatenate([ref[rows, :] for ref in flat[:count]], axis=0))
        wide = dot(both, high)
        result = wide[:planes] + (wide[planes:] + dot(high_table, low))
        for d, ref in enumerate(flat[count:]):
            ref[rows, :] = result[d * per : (d + 1) * per]


def transform(blocks, table):
    per, nodes, elements = blocks[0].shape
    count = len(blocks)
    width = 128
    block = pl.BlockSpec((per, nodes, width), lambda i: (0, 0, i))
    size = count * blocks[0].size
    return pl.pallas_call(
        functools.partial(transform_kernel, count),
        out_shape=[jax.ShapeDtypeStruct(v.shape, F32) for v in blocks],
        grid=(elements // width,),
        in_specs=[pl.BlockSpec(table.shape, lambda i: (0, 0))] + [block] * count,
        out_specs=[block] * count,
        compiler_params=params(),
        cost_estimate=cost(6 * PLANES * size, 8 * size),
        name="transform",
    )(table, *blocks)


def pack_kernel(pos_ref, *refs):
    count = len(refs) // 2
    for source, target in zip(refs[:count], refs[count:]):
        target[...] = source[0]


def pack(position, adjoint, comp, limit, distances):
    _, per, nodes, elements = adjoint.shape
    lines = len(distances)
    block = per // 2

    def source(d):
        return pl.BlockSpec((1, block, LINE, elements), lambda i, pos: (comp, i, pos[1] ^ d, 0))

    size = per * lines * LINE * elements
    return pl.pallas_call(
        pack_kernel,
        out_shape=[jax.ShapeDtypeStruct((per, LINE, elements), F32)] * lines,
        grid_spec=pltpu.PrefetchScalarGridSpec(
            num_scalar_prefetch=1,
            grid=(per // block,),
            in_specs=[source(d) for d in distances],
            out_specs=[pl.BlockSpec((block, LINE, elements), lambda i, pos: (i, 0, 0))] * lines,
        ),
        compiler_params=params(limit),
        cost_estimate=cost(0, 8 * size),
        name="pack",
    )(position, *[adjoint] * lines)


BXR, BYS, DXBX, DXBY, DYBX, DYBY, DIAG = range(7)


def line_of(me, d):
    return pl.ds(pl.multiple_of((me ^ d) * LINE, LINE), LINE)


def own_order(ref, me, *lead):
    lines = ref.shape[-2] // LINE
    return jnp.concatenate([ref[(*lead, line_of(me, d), slice(None))] for d in range(lines)], axis=0)


def prep_kernel(
    pos_ref, bank_ref, snap_ref, geo_ref, dr_ref, ds_ref, st_ref, up_ref, lo_ref,
    coef_ref, dpack_ref, spack_ref, gather_ref, scatter_ref, mask_ref, face_ref,
):
    elements = geo_ref.shape[1]
    nodes = dr_ref.shape[0]
    lines = nodes // LINE
    me = pos_ref[1]
    row = lax.broadcasted_iota(jnp.int32, (nodes, nodes), 0)
    col = lax.broadcasted_iota(jnp.int32, (nodes, nodes), 1)
    swap = jnp.where(row == ((col // LINE) ^ me) * LINE + col % LINE, 1.0, 0.0).astype(BF16)

    def permuted(ref):
        high, low = split(own_order(ref, me))
        return dot(high, swap) + dot(low, swap)

    snap = snap_ref[...]
    base = [
        sum(
            jnp.where(snap == k, own_order(bank_ref, me, k, i), 0.0)
            for k in range(bank_ref.shape[0])
        )
        for i in range(2)
    ]
    rx = geo_ref[0:1, :]
    sy = geo_ref[1:2, :]
    dpack = pack_matrix(jnp.concatenate([permuted(dr_ref), permuted(ds_ref)], axis=0))
    dpack_ref[...] = dpack
    bx = dot(dpack, pack_field(base[0]))
    by = dot(dpack, pack_field(base[1]))
    coef_ref[BXR] = base[0] * rx
    coef_ref[BYS] = base[1] * sy
    coef_ref[DXBX] = rx * bx[:nodes]
    coef_ref[DXBY] = rx * by[:nodes]
    coef_ref[DYBX] = sy * bx[nodes:]
    coef_ref[DYBY] = sy * by[nodes:]
    diag = jnp.sum(jnp.where(row == col, st_ref[...], 0.0), axis=0, keepdims=True)
    own = ((row // LINE) ^ me) * LINE + row % LINE == col
    diag = jnp.sum(jnp.where(own, diag, 0.0), axis=1, keepdims=True)
    spack_ref[...] = pack_matrix(jnp.where(row == col, 0.0, permuted(st_ref)))
    coef_ref[DIAG] = jnp.broadcast_to(diag, (nodes, elements))
    shared = up_ref.shape[1]
    mass = jnp.broadcast_to(1.0 / (rx * sy), (16, elements))
    for side, (ref, first) in enumerate(((up_ref, LINE - 1), (lo_ref, 0))):
        index = ref[...]
        node = index // elements
        element = index - node * elements
        hot = lax.broadcasted_iota(jnp.int32, (elements, shared), 0) == element
        hot = jnp.where(hot, 1.0, 0.0)
        gather_ref[side] = hot.astype(BF16)
        back = hot.T.astype(BF16)
        scatter_ref[side] = back
        mask = (lax.broadcasted_iota(jnp.int32, (lines, shared), 0) ^ me) == node // LINE
        mask = jnp.where(mask, 1.0, 0.0)
        mask_ref[side] = mask
        high, low = split(mass)
        rest = (mass - high.astype(F32) - low.astype(F32)).astype(BF16)
        at_face = sum(dot(part, gather_ref[side])[:1] for part in (high, low, rest))
        face_ref[side, 0:1, :] = at_face
        lead = jnp.concatenate([diag[s * LINE + first : s * LINE + first + 1] for s in range(lines)], axis=0)
        face_ref[side, 1:2, :] = PENALTY + jnp.sum(mask * lead, axis=0, keepdims=True)
        count = dot(mask.astype(BF16), back)
        for s in range(lines):
            n = s * LINE + first
            coef_ref[DIAG, n : n + 1, :] = coef_ref[DIAG, n : n + 1, :] + PENALTY * count[s : s + 1]


def prepare(position, base_bank, snapshot, geometry, diff_r, diff_s, stiffness, upper, lower):
    nodes = diff_r.shape[0]
    elements = geometry.shape[1]
    shared = upper.shape[1]
    return pl.pallas_call(
        prep_kernel,
        out_shape=[
            jax.ShapeDtypeStruct((7, nodes, elements), F32),
            jax.ShapeDtypeStruct((2 * nodes, 3 * nodes), BF16),
            jax.ShapeDtypeStruct((nodes, 3 * nodes), BF16),
            jax.ShapeDtypeStruct((2, elements, shared), BF16),
            jax.ShapeDtypeStruct((2, shared, elements), BF16),
            jax.ShapeDtypeStruct((2, nodes // LINE, shared), F32),
            jax.ShapeDtypeStruct((2, 2, shared), F32),
        ],
        in_specs=[SMEM_SPEC] + [pl.BlockSpec(memory_space=pltpu.VMEM)] * 8,
        compiler_params=params(),
        cost_estimate=cost(1e7, 8e6),
        name="prepare",
    )(position, base_bank, snapshot.reshape(1, elements), geometry, diff_r, diff_s, stiffness, upper, lower)


def face_of(ref, side):
    rows, elements = ref.shape
    return ref.reshape(rows // LINE, LINE, elements).at[:, LINE - 1 if side == 0 else 0, :]


def gather_faces(side, fields, gather_ref, mask_ref):
    lines = mask_ref.shape[1]
    high, low = split(jnp.concatenate(fields, axis=0))
    rows = high.shape[0]
    both = dot(jnp.concatenate([high, low], axis=0), gather_ref[side])
    picked = both[:rows] + both[rows:]
    shared = picked.shape[1]
    return jnp.sum(picked.reshape(rows // lines, lines, shared) * mask_ref[side][None], axis=1)


def scatter_faces(side, values, scatter_ref, mask_ref):
    mask = mask_ref[side]
    coefs, shared = values.shape
    spread = (values[:, None, :] * mask[None]).reshape(coefs * mask.shape[0], shared)
    high, low = split(spread)
    rows = high.shape[0]
    both = dot(jnp.concatenate([high, low], axis=0), scatter_ref[side])
    return both[:rows] + both[rows:]


def local_sweep(pot, source, inverse, spack):
    applied = dot(spack, pack_field(pot))
    return (1.0 - RELAXATION) * pot + inverse * (source - applied)


def coef_block(coefs, block=8):
    return block if coefs % block == 0 else coefs


def start_kernel(
    block, count, pos_ref, geo_ref, diag_ref, dpack_ref, spack_ref, gather_ref, mask_ref, *refs
):
    z_refs, x_refs = refs[:count], refs[count : 2 * count]
    source_ref, inverse_ref, local_ref, up_ref, lo_ref, pot_ref = refs[2 * count :]
    nodes, elements = diag_ref.shape[1:]
    beta = 4.0 / PLANES
    first = pos_ref[0] * (block * pl.num_programs(0)) + pl.program_id(0) * block
    rx = geo_ref[0:1, :]
    mass = 1.0 / (rx * geo_ref[1:2, :])
    diag = diag_ref[0]
    drpack = dpack_ref[:nodes]
    spack = spack_ref[...]
    for c in range(block):
        index = first + c
        wave = beta * (index // 2).astype(F32)
        shift = beta * jnp.where(index == 1, PLANES // 2, index // 2).astype(F32)
        shift = shift * shift
        z = slab(z_refs, c)
        other = slab(x_refs, c + 1 if c % 2 == 0 else c - 1)
        turned = (wave if c % 2 == 0 else -wave) * other
        source = turned - rx * dot(drpack, pack_field(z))
        inverse = RELAXATION / (diag + shift * mass)
        pot = inverse * source
        rows = pl.ds(c * nodes, nodes)
        source_ref[rows, :] = source
        inverse_ref[rows, :] = inverse
        pot_ref[rows, :] = pot
        local_ref[rows, :] = local_sweep(pot, source, inverse, spack)
    for side, out in ((0, up_ref), (1, lo_ref)):
        fields = [face_of(ref, side)[...] for ref in (pot_ref, local_ref)]
        picked = gather_faces(side, fields, gather_ref, mask_ref)
        for k in range(2):
            out[k] = picked[k * block : (k + 1) * block]


def whole(shape):
    return pl.BlockSpec(shape, lambda *i: (0,) * len(shape))


def start_solve(position, z, x, geometry, coef, dpack, spack, gather, mask):
    coefs, part, elements = z[0].shape
    nodes = len(z) * part
    shared = gather.shape[2]
    block = coef_block(coefs, 16)
    field = [pl.BlockSpec((block, part, elements), lambda i: (i, 0, 0))] * len(z)
    flat = pl.BlockSpec((block * nodes, elements), lambda i: (i, 0))
    face = pl.BlockSpec((2, block, shared), lambda i: (0, i, 0))
    size = coefs * nodes * elements
    return pl.pallas_call(
        functools.partial(start_kernel, block, len(z)),
        out_shape=[jax.ShapeDtypeStruct((coefs * nodes, elements), F32)] * 3
        + [jax.ShapeDtypeStruct((2, coefs, shared), F32)] * 2,
        grid=(coefs // block,),
        in_specs=[
            SMEM_SPEC, whole(geometry.shape),
            pl.BlockSpec((1, nodes, elements), lambda i: (DIAG, 0, 0)),
            whole(dpack.shape), whole(spack.shape), whole(gather.shape), whole(mask.shape),
            *field, *field,
        ],
        out_specs=[flat, flat, flat, face, face],
        scratch_shapes=[pltpu.VMEM((block * nodes, elements), F32)],
        compiler_params=params(),
        cost_estimate=SHORT,
        name="start_solve",
    )(position, geometry, coef, dpack, spack, gather, mask, *z, *x)


def face_inverse(face, first, coefs):
    index = first + lax.broadcasted_iota(jnp.int32, (coefs, 1), 0)
    wave = jnp.where(index == 1, PLANES // 2, index // 2).astype(F32)
    shift = (4.0 / PLANES) * wave
    shift = shift * shift
    return RELAXATION / (face[1:2] + shift * face[0:1])


def sweeps_kernel(
    block, keep, pos_ref, local_ref, source_ref, inverse_ref, own_up_ref, own_lo_ref,
    got_up_ref, got_lo_ref, face_ref, far_up_ref, far_lo_ref, spack_ref, gather_ref, scatter_ref,
    mask_ref, next_ref, up_ref, lo_ref, pot_ref,
):
    nodes = spack_ref.shape[0]
    spack = spack_ref[...]
    lines = block * (nodes // LINE)
    first = pos_ref[0] * (block * pl.num_programs(0)) + pl.program_id(0) * block
    partners = []
    for side, own, got, far in ((0, own_up_ref, got_up_ref, far_up_ref), (1, own_lo_ref, got_lo_ref, far_lo_ref)):
        scale = PENALTY * face_inverse(face_ref[side], first, block)
        now = scale * got[0]
        later = scale * (got[1] + PENALTY * face_inverse(far[...], first, block) * own[0])
        both = scatter_faces(side, jnp.concatenate([now, later], axis=0), scatter_ref, mask_ref)
        partners.append((both[:lines], both[lines:]))
    pot_ref[...] = local_ref[...]
    for side in range(2):
        face = face_of(pot_ref, side)
        face[...] = face[...] + partners[side][0]
    for c in range(block):
        rows = pl.ds(c * nodes, nodes)
        pot_ref[rows, :] = local_sweep(pot_ref[rows, :], source_ref[rows, :], inverse_ref[rows, :], spack)
    for side in range(2):
        face = face_of(pot_ref, side)
        face[...] = face[...] + partners[side][1]
    for c in range(block):
        rows = pl.ds(c * nodes, nodes)
        next_ref[rows, :] = local_sweep(pot_ref[rows, :], source_ref[rows, :], inverse_ref[rows, :], spack)
    for side, out in ((0, up_ref), (1, lo_ref)):
        fields = [face_of(ref, side)[...] for ref in (pot_ref, next_ref)[:keep]]
        picked = gather_faces(side, fields, gather_ref, mask_ref)
        for k in range(keep):
            out[k] = picked[k * block : (k + 1) * block]


def two_sweeps(keep, position, local, source, inverse, own, got, face, far, spack, gather, scatter, mask):
    nodes = spack.shape[0]
    elements = local.shape[1]
    coefs = local.shape[0] // nodes
    shared = gather.shape[2]
    block = coef_block(coefs, 16)
    flat = pl.BlockSpec((block * nodes, elements), lambda i: (i, 0))
    one = pl.BlockSpec((1, block, shared), lambda i: (0, i, 0))
    two = pl.BlockSpec((2, block, shared), lambda i: (0, i, 0))
    kept = pl.BlockSpec((keep, block, shared), lambda i: (0, i, 0))
    size = coefs * nodes * elements
    return pl.pallas_call(
        functools.partial(sweeps_kernel, block, keep),
        out_shape=[jax.ShapeDtypeStruct(local.shape, F32)]
        + [jax.ShapeDtypeStruct((keep, coefs, shared), F32)] * 2,
        grid=(coefs // block,),
        in_specs=[
            SMEM_SPEC, flat, flat, flat, one, one, two, two,
            whole(face.shape), whole(far[0].shape), whole(far[1].shape),
            whole(spack.shape), whole(gather.shape), whole(scatter.shape), whole(mask.shape),
        ],
        out_specs=[flat, kept, kept],
        scratch_shapes=[pltpu.VMEM((block * nodes, elements), F32)],
        compiler_params=params(),
        cost_estimate=SHORT,
        name="two_sweeps",
    )(position, local, source, inverse, *own, *got, face, *far, spack, gather, scatter, mask)


def store_own(ref, me, value, *lead):
    for d in range(value.shape[0] // LINE):
        ref[(*lead, line_of(me, d), slice(None))] = value[d * LINE : (d + 1) * LINE]


def partial_kernel(block, count, coef_ref, dpack_ref, *refs):
    z_refs, x_refs = refs[:count], refs[count : 2 * count]
    px_ref, py_ref, pz_ref = refs[2 * count :]
    nodes = coef_ref.shape[1]
    dpack = dpack_ref[...]
    for c in range(block):
        z = slab(z_refs, c)
        slopes = dot(dpack, pack_field(z))
        moved = coef_ref[BXR] * slopes[:nodes] + coef_ref[BYS] * slopes[nodes:]
        pz_ref[c] = z - TIME_STEP * (moved + INTERACTION * z)
        x = slab(x_refs, c)
        slopes = dot(dpack, pack_field(x))
        moved = coef_ref[BXR] * slopes[:nodes] + coef_ref[BYS] * slopes[nodes:]
        px_ref[c] = x + TIME_STEP * (x * coef_ref[DXBX] - moved - INTERACTION * x)
        py_ref[c] = TIME_STEP * (x * coef_ref[DYBX])


def partial_update(z, x, coef, dpack):
    coefs, part, elements = z[0].shape
    nodes = len(z) * part
    block = coef_block(coefs)
    field = [pl.BlockSpec((block, part, elements), lambda i: (i, 0, 0))] * len(z)
    out = pl.BlockSpec((block, nodes, elements), lambda i: (i, 0, 0))
    return pl.pallas_call(
        functools.partial(partial_kernel, block, len(z)),
        out_shape=[jax.ShapeDtypeStruct((coefs, nodes, elements), F32)] * 3,
        grid=(coefs // block,),
        in_specs=[whole(coef.shape), whole(dpack.shape), *field, *field],
        out_specs=[out] * 3,
        compiler_params=params(),
        cost_estimate=SHORT,
        name="partial_update",
    )(coef, dpack, *z, *x)


def force_kernel(
    block, pos_ref, local_ref, got_up_ref, got_lo_ref, face_ref, geo_ref, dpack_ref,
    scatter_ref, mask_ref, px_ref, pz_ref, o_ref, x_ref, pot_ref,
):
    nodes = dpack_ref.shape[0] // 2
    scale = TIME_STEP * INTERACTION
    me = pos_ref[1]
    pot_ref[...] = local_ref[...]
    first = pos_ref[0] * (block * pl.num_programs(0)) + pl.program_id(0) * block
    for side, got in ((0, got_up_ref), (1, got_lo_ref)):
        face = face_of(pot_ref, side)
        partner = PENALTY * face_inverse(face_ref[side], first, block) * got[0]
        face[...] = face[...] + scatter_faces(side, partner, scatter_ref, mask_ref)
    drpack = dpack_ref[:nodes]
    slope_scale = scale * geo_ref[0:1, :]
    for c in range(block):
        pot = pot_ref[pl.ds(c * nodes, nodes), :]
        slope = dot(drpack, pack_field(pot))
        store_own(o_ref, me, pz_ref[c] - slope_scale * slope, 0, c)
        wave = (4.0 / PLANES) * ((first + c) // 2).astype(F32)
        factor = scale * (wave if c % 2 else -wave)
        other = c - 1 if c % 2 else c + 1
        x_ref[other] = px_ref[other] + factor * pot


def add_force(position, local, got, face, geometry, dpack, scatter, mask, px, pz):
    coefs, nodes, elements = px.shape
    shared = scatter.shape[1]
    block = coef_block(coefs, 16)
    flat = pl.BlockSpec((block * nodes, elements), lambda i: (i, 0))
    one = pl.BlockSpec((1, block, shared), lambda i: (0, i, 0))
    part = pl.BlockSpec((block, nodes, elements), lambda i: (i, 0, 0))
    return pl.pallas_call(
        functools.partial(force_kernel, block),
        out_shape=[
            jax.ShapeDtypeStruct((3, coefs, nodes, elements), F32),
            jax.ShapeDtypeStruct(px.shape, F32),
        ],
        grid=(coefs // block,),
        in_specs=[
            SMEM_SPEC, flat, one, one, whole(face.shape), whole(geometry.shape), whole(dpack.shape),
            whole(scatter.shape), whole(mask.shape), part, part,
        ],
        out_specs=[pl.BlockSpec((1, block, nodes, elements), lambda i: (2, i, 0, 0)), part],
        scratch_shapes=[pltpu.VMEM((block * nodes, elements), F32)],
        compiler_params=params(),
        cost_estimate=SHORT,
        name="add_force",
    )(position, local, *got, face, geometry, dpack, scatter, mask, px, pz)


def finish_kernel(block, count, pos_ref, coef_ref, dpack_ref, px_ref, py_ref, filled_ref, *refs):
    del filled_ref
    y_refs, o_ref = refs[:count], refs[count]
    nodes = coef_ref.shape[1]
    me = pos_ref[1]
    dpack = dpack_ref[...]
    for c in range(block):
        y = slab(y_refs, c)
        slopes = dot(dpack, pack_field(y))
        moved = coef_ref[BXR] * slopes[:nodes] + coef_ref[BYS] * slopes[nodes:]
        change = y + TIME_STEP * (y * coef_ref[DYBY] - moved)
        store_own(o_ref, me, py_ref[c] + change, 1, c)
        store_own(o_ref, me, px_ref[c] + TIME_STEP * (y * coef_ref[DXBY]), 0, c)


def finish(position, y, coef, dpack, px, py, filled):
    coefs, part, elements = y[0].shape
    nodes = len(y) * part
    block = coef_block(coefs)
    field = pl.BlockSpec((block, part, elements), lambda i: (i, 0, 0))
    own = pl.BlockSpec((block, nodes, elements), lambda i: (i, 0, 0))
    return pl.pallas_call(
        functools.partial(finish_kernel, block, len(y)),
        out_shape=jax.ShapeDtypeStruct(filled.shape, F32),
        grid=(coefs // block,),
        in_specs=[
            SMEM_SPEC, whole(coef.shape), whole(dpack.shape), own, own,
            pl.BlockSpec(memory_space=pl.ANY), *[field] * len(y),
        ],
        out_specs=pl.BlockSpec((2, block, nodes, elements), lambda i: (0, i, 0, 0)),
        input_output_aliases={5: 0},
        compiler_params=params(),
        cost_estimate=SHORT,
        name="finish",
    )(position, coef, dpack, px, py, filled, *y)


def to_all(blocks):
    return lax.all_to_all(blocks, "four", split_axis=0, concat_axis=0, tiled=True)


def swap_faces(up, lo):
    peers = lax.axis_size("dom")
    up_way = [(i, (i + 1) % peers) for i in range(peers)]
    down_way = [(j, i) for i, j in up_way]
    return lax.ppermute(lo, "dom", down_way), lax.ppermute(up, "dom", up_way)


class Exchange:
    def __init__(self, blocks, flight):
        self.blocks = list(blocks)
        self.flight = flight
        self.places = {}
        self.order = sorted(range(1, len(self.blocks)), key=lambda d: (d < 2, d % 2, d))

    def hold(self, value):
        if len(self.places) < len(self.order):
            d = self.order[len(self.places)]
            self.blocks[d], value = lax.optimization_barrier((self.blocks[d], value))
        return value

    def send(self, count):
        for d in self.order[len(self.places) :][:count]:
            block = self.blocks[d]
            if len(self.flight) >= IN_FLIGHT:
                block, self.flight[-IN_FLIGHT] = lax.optimization_barrier((block, self.flight[-IN_FLIGHT]))
            pairs = [(i, i ^ d) for i in range(len(self.blocks))]
            self.places[d] = len(self.flight)
            self.flight.append(lax.ppermute(block, "four", pairs))

    def after(self, value, first, last):
        for d in self.order[first:last]:
            place = self.places[d]
            value, self.flight[place] = lax.optimization_barrier((value, self.flight[place]))
        return value

    def got(self):
        return [self.blocks[0]] + [self.flight[self.places[d]] for d in range(1, len(self.blocks))]


class Whole(Exchange):
    def __init__(self, blocks, exchange):
        super().__init__(blocks[:1], [])
        self.exchange = exchange

    def got(self):
        return self.exchange(self.blocks[0])


def per_device(
    adjoint, base_bank, snapshot, geometry, diff_r, diff_s, stiffness, upper_list, lower_list
):
    _, per, nodes, elements = adjoint.shape
    peers = lax.axis_size("four")
    lines = nodes // LINE
    direct = peers == lines
    place = lax.axis_index("four").astype(jnp.int32)
    position = jnp.stack([place, place if direct else jnp.zeros_like(place)])
    natural = jnp.asarray(coef_table(PLANES))
    table = permuted_table(position, natural, lines)
    flight = []
    share = nodes // peers

    def columns(comp):
        if direct:
            if comp != 2:
                return pack(position, adjoint, comp, VMEM_LIMIT, range(lines))
            early = (2, 4, 6)
            late = [d for d in range(lines) if d not in early]
            got = dict(zip(early, pack(position, adjoint, comp, LARGE_LIMIT, early)))
            got.update(zip(late, pack(position, adjoint, comp, LARGE_LIMIT, late)))
            return [got[d] for d in range(lines)]
        return [jnp.moveaxis(adjoint[comp].reshape(per, peers, share, elements), 1, 0)]

    def gather_planes(block):
        return [to_all(block).reshape(PLANES, share, elements)]

    def gather_lines(block):
        got = jnp.moveaxis(to_all(block.reshape(peers, per, share, elements)), 0, 1)
        got = got.reshape(per, lines, LINE, elements)
        return [got[:, d] for d in range(lines)]

    def spread(blocks):
        return Exchange(blocks, flight) if direct else Whole(blocks, gather_planes)

    def collect(blocks):
        return Exchange(blocks, flight) if direct else Whole(blocks, gather_lines)

    z_out = spread(columns(2))
    z_out.send(3)
    *constants, face = prepare(
        position, base_bank, snapshot, geometry, diff_r, diff_s, stiffness, upper_list, lower_list
    )
    coef, dpack, spack, gather, scatter, mask = constants
    far = z_out.hold(swap_faces(face[0], face[1]))
    z_out.send(4)
    x_out = spread(columns(0))
    table = x_out.hold(table)
    x_out.send(5)
    z_coefs = x_out.hold(transform(z_out.got(), table))
    x_out.send(2)
    y_blocks = columns(1)
    z_back = collect(z_coefs)
    z_back.send(5)
    x_coefs, y_blocks = z_back.hold((transform(x_out.got(), table), y_blocks))
    z_back.send(2)
    x_back = collect(x_coefs)
    x_back.send(7)
    y_out = spread(y_blocks)
    y_out.send(7)
    z = z_back.got()
    x = x_back.got()
    source, inverse, local, up, lo = start_solve(
        position, z, x, geometry, coef, dpack, spack, gather, mask
    )
    got = swap_faces(up, lo)
    parts = partial_update(z, x, coef, dpack)
    local, (px, py, pz) = lax.optimization_barrier((local, parts))
    local = y_out.after(local, 2, 3)
    local, up, lo = two_sweeps(
        2, position, local, source, inverse, (up, lo), got, face, far, spack, gather, scatter, mask
    )
    y_got = list(y_out.got())
    y_got[0], local = lax.optimization_barrier((y_got[0], local))
    got = swap_faces(up, lo)
    y_back = collect(transform(y_got, table))
    y_back.send(7)
    local = y_back.after(local, 0, 2)
    local, up, lo = two_sweeps(
        1, position, local, source, inverse, (up, lo), got, face, far, spack, gather, scatter, mask
    )
    up, lo = y_back.after((up, lo), 2, 4)
    got = swap_faces(up, lo)
    local = y_back.after(local, 4, 5)
    filled, px = add_force(position, local, got, face, geometry, dpack, scatter, mask, px, pz)
    return finish(position, y_back.got(), coef, dpack, px, py, filled)


def solution(mesh):
    in_specs = (
        P(None, "four", None, "dom"),
        P(None, None, None, "dom"),
        P("dom"),
        P(None, "dom"),
        P(),
        P(),
        P(),
        P("dom", None),
        P("dom", None),
    )
    out_specs = P(None, "four", None, "dom")
    return jax.shard_map(
        per_device, mesh=mesh, in_specs=in_specs, out_specs=out_specs, check_vma=False
    )
```

```python
import functools
import math

import jax
import jax.numpy as jnp
import ml_dtypes
import numpy as np
from jax import lax
from jax.experimental import pallas as pl
from jax.experimental.pallas import tpu as pltpu
from jax.sharding import PartitionSpec as P

PLANES = 256
PENALTY = 0.5
RELAXATION = 0.8
TIME_STEP = 0.2
INTERACTION = 2.0
LINE = 8
IN_FLIGHT = 5

F32 = jnp.float32
BF16 = jnp.bfloat16
VMEM_LIMIT = 20 * 1024 * 1024
LARGE_LIMIT = 48 * 1024 * 1024
SMEM_SPEC = pl.BlockSpec(memory_space=pltpu.SMEM)


def params(limit=VMEM_LIMIT):
    return pltpu.CompilerParams(vmem_limit_bytes=limit)


SHORT = pl.CostEstimate(flops=10**6, bytes_accessed=10**5, transcendentals=0)


def cost(flops, moved):
    return pl.CostEstimate(flops=int(flops), bytes_accessed=int(moved), transcendentals=0)


def split(x):
    high = x.astype(BF16)
    low = (x - high.astype(F32)).astype(BF16)
    return high, low


def dot(a, b):
    return lax.dot_general(a, b, (((1,), (0,)), ((), ())), preferred_element_type=F32)


def pack_matrix(m):
    high, low = split(m)
    return jnp.concatenate([high, low, high], axis=1)


def slab(refs, c):
    return jnp.concatenate([ref[c] for ref in refs], axis=0)


def pack_field(v):
    high, low = split(v)
    return jnp.concatenate([high, high, low], axis=0)


def coef_table(length):
    c = np.arange(length)[:, None]
    j = np.arange(length)[None, :]
    angle = ((c // 2) * j % length) * (2.0 * math.pi / length)
    table = np.where(c % 2 == 1, np.sin(angle), np.cos(angle)) * math.sqrt(2.0 / length)
    table[0] = 1.0 / math.sqrt(length)
    table[1] = np.where(np.arange(length) % 2 == 0, 1.0, -1.0) / math.sqrt(length)
    high = table.astype(ml_dtypes.bfloat16)
    low = (table - high.astype(np.float64)).astype(ml_dtypes.bfloat16)
    return np.concatenate([high, low], axis=0)


def permute_kernel(peers, pos_ref, table_ref, o_ref):
    planes = table_ref.shape[1]
    per = planes // peers
    me = pos_ref[1]
    row = lax.broadcasted_iota(jnp.int32, (planes, planes), 0)
    col = lax.broadcasted_iota(jnp.int32, (planes, planes), 1)
    swap = jnp.where(row == ((col // per) ^ me) * per + col % per, 1.0, 0.0).astype(BF16)
    for half in range(2):
        rows = pl.ds(half * planes, planes)
        turned = dot(swap, table_ref[rows, :]).astype(BF16)
        o_ref[rows, :] = dot(turned, swap).astype(BF16)


def permuted_table(position, table, peers):
    return pl.pallas_call(
        functools.partial(permute_kernel, peers),
        out_shape=jax.ShapeDtypeStruct(table.shape, BF16),
        in_specs=[SMEM_SPEC, pl.BlockSpec(memory_space=pltpu.VMEM)],
        compiler_params=params(),
        cost_estimate=cost(1e8, 4e6),
        name="permuted_table",
    )(position, table)


def transform_kernel(count, table_ref, *refs):
    planes = table_ref.shape[1]
    both = table_ref[...]
    high_table = both[:planes]
    width = refs[0].shape[-1]
    nodes = refs[0].shape[-2]
    per = planes // count
    flat = [ref.reshape(per * nodes, width) for ref in refs]
    for n in range(nodes):
        rows = pl.ds(n, per, stride=nodes) if nodes > 1 else pl.ds(0, per)
        high, low = split(jnp.concatenate([ref[rows, :] for ref in flat[:count]], axis=0))
        wide = dot(both, high)
        result = wide[:planes] + (wide[planes:] + dot(high_table, low))
        for d, ref in enumerate(flat[count:]):
            ref[rows, :] = result[d * per : (d + 1) * per]


def transform(blocks, table):
    per, nodes, elements = blocks[0].shape
    count = len(blocks)
    width = 128
    block = pl.BlockSpec((per, nodes, width), lambda i: (0, 0, i))
    size = count * blocks[0].size
    return pl.pallas_call(
        functools.partial(transform_kernel, count),
        out_shape=[jax.ShapeDtypeStruct(v.shape, F32) for v in blocks],
        grid=(elements // width,),
        in_specs=[pl.BlockSpec(table.shape, lambda i: (0, 0))] + [block] * count,
        out_specs=[block] * count,
        compiler_params=params(),
        cost_estimate=cost(6 * PLANES * size, 8 * size),
        name="transform",
    )(table, *blocks)


def pack_kernel(pos_ref, *refs):
    count = len(refs) // 2
    for source, target in zip(refs[:count], refs[count:]):
        target[...] = source[0]


def pack(position, adjoint, comp, limit):
    _, per, nodes, elements = adjoint.shape
    lines = nodes // LINE
    block = per // 2

    def source(d):
        return pl.BlockSpec((1, block, LINE, elements), lambda i, pos: (comp, i, pos[1] ^ d, 0))

    size = per * nodes * elements
    return pl.pallas_call(
        pack_kernel,
        out_shape=[jax.ShapeDtypeStruct((per, LINE, elements), F32)] * lines,
        grid_spec=pltpu.PrefetchScalarGridSpec(
            num_scalar_prefetch=1,
            grid=(per // block,),
            in_specs=[source(d) for d in range(lines)],
            out_specs=[pl.BlockSpec((block, LINE, elements), lambda i, pos: (i, 0, 0))] * lines,
        ),
        compiler_params=params(limit),
        cost_estimate=cost(0, 8 * size),
        name="pack",
    )(position, *[adjoint] * lines)


BXR, BYS, DXBX, DXBY, DYBX, DYBY, DIAG = range(7)


def line_of(me, d):
    return pl.ds(pl.multiple_of((me ^ d) * LINE, LINE), LINE)


def own_order(ref, me, *lead):
    lines = ref.shape[-2] // LINE
    return jnp.concatenate([ref[(*lead, line_of(me, d), slice(None))] for d in range(lines)], axis=0)


def prep_kernel(
    pos_ref, bank_ref, snap_ref, geo_ref, dr_ref, ds_ref, st_ref, up_ref, lo_ref,
    coef_ref, dpack_ref, spack_ref, gather_ref, scatter_ref, mask_ref, face_ref,
):
    elements = geo_ref.shape[1]
    nodes = dr_ref.shape[0]
    lines = nodes // LINE
    me = pos_ref[1]
    row = lax.broadcasted_iota(jnp.int32, (nodes, nodes), 0)
    col = lax.broadcasted_iota(jnp.int32, (nodes, nodes), 1)
    swap = jnp.where(row == ((col // LINE) ^ me) * LINE + col % LINE, 1.0, 0.0).astype(BF16)

    def permuted(ref):
        high, low = split(own_order(ref, me))
        return dot(high, swap) + dot(low, swap)

    snap = snap_ref[...]
    base = [
        sum(
            jnp.where(snap == k, own_order(bank_ref, me, k, i), 0.0)
            for k in range(bank_ref.shape[0])
        )
        for i in range(2)
    ]
    rx = geo_ref[0:1, :]
    sy = geo_ref[1:2, :]
    dpack = pack_matrix(jnp.concatenate([permuted(dr_ref), permuted(ds_ref)], axis=0))
    dpack_ref[...] = dpack
    bx = dot(dpack, pack_field(base[0]))
    by = dot(dpack, pack_field(base[1]))
    coef_ref[BXR] = base[0] * rx
    coef_ref[BYS] = base[1] * sy
    coef_ref[DXBX] = rx * bx[:nodes]
    coef_ref[DXBY] = rx * by[:nodes]
    coef_ref[DYBX] = sy * bx[nodes:]
    coef_ref[DYBY] = sy * by[nodes:]
    diag = jnp.sum(jnp.where(row == col, st_ref[...], 0.0), axis=0, keepdims=True)
    own = ((row // LINE) ^ me) * LINE + row % LINE == col
    diag = jnp.sum(jnp.where(own, diag, 0.0), axis=1, keepdims=True)
    spack_ref[...] = pack_matrix(jnp.where(row == col, 0.0, permuted(st_ref)))
    coef_ref[DIAG] = jnp.broadcast_to(diag, (nodes, elements))
    shared = up_ref.shape[1]
    mass = jnp.broadcast_to(1.0 / (rx * sy), (16, elements))
    for side, (ref, first) in enumerate(((up_ref, LINE - 1), (lo_ref, 0))):
        index = ref[...]
        node = index // elements
        element = index - node * elements
        hot = lax.broadcasted_iota(jnp.int32, (elements, shared), 0) == element
        hot = jnp.where(hot, 1.0, 0.0)
        gather_ref[side] = hot.astype(BF16)
        back = hot.T.astype(BF16)
        scatter_ref[side] = back
        mask = (lax.broadcasted_iota(jnp.int32, (lines, shared), 0) ^ me) == node // LINE
        mask = jnp.where(mask, 1.0, 0.0)
        mask_ref[side] = mask
        high, low = split(mass)
        rest = (mass - high.astype(F32) - low.astype(F32)).astype(BF16)
        at_face = sum(dot(part, gather_ref[side])[:1] for part in (high, low, rest))
        face_ref[side, 0:1, :] = at_face
        lead = jnp.concatenate([diag[s * LINE + first : s * LINE + first + 1] for s in range(lines)], axis=0)
        face_ref[side, 1:2, :] = PENALTY + jnp.sum(mask * lead, axis=0, keepdims=True)
        count = dot(mask.astype(BF16), back)
        for s in range(lines):
            n = s * LINE + first
            coef_ref[DIAG, n : n + 1, :] = coef_ref[DIAG, n : n + 1, :] + PENALTY * count[s : s + 1]


def prepare(position, base_bank, snapshot, geometry, diff_r, diff_s, stiffness, upper, lower):
    nodes = diff_r.shape[0]
    elements = geometry.shape[1]
    shared = upper.shape[1]
    return pl.pallas_call(
        prep_kernel,
        out_shape=[
            jax.ShapeDtypeStruct((7, nodes, elements), F32),
            jax.ShapeDtypeStruct((2 * nodes, 3 * nodes), BF16),
            jax.ShapeDtypeStruct((nodes, 3 * nodes), BF16),
            jax.ShapeDtypeStruct((2, elements, shared), BF16),
            jax.ShapeDtypeStruct((2, shared, elements), BF16),
            jax.ShapeDtypeStruct((2, nodes // LINE, shared), F32),
            jax.ShapeDtypeStruct((2, 2, shared), F32),
        ],
        in_specs=[SMEM_SPEC] + [pl.BlockSpec(memory_space=pltpu.VMEM)] * 8,
        compiler_params=params(),
        cost_estimate=cost(1e7, 8e6),
        name="prepare",
    )(position, base_bank, snapshot.reshape(1, elements), geometry, diff_r, diff_s, stiffness, upper, lower)


def face_of(ref, side):
    rows, elements = ref.shape
    return ref.reshape(rows // LINE, LINE, elements).at[:, LINE - 1 if side == 0 else 0, :]


def gather_faces(side, fields, gather_ref, mask_ref):
    lines = mask_ref.shape[1]
    high, low = split(jnp.concatenate(fields, axis=0))
    rows = high.shape[0]
    both = dot(jnp.concatenate([high, low], axis=0), gather_ref[side])
    picked = both[:rows] + both[rows:]
    shared = picked.shape[1]
    return jnp.sum(picked.reshape(rows // lines, lines, shared) * mask_ref[side][None], axis=1)


def scatter_faces(side, values, scatter_ref, mask_ref):
    mask = mask_ref[side]
    coefs, shared = values.shape
    spread = (values[:, None, :] * mask[None]).reshape(coefs * mask.shape[0], shared)
    high, low = split(spread)
    rows = high.shape[0]
    both = dot(jnp.concatenate([high, low], axis=0), scatter_ref[side])
    return both[:rows] + both[rows:]


def local_sweep(pot, source, inverse, spack):
    applied = dot(spack, pack_field(pot))
    return (1.0 - RELAXATION) * pot + inverse * (source - applied)


def coef_block(coefs, block=8):
    return block if coefs % block == 0 else coefs


def start_kernel(
    block, count, pos_ref, geo_ref, diag_ref, dpack_ref, spack_ref, gather_ref, mask_ref, *refs
):
    z_refs, x_refs = refs[:count], refs[count : 2 * count]
    source_ref, inverse_ref, local_ref, up_ref, lo_ref, pot_ref = refs[2 * count :]
    nodes, elements = diag_ref.shape[1:]
    beta = 4.0 / PLANES
    first = pos_ref[0] * (block * pl.num_programs(0)) + pl.program_id(0) * block
    rx = geo_ref[0:1, :]
    mass = 1.0 / (rx * geo_ref[1:2, :])
    diag = diag_ref[0]
    drpack = dpack_ref[:nodes]
    spack = spack_ref[...]
    for c in range(block):
        index = first + c
        wave = beta * (index // 2).astype(F32)
        shift = beta * jnp.where(index == 1, PLANES // 2, index // 2).astype(F32)
        shift = shift * shift
        z = slab(z_refs, c)
        other = slab(x_refs, c + 1 if c % 2 == 0 else c - 1)
        turned = (wave if c % 2 == 0 else -wave) * other
        source = turned - rx * dot(drpack, pack_field(z))
        inverse = RELAXATION / (diag + shift * mass)
        pot = inverse * source
        rows = pl.ds(c * nodes, nodes)
        source_ref[rows, :] = source
        inverse_ref[rows, :] = inverse
        pot_ref[rows, :] = pot
        local_ref[rows, :] = local_sweep(pot, source, inverse, spack)
    for side, out in ((0, up_ref), (1, lo_ref)):
        fields = [face_of(ref, side)[...] for ref in (pot_ref, local_ref)]
        picked = gather_faces(side, fields, gather_ref, mask_ref)
        for k in range(2):
            out[k] = picked[k * block : (k + 1) * block]


def whole(shape):
    return pl.BlockSpec(shape, lambda *i: (0,) * len(shape))


def start_solve(position, z, x, geometry, coef, dpack, spack, gather, mask):
    coefs, part, elements = z[0].shape
    nodes = len(z) * part
    shared = gather.shape[2]
    block = coef_block(coefs, 16)
    field = [pl.BlockSpec((block, part, elements), lambda i: (i, 0, 0))] * len(z)
    flat = pl.BlockSpec((block * nodes, elements), lambda i: (i, 0))
    face = pl.BlockSpec((2, block, shared), lambda i: (0, i, 0))
    size = coefs * nodes * elements
    return pl.pallas_call(
        functools.partial(start_kernel, block, len(z)),
        out_shape=[jax.ShapeDtypeStruct((coefs * nodes, elements), F32)] * 3
        + [jax.ShapeDtypeStruct((2, coefs, shared), F32)] * 2,
        grid=(coefs // block,),
        in_specs=[
            SMEM_SPEC, whole(geometry.shape),
            pl.BlockSpec((1, nodes, elements), lambda i: (DIAG, 0, 0)),
            whole(dpack.shape), whole(spack.shape), whole(gather.shape), whole(mask.shape),
            *field, *field,
        ],
        out_specs=[flat, flat, flat, face, face],
        scratch_shapes=[pltpu.VMEM((block * nodes, elements), F32)],
        compiler_params=params(),
        cost_estimate=SHORT,
        name="start_solve",
    )(position, geometry, coef, dpack, spack, gather, mask, *z, *x)


def face_inverse(face, first, coefs):
    index = first + lax.broadcasted_iota(jnp.int32, (coefs, 1), 0)
    wave = jnp.where(index == 1, PLANES // 2, index // 2).astype(F32)
    shift = (4.0 / PLANES) * wave
    shift = shift * shift
    return RELAXATION / (face[1:2] + shift * face[0:1])


def sweeps_kernel(
    block, keep, pos_ref, local_ref, source_ref, inverse_ref, own_up_ref, own_lo_ref,
    got_up_ref, got_lo_ref, face_ref, far_up_ref, far_lo_ref, spack_ref, gather_ref, scatter_ref,
    mask_ref, next_ref, up_ref, lo_ref, pot_ref,
):
    nodes = spack_ref.shape[0]
    spack = spack_ref[...]
    lines = block * (nodes // LINE)
    first = pos_ref[0] * (block * pl.num_programs(0)) + pl.program_id(0) * block
    partners = []
    for side, own, got, far in ((0, own_up_ref, got_up_ref, far_up_ref), (1, own_lo_ref, got_lo_ref, far_lo_ref)):
        scale = PENALTY * face_inverse(face_ref[side], first, block)
        now = scale * got[0]
        later = scale * (got[1] + PENALTY * face_inverse(far[...], first, block) * own[0])
        both = scatter_faces(side, jnp.concatenate([now, later], axis=0), scatter_ref, mask_ref)
        partners.append((both[:lines], both[lines:]))
    pot_ref[...] = local_ref[...]
    for side in range(2):
        face = face_of(pot_ref, side)
        face[...] = face[...] + partners[side][0]
    for c in range(block):
        rows = pl.ds(c * nodes, nodes)
        pot_ref[rows, :] = local_sweep(pot_ref[rows, :], source_ref[rows, :], inverse_ref[rows, :], spack)
    for side in range(2):
        face = face_of(pot_ref, side)
        face[...] = face[...] + partners[side][1]
    for c in range(block):
        rows = pl.ds(c * nodes, nodes)
        next_ref[rows, :] = local_sweep(pot_ref[rows, :], source_ref[rows, :], inverse_ref[rows, :], spack)
    for side, out in ((0, up_ref), (1, lo_ref)):
        fields = [face_of(ref, side)[...] for ref in (pot_ref, next_ref)[:keep]]
        picked = gather_faces(side, fields, gather_ref, mask_ref)
        for k in range(keep):
            out[k] = picked[k * block : (k + 1) * block]


def two_sweeps(keep, position, local, source, inverse, own, got, face, far, spack, gather, scatter, mask):
    nodes = spack.shape[0]
    elements = local.shape[1]
    coefs = local.shape[0] // nodes
    shared = gather.shape[2]
    block = coef_block(coefs, 16)
    flat = pl.BlockSpec((block * nodes, elements), lambda i: (i, 0))
    one = pl.BlockSpec((1, block, shared), lambda i: (0, i, 0))
    two = pl.BlockSpec((2, block, shared), lambda i: (0, i, 0))
    kept = pl.BlockSpec((keep, block, shared), lambda i: (0, i, 0))
    size = coefs * nodes * elements
    return pl.pallas_call(
        functools.partial(sweeps_kernel, block, keep),
        out_shape=[jax.ShapeDtypeStruct(local.shape, F32)]
        + [jax.ShapeDtypeStruct((keep, coefs, shared), F32)] * 2,
        grid=(coefs // block,),
        in_specs=[
            SMEM_SPEC, flat, flat, flat, one, one, two, two,
            whole(face.shape), whole(far[0].shape), whole(far[1].shape),
            whole(spack.shape), whole(gather.shape), whole(scatter.shape), whole(mask.shape),
        ],
        out_specs=[flat, kept, kept],
        scratch_shapes=[pltpu.VMEM((block * nodes, elements), F32)],
        compiler_params=params(),
        cost_estimate=SHORT,
        name="two_sweeps",
    )(position, local, source, inverse, *own, *got, face, *far, spack, gather, scatter, mask)


def store_own(ref, me, value, *lead):
    for d in range(value.shape[0] // LINE):
        ref[(*lead, line_of(me, d), slice(None))] = value[d * LINE : (d + 1) * LINE]


def partial_kernel(block, count, coef_ref, dpack_ref, *refs):
    z_refs, x_refs = refs[:count], refs[count : 2 * count]
    px_ref, py_ref, pz_ref = refs[2 * count :]
    nodes = coef_ref.shape[1]
    dpack = dpack_ref[...]
    for c in range(block):
        z = slab(z_refs, c)
        slopes = dot(dpack, pack_field(z))
        moved = coef_ref[BXR] * slopes[:nodes] + coef_ref[BYS] * slopes[nodes:]
        pz_ref[c] = z - TIME_STEP * (moved + INTERACTION * z)
        x = slab(x_refs, c)
        slopes = dot(dpack, pack_field(x))
        moved = coef_ref[BXR] * slopes[:nodes] + coef_ref[BYS] * slopes[nodes:]
        px_ref[c] = x + TIME_STEP * (x * coef_ref[DXBX] - moved - INTERACTION * x)
        py_ref[c] = TIME_STEP * (x * coef_ref[DYBX])


def partial_update(z, x, coef, dpack):
    coefs, part, elements = z[0].shape
    nodes = len(z) * part
    block = coef_block(coefs)
    field = [pl.BlockSpec((block, part, elements), lambda i: (i, 0, 0))] * len(z)
    out = pl.BlockSpec((block, nodes, elements), lambda i: (i, 0, 0))
    return pl.pallas_call(
        functools.partial(partial_kernel, block, len(z)),
        out_shape=[jax.ShapeDtypeStruct((coefs, nodes, elements), F32)] * 3,
        grid=(coefs // block,),
        in_specs=[whole(coef.shape), whole(dpack.shape), *field, *field],
        out_specs=[out] * 3,
        compiler_params=params(),
        cost_estimate=SHORT,
        name="partial_update",
    )(coef, dpack, *z, *x)


def force_kernel(
    block, pos_ref, local_ref, got_up_ref, got_lo_ref, face_ref, geo_ref, dpack_ref,
    scatter_ref, mask_ref, px_ref, pz_ref, o_ref, x_ref, pot_ref,
):
    nodes = dpack_ref.shape[0] // 2
    scale = TIME_STEP * INTERACTION
    me = pos_ref[1]
    pot_ref[...] = local_ref[...]
    first = pos_ref[0] * (block * pl.num_programs(0)) + pl.program_id(0) * block
    for side, got in ((0, got_up_ref), (1, got_lo_ref)):
        face = face_of(pot_ref, side)
        partner = PENALTY * face_inverse(face_ref[side], first, block) * got[0]
        face[...] = face[...] + scatter_faces(side, partner, scatter_ref, mask_ref)
    drpack = dpack_ref[:nodes]
    slope_scale = scale * geo_ref[0:1, :]
    for c in range(block):
        pot = pot_ref[pl.ds(c * nodes, nodes), :]
        slope = dot(drpack, pack_field(pot))
        store_own(o_ref, me, pz_ref[c] - slope_scale * slope, 0, c)
        wave = (4.0 / PLANES) * ((first + c) // 2).astype(F32)
        factor = scale * (wave if c % 2 else -wave)
        other = c - 1 if c % 2 else c + 1
        x_ref[other] = px_ref[other] + factor * pot


def add_force(position, local, got, face, geometry, dpack, scatter, mask, px, pz):
    coefs, nodes, elements = px.shape
    shared = scatter.shape[1]
    block = coef_block(coefs, 16)
    flat = pl.BlockSpec((block * nodes, elements), lambda i: (i, 0))
    one = pl.BlockSpec((1, block, shared), lambda i: (0, i, 0))
    part = pl.BlockSpec((block, nodes, elements), lambda i: (i, 0, 0))
    return pl.pallas_call(
        functools.partial(force_kernel, block),
        out_shape=[
            jax.ShapeDtypeStruct((3, coefs, nodes, elements), F32),
            jax.ShapeDtypeStruct(px.shape, F32),
        ],
        grid=(coefs // block,),
        in_specs=[
            SMEM_SPEC, flat, one, one, whole(face.shape), whole(geometry.shape), whole(dpack.shape),
            whole(scatter.shape), whole(mask.shape), part, part,
        ],
        out_specs=[pl.BlockSpec((1, block, nodes, elements), lambda i: (2, i, 0, 0)), part],
        scratch_shapes=[pltpu.VMEM((block * nodes, elements), F32)],
        compiler_params=params(),
        cost_estimate=SHORT,
        name="add_force",
    )(position, local, *got, face, geometry, dpack, scatter, mask, px, pz)


def finish_kernel(block, count, pos_ref, coef_ref, dpack_ref, px_ref, py_ref, filled_ref, *refs):
    del filled_ref
    y_refs, o_ref = refs[:count], refs[count]
    nodes = coef_ref.shape[1]
    me = pos_ref[1]
    dpack = dpack_ref[...]
    for c in range(block):
        y = slab(y_refs, c)
        slopes = dot(dpack, pack_field(y))
        moved = coef_ref[BXR] * slopes[:nodes] + coef_ref[BYS] * slopes[nodes:]
        change = y + TIME_STEP * (y * coef_ref[DYBY] - moved)
        store_own(o_ref, me, py_ref[c] + change, 1, c)
        store_own(o_ref, me, px_ref[c] + TIME_STEP * (y * coef_ref[DXBY]), 0, c)


def finish(position, y, coef, dpack, px, py, filled):
    coefs, part, elements = y[0].shape
    nodes = len(y) * part
    block = coef_block(coefs)
    field = pl.BlockSpec((block, part, elements), lambda i: (i, 0, 0))
    own = pl.BlockSpec((block, nodes, elements), lambda i: (i, 0, 0))
    return pl.pallas_call(
        functools.partial(finish_kernel, block, len(y)),
        out_shape=jax.ShapeDtypeStruct(filled.shape, F32),
        grid=(coefs // block,),
        in_specs=[
            SMEM_SPEC, whole(coef.shape), whole(dpack.shape), own, own,
            pl.BlockSpec(memory_space=pl.ANY), *[field] * len(y),
        ],
        out_specs=pl.BlockSpec((2, block, nodes, elements), lambda i: (0, i, 0, 0)),
        input_output_aliases={5: 0},
        compiler_params=params(),
        cost_estimate=SHORT,
        name="finish",
    )(position, coef, dpack, px, py, filled, *y)


def to_all(blocks):
    return lax.all_to_all(blocks, "four", split_axis=0, concat_axis=0, tiled=True)


def swap_faces(up, lo):
    peers = lax.axis_size("dom")
    up_way = [(i, (i + 1) % peers) for i in range(peers)]
    down_way = [(j, i) for i, j in up_way]
    return lax.ppermute(lo, "dom", down_way), lax.ppermute(up, "dom", up_way)


class Exchange:
    def __init__(self, blocks, flight):
        self.blocks = list(blocks)
        self.flight = flight
        self.places = {}
        self.order = sorted(range(1, len(self.blocks)), key=lambda d: (d < 2, d % 2, d))

    def hold(self, value):
        if len(self.places) < len(self.order):
            d = self.order[len(self.places)]
            self.blocks[d], value = lax.optimization_barrier((self.blocks[d], value))
        return value

    def send(self, count):
        for d in self.order[len(self.places) :][:count]:
            block = self.blocks[d]
            if len(self.flight) >= IN_FLIGHT:
                block, self.flight[-IN_FLIGHT] = lax.optimization_barrier((block, self.flight[-IN_FLIGHT]))
            pairs = [(i, i ^ d) for i in range(len(self.blocks))]
            self.places[d] = len(self.flight)
            self.flight.append(lax.ppermute(block, "four", pairs))

    def after(self, value, first, last):
        for d in self.order[first:last]:
            place = self.places[d]
            value, self.flight[place] = lax.optimization_barrier((value, self.flight[place]))
        return value

    def got(self):
        return [self.blocks[0]] + [self.flight[self.places[d]] for d in range(1, len(self.blocks))]


class Whole(Exchange):
    def __init__(self, blocks, exchange):
        super().__init__(blocks[:1], [])
        self.exchange = exchange

    def got(self):
        return self.exchange(self.blocks[0])


def per_device(
    adjoint, base_bank, snapshot, geometry, diff_r, diff_s, stiffness, upper_list, lower_list
):
    _, per, nodes, elements = adjoint.shape
    peers = lax.axis_size("four")
    lines = nodes // LINE
    direct = peers == lines
    place = lax.axis_index("four").astype(jnp.int32)
    position = jnp.stack([place, place if direct else jnp.zeros_like(place)])
    natural = jnp.asarray(coef_table(PLANES))
    table = permuted_table(position, natural, lines)
    flight = []
    share = nodes // peers

    def columns(comp):
        if direct:
            return pack(position, adjoint, comp, LARGE_LIMIT if comp == 2 else VMEM_LIMIT)
        return [jnp.moveaxis(adjoint[comp].reshape(per, peers, share, elements), 1, 0)]

    def gather_planes(block):
        return [to_all(block).reshape(PLANES, share, elements)]

    def gather_lines(block):
        got = jnp.moveaxis(to_all(block.reshape(peers, per, share, elements)), 0, 1)
        got = got.reshape(per, lines, LINE, elements)
        return [got[:, d] for d in range(lines)]

    def spread(blocks):
        return Exchange(blocks, flight) if direct else Whole(blocks, gather_planes)

    def collect(blocks):
        return Exchange(blocks, flight) if direct else Whole(blocks, gather_lines)

    z_out = spread(columns(2))
    z_out.send(3)
    *constants, face = prepare(
        position, base_bank, snapshot, geometry, diff_r, diff_s, stiffness, upper_list, lower_list
    )
    coef, dpack, spack, gather, scatter, mask = constants
    far = z_out.hold(swap_faces(face[0], face[1]))
    z_out.send(4)
    x_out = spread(columns(0))
    table = x_out.hold(table)
    x_out.send(5)
    z_coefs = x_out.hold(transform(z_out.got(), table))
    x_out.send(2)
    y_blocks = columns(1)
    z_back = collect(z_coefs)
    z_back.send(5)
    x_coefs, y_blocks = z_back.hold((transform(x_out.got(), table), y_blocks))
    z_back.send(2)
    x_back = collect(x_coefs)
    x_back.send(7)
    y_out = spread(y_blocks)
    y_out.send(7)
    z = z_back.got()
    x = x_back.got()
    source, inverse, local, up, lo = start_solve(
        position, z, x, geometry, coef, dpack, spack, gather, mask
    )
    got = swap_faces(up, lo)
    parts = partial_update(z, x, coef, dpack)
    local, (px, py, pz) = lax.optimization_barrier((local, parts))
    local = y_out.after(local, 2, 3)
    local, up, lo = two_sweeps(
        2, position, local, source, inverse, (up, lo), got, face, far, spack, gather, scatter, mask
    )
    y_got = list(y_out.got())
    y_got[0], local = lax.optimization_barrier((y_got[0], local))
    got = swap_faces(up, lo)
    y_back = collect(transform(y_got, table))
    y_back.send(7)
    local = y_back.after(local, 0, 2)
    local, up, lo = two_sweeps(
        1, position, local, source, inverse, (up, lo), got, face, far, spack, gather, scatter, mask
    )
    up, lo = y_back.after((up, lo), 2, 4)
    got = swap_faces(up, lo)
    local = y_back.after(local, 4, 5)
    filled, px = add_force(position, local, got, face, geometry, dpack, scatter, mask, px, pz)
    return finish(position, y_back.got(), coef, dpack, px, py, filled)


def solution(mesh):
    in_specs = (
        P(None, "four", None, "dom"),
        P(None, None, None, "dom"),
        P("dom"),
        P(None, "dom"),
        P(),
        P(),
        P(),
        P("dom", None),
        P("dom", None),
    )
    out_specs = P(None, "four", None, "dom")
    return jax.shard_map(
        per_device, mesh=mesh, in_specs=in_specs, out_specs=out_specs, check_vma=False
    )
```

```python
import functools
import math

import jax
import jax.numpy as jnp
import ml_dtypes
import numpy as np
from jax import lax
from jax.experimental import pallas as pl
from jax.experimental.pallas import tpu as pltpu
from jax.sharding import PartitionSpec as P

PLANES = 256
PENALTY = 0.5
RELAXATION = 0.8
TIME_STEP = 0.2
INTERACTION = 2.0
LINE = 8
IN_FLIGHT = 5

F32 = jnp.float32
BF16 = jnp.bfloat16
VMEM_LIMIT = 20 * 1024 * 1024
LARGE_LIMIT = 48 * 1024 * 1024
SMEM_SPEC = pl.BlockSpec(memory_space=pltpu.SMEM)


def params(limit=VMEM_LIMIT):
    return pltpu.CompilerParams(vmem_limit_bytes=limit)


SHORT = pl.CostEstimate(flops=10**6, bytes_accessed=10**5, transcendentals=0)


def cost(flops, moved):
    return pl.CostEstimate(flops=int(flops), bytes_accessed=int(moved), transcendentals=0)


def split(x):
    high = x.astype(BF16)
    low = (x - high.astype(F32)).astype(BF16)
    return high, low


def dot(a, b):
    return lax.dot_general(a, b, (((1,), (0,)), ((), ())), preferred_element_type=F32)


def pack_matrix(m):
    high, low = split(m)
    return jnp.concatenate([high, low, high], axis=1)


def slab(refs, c):
    return jnp.concatenate([ref[c] for ref in refs], axis=0)


def pack_field(v):
    high, low = split(v)
    return jnp.concatenate([high, high, low], axis=0)


def coef_table(length):
    c = np.arange(length)[:, None]
    j = np.arange(length)[None, :]
    angle = ((c // 2) * j % length) * (2.0 * math.pi / length)
    table = np.where(c % 2 == 1, np.sin(angle), np.cos(angle)) * math.sqrt(2.0 / length)
    table[0] = 1.0 / math.sqrt(length)
    table[1] = np.where(np.arange(length) % 2 == 0, 1.0, -1.0) / math.sqrt(length)
    high = table.astype(ml_dtypes.bfloat16)
    low = (table - high.astype(np.float64)).astype(ml_dtypes.bfloat16)
    return np.concatenate([high, low], axis=0)


def permute_kernel(peers, pos_ref, table_ref, o_ref):
    planes = table_ref.shape[1]
    per = planes // peers
    me = pos_ref[1]
    row = lax.broadcasted_iota(jnp.int32, (planes, planes), 0)
    col = lax.broadcasted_iota(jnp.int32, (planes, planes), 1)
    swap = jnp.where(row == ((col // per) ^ me) * per + col % per, 1.0, 0.0).astype(BF16)
    for half in range(2):
        rows = pl.ds(half * planes, planes)
        turned = dot(swap, table_ref[rows, :]).astype(BF16)
        o_ref[rows, :] = dot(turned, swap).astype(BF16)


def permuted_table(position, table, peers):
    return pl.pallas_call(
        functools.partial(permute_kernel, peers),
        out_shape=jax.ShapeDtypeStruct(table.shape, BF16),
        in_specs=[SMEM_SPEC, pl.BlockSpec(memory_space=pltpu.VMEM)],
        compiler_params=params(),
        cost_estimate=cost(1e8, 4e6),
        name="permuted_table",
    )(position, table)


def transform_kernel(count, table_ref, *refs):
    planes = table_ref.shape[1]
    both = table_ref[...]
    high_table = both[:planes]
    width = refs[0].shape[-1]
    nodes = refs[0].shape[-2]
    per = planes // count
    flat = [ref.reshape(per * nodes, width) for ref in refs]
    for n in range(nodes):
        rows = pl.ds(n, per, stride=nodes) if nodes > 1 else pl.ds(0, per)
        high, low = split(jnp.concatenate([ref[rows, :] for ref in flat[:count]], axis=0))
        wide = dot(both, high)
        result = wide[:planes] + (wide[planes:] + dot(high_table, low))
        for d, ref in enumerate(flat[count:]):
            ref[rows, :] = result[d * per : (d + 1) * per]


def transform(blocks, table):
    per, nodes, elements = blocks[0].shape
    count = len(blocks)
    width = 128
    block = pl.BlockSpec((per, nodes, width), lambda i: (0, 0, i))
    size = count * blocks[0].size
    return pl.pallas_call(
        functools.partial(transform_kernel, count),
        out_shape=[jax.ShapeDtypeStruct(v.shape, F32) for v in blocks],
        grid=(elements // width,),
        in_specs=[pl.BlockSpec(table.shape, lambda i: (0, 0))] + [block] * count,
        out_specs=[block] * count,
        compiler_params=params(),
        cost_estimate=cost(6 * PLANES * size, 8 * size),
        name="transform",
    )(table, *blocks)


def pack_kernel(pos_ref, *refs):
    count = len(refs) // 2
    for source, target in zip(refs[:count], refs[count:]):
        target[...] = source[0]


def pack(position, adjoint, comp, limit):
    _, per, nodes, elements = adjoint.shape
    lines = nodes // LINE
    block = per // 2

    def source(d):
        return pl.BlockSpec((1, block, LINE, elements), lambda i, pos: (comp, i, pos[1] ^ d, 0))

    size = per * nodes * elements
    return pl.pallas_call(
        pack_kernel,
        out_shape=[jax.ShapeDtypeStruct((per, LINE, elements), F32)] * lines,
        grid_spec=pltpu.PrefetchScalarGridSpec(
            num_scalar_prefetch=1,
            grid=(per // block,),
            in_specs=[source(d) for d in range(lines)],
            out_specs=[pl.BlockSpec((block, LINE, elements), lambda i, pos: (i, 0, 0))] * lines,
        ),
        compiler_params=params(limit),
        cost_estimate=cost(0, 8 * size),
        name="pack",
    )(position, *[adjoint] * lines)


BXR, BYS, DXBX, DXBY, DYBX, DYBY, DIAG = range(7)


def line_of(me, d):
    return pl.ds(pl.multiple_of((me ^ d) * LINE, LINE), LINE)


def own_order(ref, me, *lead):
    lines = ref.shape[-2] // LINE
    return jnp.concatenate([ref[(*lead, line_of(me, d), slice(None))] for d in range(lines)], axis=0)


def prep_kernel(
    pos_ref, bank_ref, snap_ref, geo_ref, dr_ref, ds_ref, st_ref, up_ref, lo_ref,
    coef_ref, dpack_ref, spack_ref, gather_ref, scatter_ref, mask_ref, face_ref,
):
    elements = geo_ref.shape[1]
    nodes = dr_ref.shape[0]
    lines = nodes // LINE
    me = pos_ref[1]
    row = lax.broadcasted_iota(jnp.int32, (nodes, nodes), 0)
    col = lax.broadcasted_iota(jnp.int32, (nodes, nodes), 1)
    swap = jnp.where(row == ((col // LINE) ^ me) * LINE + col % LINE, 1.0, 0.0).astype(BF16)

    def permuted(ref):
        high, low = split(own_order(ref, me))
        return dot(high, swap) + dot(low, swap)

    snap = snap_ref[...]
    base = [
        sum(
            jnp.where(snap == k, own_order(bank_ref, me, k, i), 0.0)
            for k in range(bank_ref.shape[0])
        )
        for i in range(2)
    ]
    rx = geo_ref[0:1, :]
    sy = geo_ref[1:2, :]
    dpack = pack_matrix(jnp.concatenate([permuted(dr_ref), permuted(ds_ref)], axis=0))
    dpack_ref[...] = dpack
    bx = dot(dpack, pack_field(base[0]))
    by = dot(dpack, pack_field(base[1]))
    coef_ref[BXR] = base[0] * rx
    coef_ref[BYS] = base[1] * sy
    coef_ref[DXBX] = rx * bx[:nodes]
    coef_ref[DXBY] = rx * by[:nodes]
    coef_ref[DYBX] = sy * bx[nodes:]
    coef_ref[DYBY] = sy * by[nodes:]
    diag = jnp.sum(jnp.where(row == col, st_ref[...], 0.0), axis=0, keepdims=True)
    own = ((row // LINE) ^ me) * LINE + row % LINE == col
    diag = jnp.sum(jnp.where(own, diag, 0.0), axis=1, keepdims=True)
    spack_ref[...] = pack_matrix(jnp.where(row == col, 0.0, permuted(st_ref)))
    coef_ref[DIAG] = jnp.broadcast_to(diag, (nodes, elements))
    shared = up_ref.shape[1]
    mass = jnp.broadcast_to(1.0 / (rx * sy), (16, elements))
    for side, (ref, first) in enumerate(((up_ref, LINE - 1), (lo_ref, 0))):
        index = ref[...]
        node = index // elements
        element = index - node * elements
        hot = lax.broadcasted_iota(jnp.int32, (elements, shared), 0) == element
        hot = jnp.where(hot, 1.0, 0.0)
        gather_ref[side] = hot.astype(BF16)
        back = hot.T.astype(BF16)
        scatter_ref[side] = back
        mask = (lax.broadcasted_iota(jnp.int32, (lines, shared), 0) ^ me) == node // LINE
        mask = jnp.where(mask, 1.0, 0.0)
        mask_ref[side] = mask
        high, low = split(mass)
        rest = (mass - high.astype(F32) - low.astype(F32)).astype(BF16)
        at_face = sum(dot(part, gather_ref[side])[:1] for part in (high, low, rest))
        face_ref[side, 0:1, :] = at_face
        lead = jnp.concatenate([diag[s * LINE + first : s * LINE + first + 1] for s in range(lines)], axis=0)
        face_ref[side, 1:2, :] = PENALTY + jnp.sum(mask * lead, axis=0, keepdims=True)
        count = dot(mask.astype(BF16), back)
        for s in range(lines):
            n = s * LINE + first
            coef_ref[DIAG, n : n + 1, :] = coef_ref[DIAG, n : n + 1, :] + PENALTY * count[s : s + 1]


def prepare(position, base_bank, snapshot, geometry, diff_r, diff_s, stiffness, upper, lower):
    nodes = diff_r.shape[0]
    elements = geometry.shape[1]
    shared = upper.shape[1]
    return pl.pallas_call(
        prep_kernel,
        out_shape=[
            jax.ShapeDtypeStruct((7, nodes, elements), F32),
            jax.ShapeDtypeStruct((2 * nodes, 3 * nodes), BF16),
            jax.ShapeDtypeStruct((nodes, 3 * nodes), BF16),
            jax.ShapeDtypeStruct((2, elements, shared), BF16),
            jax.ShapeDtypeStruct((2, shared, elements), BF16),
            jax.ShapeDtypeStruct((2, nodes // LINE, shared), F32),
            jax.ShapeDtypeStruct((2, 2, shared), F32),
        ],
        in_specs=[SMEM_SPEC] + [pl.BlockSpec(memory_space=pltpu.VMEM)] * 8,
        compiler_params=params(),
        cost_estimate=cost(1e7, 8e6),
        name="prepare",
    )(position, base_bank, snapshot.reshape(1, elements), geometry, diff_r, diff_s, stiffness, upper, lower)


def face_of(ref, side):
    rows, elements = ref.shape
    return ref.reshape(rows // LINE, LINE, elements).at[:, LINE - 1 if side == 0 else 0, :]


def gather_faces(side, fields, gather_ref, mask_ref):
    lines = mask_ref.shape[1]
    high, low = split(jnp.concatenate(fields, axis=0))
    rows = high.shape[0]
    both = dot(jnp.concatenate([high, low], axis=0), gather_ref[side])
    picked = both[:rows] + both[rows:]
    shared = picked.shape[1]
    return jnp.sum(picked.reshape(rows // lines, lines, shared) * mask_ref[side][None], axis=1)


def scatter_faces(side, values, scatter_ref, mask_ref):
    mask = mask_ref[side]
    coefs, shared = values.shape
    spread = (values[:, None, :] * mask[None]).reshape(coefs * mask.shape[0], shared)
    high, low = split(spread)
    rows = high.shape[0]
    both = dot(jnp.concatenate([high, low], axis=0), scatter_ref[side])
    return both[:rows] + both[rows:]


def local_sweep(pot, source, inverse, spack):
    applied = dot(spack, pack_field(pot))
    return (1.0 - RELAXATION) * pot + inverse * (source - applied)


def coef_block(coefs, block=8):
    return block if coefs % block == 0 else coefs


def start_kernel(
    block, count, pos_ref, geo_ref, diag_ref, dpack_ref, spack_ref, gather_ref, mask_ref, *refs
):
    z_refs, x_refs = refs[:count], refs[count : 2 * count]
    source_ref, inverse_ref, local_ref, up_ref, lo_ref, pot_ref = refs[2 * count :]
    nodes, elements = diag_ref.shape[1:]
    beta = 4.0 / PLANES
    first = pos_ref[0] * (block * pl.num_programs(0)) + pl.program_id(0) * block
    rx = geo_ref[0:1, :]
    mass = 1.0 / (rx * geo_ref[1:2, :])
    diag = diag_ref[0]
    drpack = dpack_ref[:nodes]
    spack = spack_ref[...]
    for c in range(block):
        index = first + c
        wave = beta * (index // 2).astype(F32)
        shift = beta * jnp.where(index == 1, PLANES // 2, index // 2).astype(F32)
        shift = shift * shift
        z = slab(z_refs, c)
        other = slab(x_refs, c + 1 if c % 2 == 0 else c - 1)
        turned = (wave if c % 2 == 0 else -wave) * other
        source = turned - rx * dot(drpack, pack_field(z))
        inverse = RELAXATION / (diag + shift * mass)
        pot = inverse * source
        rows = pl.ds(c * nodes, nodes)
        source_ref[rows, :] = source
        inverse_ref[rows, :] = inverse
        pot_ref[rows, :] = pot
        local_ref[rows, :] = local_sweep(pot, source, inverse, spack)
    for side, out in ((0, up_ref), (1, lo_ref)):
        fields = [face_of(ref, side)[...] for ref in (pot_ref, local_ref)]
        picked = gather_faces(side, fields, gather_ref, mask_ref)
        for k in range(2):
            out[k] = picked[k * block : (k + 1) * block]


def whole(shape):
    return pl.BlockSpec(shape, lambda *i: (0,) * len(shape))


def start_solve(position, z, x, geometry, coef, dpack, spack, gather, mask):
    coefs, part, elements = z[0].shape
    nodes = len(z) * part
    shared = gather.shape[2]
    block = coef_block(coefs, 16)
    field = [pl.BlockSpec((block, part, elements), lambda i: (i, 0, 0))] * len(z)
    flat = pl.BlockSpec((block * nodes, elements), lambda i: (i, 0))
    face = pl.BlockSpec((2, block, shared), lambda i: (0, i, 0))
    size = coefs * nodes * elements
    return pl.pallas_call(
        functools.partial(start_kernel, block, len(z)),
        out_shape=[jax.ShapeDtypeStruct((coefs * nodes, elements), F32)] * 3
        + [jax.ShapeDtypeStruct((2, coefs, shared), F32)] * 2,
        grid=(coefs // block,),
        in_specs=[
            SMEM_SPEC, whole(geometry.shape),
            pl.BlockSpec((1, nodes, elements), lambda i: (DIAG, 0, 0)),
            whole(dpack.shape), whole(spack.shape), whole(gather.shape), whole(mask.shape),
            *field, *field,
        ],
        out_specs=[flat, flat, flat, face, face],
        scratch_shapes=[pltpu.VMEM((block * nodes, elements), F32)],
        compiler_params=params(),
        cost_estimate=SHORT,
        name="start_solve",
    )(position, geometry, coef, dpack, spack, gather, mask, *z, *x)


def face_inverse(face, first, coefs):
    index = first + lax.broadcasted_iota(jnp.int32, (coefs, 1), 0)
    wave = jnp.where(index == 1, PLANES // 2, index // 2).astype(F32)
    shift = (4.0 / PLANES) * wave
    shift = shift * shift
    return RELAXATION / (face[1:2] + shift * face[0:1])


def sweeps_kernel(
    block, keep, pos_ref, local_ref, source_ref, inverse_ref, own_up_ref, own_lo_ref,
    got_up_ref, got_lo_ref, face_ref, far_up_ref, far_lo_ref, spack_ref, gather_ref, scatter_ref,
    mask_ref, next_ref, up_ref, lo_ref, pot_ref,
):
    nodes = spack_ref.shape[0]
    spack = spack_ref[...]
    lines = block * (nodes // LINE)
    first = pos_ref[0] * (block * pl.num_programs(0)) + pl.program_id(0) * block
    partners = []
    for side, own, got, far in ((0, own_up_ref, got_up_ref, far_up_ref), (1, own_lo_ref, got_lo_ref, far_lo_ref)):
        scale = PENALTY * face_inverse(face_ref[side], first, block)
        now = scale * got[0]
        later = scale * (got[1] + PENALTY * face_inverse(far[...], first, block) * own[0])
        both = scatter_faces(side, jnp.concatenate([now, later], axis=0), scatter_ref, mask_ref)
        partners.append((both[:lines], both[lines:]))
    pot_ref[...] = local_ref[...]
    for side in range(2):
        face = face_of(pot_ref, side)
        face[...] = face[...] + partners[side][0]
    for c in range(block):
        rows = pl.ds(c * nodes, nodes)
        pot_ref[rows, :] = local_sweep(pot_ref[rows, :], source_ref[rows, :], inverse_ref[rows, :], spack)
    for side in range(2):
        face = face_of(pot_ref, side)
        face[...] = face[...] + partners[side][1]
    for c in range(block):
        rows = pl.ds(c * nodes, nodes)
        next_ref[rows, :] = local_sweep(pot_ref[rows, :], source_ref[rows, :], inverse_ref[rows, :], spack)
    for side, out in ((0, up_ref), (1, lo_ref)):
        fields = [face_of(ref, side)[...] for ref in (pot_ref, next_ref)[:keep]]
        picked = gather_faces(side, fields, gather_ref, mask_ref)
        for k in range(keep):
            out[k] = picked[k * block : (k + 1) * block]


def two_sweeps(keep, position, local, source, inverse, own, got, face, far, spack, gather, scatter, mask):
    nodes = spack.shape[0]
    elements = local.shape[1]
    coefs = local.shape[0] // nodes
    shared = gather.shape[2]
    block = coef_block(coefs, 16)
    flat = pl.BlockSpec((block * nodes, elements), lambda i: (i, 0))
    one = pl.BlockSpec((1, block, shared), lambda i: (0, i, 0))
    two = pl.BlockSpec((2, block, shared), lambda i: (0, i, 0))
    kept = pl.BlockSpec((keep, block, shared), lambda i: (0, i, 0))
    size = coefs * nodes * elements
    return pl.pallas_call(
        functools.partial(sweeps_kernel, block, keep),
        out_shape=[jax.ShapeDtypeStruct(local.shape, F32)]
        + [jax.ShapeDtypeStruct((keep, coefs, shared), F32)] * 2,
        grid=(coefs // block,),
        in_specs=[
            SMEM_SPEC, flat, flat, flat, one, one, two, two,
            whole(face.shape), whole(far[0].shape), whole(far[1].shape),
            whole(spack.shape), whole(gather.shape), whole(scatter.shape), whole(mask.shape),
        ],
        out_specs=[flat, kept, kept],
        scratch_shapes=[pltpu.VMEM((block * nodes, elements), F32)],
        compiler_params=params(),
        cost_estimate=SHORT,
        name="two_sweeps",
    )(position, local, source, inverse, *own, *got, face, *far, spack, gather, scatter, mask)


def store_own(ref, me, value, *lead):
    for d in range(value.shape[0] // LINE):
        ref[(*lead, line_of(me, d), slice(None))] = value[d * LINE : (d + 1) * LINE]


def partial_kernel(block, count, coef_ref, dpack_ref, *refs):
    z_refs, x_refs = refs[:count], refs[count : 2 * count]
    px_ref, py_ref, pz_ref = refs[2 * count :]
    nodes = coef_ref.shape[1]
    dpack = dpack_ref[...]
    for c in range(block):
        z = slab(z_refs, c)
        slopes = dot(dpack, pack_field(z))
        moved = coef_ref[BXR] * slopes[:nodes] + coef_ref[BYS] * slopes[nodes:]
        pz_ref[c] = z - TIME_STEP * (moved + INTERACTION * z)
        x = slab(x_refs, c)
        slopes = dot(dpack, pack_field(x))
        moved = coef_ref[BXR] * slopes[:nodes] + coef_ref[BYS] * slopes[nodes:]
        px_ref[c] = x + TIME_STEP * (x * coef_ref[DXBX] - moved - INTERACTION * x)
        py_ref[c] = TIME_STEP * (x * coef_ref[DYBX])


def partial_update(z, x, coef, dpack):
    coefs, part, elements = z[0].shape
    nodes = len(z) * part
    block = coef_block(coefs)
    field = [pl.BlockSpec((block, part, elements), lambda i: (i, 0, 0))] * len(z)
    out = pl.BlockSpec((block, nodes, elements), lambda i: (i, 0, 0))
    return pl.pallas_call(
        functools.partial(partial_kernel, block, len(z)),
        out_shape=[jax.ShapeDtypeStruct((coefs, nodes, elements), F32)] * 3,
        grid=(coefs // block,),
        in_specs=[whole(coef.shape), whole(dpack.shape), *field, *field],
        out_specs=[out] * 3,
        compiler_params=params(),
        cost_estimate=SHORT,
        name="partial_update",
    )(coef, dpack, *z, *x)


def force_kernel(
    block, pos_ref, local_ref, got_up_ref, got_lo_ref, face_ref, geo_ref, dpack_ref,
    scatter_ref, mask_ref, px_ref, pz_ref, o_ref, x_ref, pot_ref,
):
    nodes = dpack_ref.shape[0] // 2
    scale = TIME_STEP * INTERACTION
    me = pos_ref[1]
    pot_ref[...] = local_ref[...]
    first = pos_ref[0] * (block * pl.num_programs(0)) + pl.program_id(0) * block
    for side, got in ((0, got_up_ref), (1, got_lo_ref)):
        face = face_of(pot_ref, side)
        partner = PENALTY * face_inverse(face_ref[side], first, block) * got[0]
        face[...] = face[...] + scatter_faces(side, partner, scatter_ref, mask_ref)
    drpack = dpack_ref[:nodes]
    slope_scale = scale * geo_ref[0:1, :]
    for c in range(block):
        pot = pot_ref[pl.ds(c * nodes, nodes), :]
        slope = dot(drpack, pack_field(pot))
        store_own(o_ref, me, pz_ref[c] - slope_scale * slope, 0, c)
        wave = (4.0 / PLANES) * ((first + c) // 2).astype(F32)
        factor = scale * (wave if c % 2 else -wave)
        other = c - 1 if c % 2 else c + 1
        x_ref[other] = px_ref[other] + factor * pot


def add_force(position, local, got, face, geometry, dpack, scatter, mask, px, pz):
    coefs, nodes, elements = px.shape
    shared = scatter.shape[1]
    block = coef_block(coefs, 16)
    flat = pl.BlockSpec((block * nodes, elements), lambda i: (i, 0))
    one = pl.BlockSpec((1, block, shared), lambda i: (0, i, 0))
    part = pl.BlockSpec((block, nodes, elements), lambda i: (i, 0, 0))
    return pl.pallas_call(
        functools.partial(force_kernel, block),
        out_shape=[
            jax.ShapeDtypeStruct((3, coefs, nodes, elements), F32),
            jax.ShapeDtypeStruct(px.shape, F32),
        ],
        grid=(coefs // block,),
        in_specs=[
            SMEM_SPEC, flat, one, one, whole(face.shape), whole(geometry.shape), whole(dpack.shape),
            whole(scatter.shape), whole(mask.shape), part, part,
        ],
        out_specs=[pl.BlockSpec((1, block, nodes, elements), lambda i: (2, i, 0, 0)), part],
        scratch_shapes=[pltpu.VMEM((block * nodes, elements), F32)],
        compiler_params=params(),
        cost_estimate=SHORT,
        name="add_force",
    )(position, local, *got, face, geometry, dpack, scatter, mask, px, pz)


def finish_kernel(block, count, pos_ref, coef_ref, dpack_ref, px_ref, py_ref, filled_ref, *refs):
    del filled_ref
    y_refs, o_ref = refs[:count], refs[count]
    nodes = coef_ref.shape[1]
    me = pos_ref[1]
    dpack = dpack_ref[...]
    for c in range(block):
        y = slab(y_refs, c)
        slopes = dot(dpack, pack_field(y))
        moved = coef_ref[BXR] * slopes[:nodes] + coef_ref[BYS] * slopes[nodes:]
        change = y + TIME_STEP * (y * coef_ref[DYBY] - moved)
        store_own(o_ref, me, py_ref[c] + change, 1, c)
        store_own(o_ref, me, px_ref[c] + TIME_STEP * (y * coef_ref[DXBY]), 0, c)


def finish(position, y, coef, dpack, px, py, filled):
    coefs, part, elements = y[0].shape
    nodes = len(y) * part
    block = coef_block(coefs, 16)
    field = pl.BlockSpec((block, part, elements), lambda i: (i, 0, 0))
    own = pl.BlockSpec((block, nodes, elements), lambda i: (i, 0, 0))
    return pl.pallas_call(
        functools.partial(finish_kernel, block, len(y)),
        out_shape=jax.ShapeDtypeStruct(filled.shape, F32),
        grid=(coefs // block,),
        in_specs=[
            SMEM_SPEC, whole(coef.shape), whole(dpack.shape), own, own,
            pl.BlockSpec(memory_space=pl.ANY), *[field] * len(y),
        ],
        out_specs=pl.BlockSpec((2, block, nodes, elements), lambda i: (0, i, 0, 0)),
        input_output_aliases={5: 0},
        compiler_params=params(),
        cost_estimate=SHORT,
        name="finish",
    )(position, coef, dpack, px, py, filled, *y)


def to_all(blocks):
    return lax.all_to_all(blocks, "four", split_axis=0, concat_axis=0, tiled=True)


def swap_faces(up, lo):
    peers = lax.axis_size("dom")
    up_way = [(i, (i + 1) % peers) for i in range(peers)]
    down_way = [(j, i) for i, j in up_way]
    return lax.ppermute(lo, "dom", down_way), lax.ppermute(up, "dom", up_way)


class Exchange:
    def __init__(self, blocks, flight):
        self.blocks = list(blocks)
        self.flight = flight
        self.places = {}
        self.order = sorted(range(1, len(self.blocks)), key=lambda d: (d < 2, d % 2, d))

    def hold(self, value):
        if len(self.places) < len(self.order):
            d = self.order[len(self.places)]
            self.blocks[d], value = lax.optimization_barrier((self.blocks[d], value))
        return value

    def send(self, count):
        for d in self.order[len(self.places) :][:count]:
            block = self.blocks[d]
            if len(self.flight) >= IN_FLIGHT:
                block, self.flight[-IN_FLIGHT] = lax.optimization_barrier((block, self.flight[-IN_FLIGHT]))
            pairs = [(i, i ^ d) for i in range(len(self.blocks))]
            self.places[d] = len(self.flight)
            self.flight.append(lax.ppermute(block, "four", pairs))

    def after(self, value, first, last):
        for d in self.order[first:last]:
            place = self.places[d]
            value, self.flight[place] = lax.optimization_barrier((value, self.flight[place]))
        return value

    def got(self):
        return [self.blocks[0]] + [self.flight[self.places[d]] for d in range(1, len(self.blocks))]


class Whole(Exchange):
    def __init__(self, blocks, exchange):
        super().__init__(blocks[:1], [])
        self.exchange = exchange

    def got(self):
        return self.exchange(self.blocks[0])


def per_device(
    adjoint, base_bank, snapshot, geometry, diff_r, diff_s, stiffness, upper_list, lower_list
):
    _, per, nodes, elements = adjoint.shape
    peers = lax.axis_size("four")
    lines = nodes // LINE
    direct = peers == lines
    place = lax.axis_index("four").astype(jnp.int32)
    position = jnp.stack([place, place if direct else jnp.zeros_like(place)])
    natural = jnp.asarray(coef_table(PLANES))
    table = permuted_table(position, natural, lines)
    flight = []
    share = nodes // peers

    def columns(comp):
        if direct:
            return pack(position, adjoint, comp, LARGE_LIMIT if comp == 2 else VMEM_LIMIT)
        return [jnp.moveaxis(adjoint[comp].reshape(per, peers, share, elements), 1, 0)]

    def gather_planes(block):
        return [to_all(block).reshape(PLANES, share, elements)]

    def gather_lines(block):
        got = jnp.moveaxis(to_all(block.reshape(peers, per, share, elements)), 0, 1)
        got = got.reshape(per, lines, LINE, elements)
        return [got[:, d] for d in range(lines)]

    def spread(blocks):
        return Exchange(blocks, flight) if direct else Whole(blocks, gather_planes)

    def collect(blocks):
        return Exchange(blocks, flight) if direct else Whole(blocks, gather_lines)

    z_out = spread(columns(2))
    z_out.send(3)
    *constants, face = prepare(
        position, base_bank, snapshot, geometry, diff_r, diff_s, stiffness, upper_list, lower_list
    )
    coef, dpack, spack, gather, scatter, mask = constants
    far = z_out.hold(swap_faces(face[0], face[1]))
    z_out.send(4)
    x_out = spread(columns(0))
    table = x_out.hold(table)
    x_out.send(5)
    z_coefs = x_out.hold(transform(z_out.got(), table))
    x_out.send(2)
    y_blocks = columns(1)
    z_back = collect(z_coefs)
    z_back.send(5)
    x_coefs, y_blocks = z_back.hold((transform(x_out.got(), table), y_blocks))
    z_back.send(2)
    x_back = collect(x_coefs)
    x_back.send(7)
    y_out = spread(y_blocks)
    y_out.send(7)
    z = z_back.got()
    x = x_back.got()
    source, inverse, local, up, lo = start_solve(
        position, z, x, geometry, coef, dpack, spack, gather, mask
    )
    got = swap_faces(up, lo)
    parts = partial_update(z, x, coef, dpack)
    local, (px, py, pz) = lax.optimization_barrier((local, parts))
    local = y_out.after(local, 2, 3)
    local, up, lo = two_sweeps(
        2, position, local, source, inverse, (up, lo), got, face, far, spack, gather, scatter, mask
    )
    y_got = list(y_out.got())
    y_got[0], local = lax.optimization_barrier((y_got[0], local))
    got = swap_faces(up, lo)
    y_back = collect(transform(y_got, table))
    y_back.send(7)
    local = y_back.after(local, 0, 2)
    local, up, lo = two_sweeps(
        1, position, local, source, inverse, (up, lo), got, face, far, spack, gather, scatter, mask
    )
    up, lo = y_back.after((up, lo), 2, 4)
    got = swap_faces(up, lo)
    local = y_back.after(local, 4, 5)
    filled, px = add_force(position, local, got, face, geometry, dpack, scatter, mask, px, pz)
    return finish(position, y_back.got(), coef, dpack, px, py, filled)


def solution(mesh):
    in_specs = (
        P(None, "four", None, "dom"),
        P(None, None, None, "dom"),
        P("dom"),
        P(None, "dom"),
        P(),
        P(),
        P(),
        P("dom", None),
        P("dom", None),
    )
    out_specs = P(None, "four", None, "dom")
    return jax.shard_map(
        per_device, mesh=mesh, in_specs=in_specs, out_specs=out_specs, check_vma=False
    )
```
